1024 devices in a mesh: win: 64 (over z_lo, y, core), wout: 16 (over x, z_hi).
Axes of the slice: x: 4, y: 8, z: 16 (z_hi: 4, z_lo: 4; z = z_hi * 4 + z_lo), core: 2. Of those that a mesh axis runs over, the one named last changes fastest.
Arguments:
- inputs: bfloat16 [256, 18432], P(None, 'win'), may hold values from -6 to 6
- w_query: bfloat16 [18432, 12288], P('win', 'wout'), may hold values from -0.046875 to 0.046875
- w_keyval: bfloat16 [18432, 512], P('win', 'wout'), may hold values from -0.046875 to 0.046875
- w_out: bfloat16 [12288, 18432], P('wout', 'win'), may hold values from -0.375 to 0.375
- key_cache: bfloat16 [256, 2048, 256], P('win', 'wout'), may hold values from -400 to 400
- value_cache: bfloat16 [256, 2048, 256], P('win', 'wout'), may hold values from -6 to 6
- lengths: int32 [256], P('win'), may hold values from 1 to 2048, as said below
- positions: int32 [256], P('win'), may hold values from 2048 to 16383
Outputs:
- mixed: bfloat16 [256, 18432], P('wout', 'win')
The draws below stay inside these ranges and needn't reach their ends.
Inputs may be any that keep to these rules, and one draw needn't show every extreme that they name: `lengths`: slots at and past a row's length are not read; some row fills all 2048 slots.
All inputs are finite; a program needn't handle non-finite values.
Results may differ from the reference program's by a relative error of at most 0.014.
Values may be sent and summed in bfloat16 or wider, within the bound.
No kernel may reach another device: no remote copies, remote signals or barrier semaphores. Data moves between devices by JAX's collectives and lax.ppermute only.
A program may use at most 32 MiB of HBM per device.

```python
import jax
import jax.numpy as jnp
from jax import lax

D = 18432
HEADS = 48
HEAD = 256
ROW_DEV = 4
QD = 12288
ROWS = 256
CACHE = 2048


def draw_key_cache(key, part):
    key = jax.random.fold_in(key, 11)
    first = jax.random.fold_in(key, 0)
    base = jnp.clip(jax.random.normal(first, (ROWS, CACHE, HEAD), jnp.float32), -6.0, 6.0)
    return base.astype(jnp.bfloat16)


def draw_lengths(key, part):
    key = jax.random.fold_in(key, 5)
    first, second = jax.random.split(key)
    drawn = jax.random.randint(first, (ROWS,), 1, CACHE + 1)
    chosen = jax.random.randint(second, (), 0, ROWS)
    return jnp.where(jnp.arange(ROWS) == chosen, CACHE, drawn).astype(jnp.int32)


def with_ends(entries, rng, low, top_value):
    shape = entries.shape
    spot = [jax.random.randint(jax.random.fold_in(rng, axis), (), 0, shape[axis]) for axis in range(len(shape))]
    entries = entries.at[tuple(spot)].set(low)
    longest = shape.index(max(shape))
    spot[longest] = (spot[longest] + 1) % shape[longest]
    return entries.at[tuple(spot)].set(top_value)


def level_of(own_key, extent, cuts, smallest, high):
    level, own = 1.0, jax.random.fold_in(own_key, 6)
    for axis_at, blocks in cuts:
        draws = jnp.exp(jax.random.uniform(jax.random.fold_in(own, axis_at), (blocks,), jnp.float32, smallest / len(cuts), high / len(cuts)))
        level = level * jnp.repeat(draws, extent[axis_at] // blocks).reshape([-1 if axis == axis_at else 1 for axis in range(len(extent))])
    return level


def centred(own_key, dims, spread, reach, cuts=(), kind=jnp.bfloat16):
    values = jax.random.normal(own_key, dims, jnp.float32) * spread
    if len(cuts) > 0:
        values = level_of(own_key, dims, cuts, -0.22, 0.18) * values
    return jnp.clip(values, min=-reach, max=reach).astype(kind)


def setup_inputs(seed: int = 0) -> dict:
    seeds = jax.random.split(jax.random.key(seed), 9)
    return {
        "inputs": centred(seeds[0], (ROWS, D), 1.0, 6.0, ((1, 64),)),
        "w_query": centred(seeds[1], (D, QD), D ** -0.5, 0.046875, ((0, 64), (1, 16))),
        "w_keyval": centred(seeds[2], (D, 2 * HEAD), D ** -0.5, 0.046875, ((0, 64), (1, 16))),
        "w_out": centred(seeds[3], (QD, D), HEAD ** -0.5, 0.375, ((0, 16), (1, 64))),
        "key_cache": draw_key_cache(jax.random.fold_in(seeds[8], 71), 0),
        "value_cache": centred(seeds[5], (ROWS, CACHE, HEAD), 1.0, 6.0, ((0, 64), (1, 16))),
        "lengths": draw_lengths(jax.random.fold_in(seeds[8], 71), 0),
        "positions": with_ends(jax.random.randint(seeds[7], (ROWS,), CACHE, 8 * CACHE), jax.random.fold_in(seeds[7], 1), CACHE, (8 * CACHE) - 1).astype(jnp.int32),
    }


def rotate(values, angles_pos):
    half = values.shape[-1] // 2
    freq = 10000.0 ** (-(2.0 * jnp.arange(half, dtype=jnp.float32)) / values.shape[-1])
    angle = angles_pos[..., None] * freq
    first = values[..., :half]
    second = values[..., half:]
    cosine = jnp.cos(angle)
    sine = jnp.sin(angle)
    return jnp.concatenate([first * cosine - second * sine, first * sine + second * cosine], -1)


def reference(inputs, w_query, w_keyval, w_out, key_cache, value_cache, lengths, positions):
    query = jnp.dot(inputs, w_query, preferred_element_type=jnp.float32).astype(jnp.bfloat16)
    fresh = jnp.dot(inputs, w_keyval, preferred_element_type=jnp.float32).astype(jnp.bfloat16)
    place = positions.astype(jnp.float32)
    qrot = rotate(query.reshape(ROWS, HEADS, HEAD).astype(jnp.float32), place[:, None]).astype(jnp.bfloat16)
    newkey = rotate(fresh[:, :HEAD].astype(jnp.float32), place).astype(jnp.bfloat16)
    newval = fresh[:, HEAD:]
    scale = HEAD ** -0.5

    def block(items):
        qb, kb, vb, lb, nk, nv = items
        scores = jnp.einsum('rhd,rtd->rht', qb.astype(jnp.float32), kb.astype(jnp.float32)) * scale
        valid = jnp.arange(CACHE)[None, :] < lb[:, None]
        scores = jnp.where(valid[:, None, :], scores, -1e30)
        own = jnp.einsum('rhd,rd->rh', qb.astype(jnp.float32), nk.astype(jnp.float32)) * scale
        top = jnp.maximum(jnp.max(scores, -1), own)
        weights = jnp.where(valid[:, None, :], jnp.exp(scores - top[..., None]), 0.0)
        pself = jnp.exp(own - top)
        total = jnp.sum(weights, -1) + pself
        acc = jnp.einsum('rht,rtd->rhd', weights, vb.astype(jnp.float32))
        acc = acc + pself[..., None] * nv.astype(jnp.float32)[:, None, :]
        return (acc / total[..., None]).reshape(qb.shape[0], QD).astype(jnp.bfloat16)

    count = ROWS // ROW_DEV
    items = (qrot.reshape(count, ROW_DEV, HEADS, HEAD), key_cache.reshape(count, ROW_DEV, CACHE, HEAD),
             value_cache.reshape(count, ROW_DEV, CACHE, HEAD), lengths.reshape(count, ROW_DEV),
             newkey.reshape(count, ROW_DEV, HEAD), newval.reshape(count, ROW_DEV, HEAD))
    attended = lax.map(block, items).reshape(ROWS, QD)
    return jnp.dot(attended, w_out, preferred_element_type=jnp.float32).astype(jnp.bfloat16)
```

```python
import jax
import jax.numpy as jnp
from jax import lax
from jax.sharding import PartitionSpec as P


def exchange(pieces, axis):
    return lax.all_to_all(pieces, axis, 0, 0, tiled=True)


def spread(value, axis):
    count = lax.axis_size(axis)
    return exchange(jnp.broadcast_to(value[None], (count,) + value.shape), axis)


def turn(values, cosine, sine):
    half = values.shape[-1] // 2
    first = values[..., :half]
    second = values[..., half:]
    return jnp.concatenate([first * cosine - second * sine, first * sine + second * cosine], -1)


def body(inputs, w_query, w_keyval, w_out, key_cache, value_cache, lengths, positions):
    rows, slots, head = key_cache.shape
    qcols = w_query.shape[1]
    own = qcols // head
    wins = lax.axis_size("win")
    wouts = lax.axis_size("wout")
    heads = own * wouts
    me = lax.axis_index("wout")
    wide = jnp.float32
    narrow = jnp.bfloat16
    scale = head ** (-0.5)

    half = head // 2
    freq = 10000.0 ** (-(2.0 * jnp.arange(half, dtype=wide)) / head)
    angle = positions.astype(wide)[:, None] * freq
    cosine = jnp.cos(angle)
    sine = jnp.sin(angle)

    partial = jnp.concatenate(
        [
            jnp.dot(inputs, w_query, preferred_element_type=wide).astype(narrow),
            jnp.dot(inputs, w_keyval, preferred_element_type=wide).astype(narrow),
        ],
        1,
    )
    pieces = exchange(partial.reshape(wins, rows, -1), "win")
    summed = jnp.sum(pieces.astype(wide), 0).astype(narrow)
    q_part = summed[:, :qcols].reshape(rows, own, head).astype(wide)
    q_turned = turn(q_part, cosine[:, None], sine[:, None]).astype(narrow)
    sent = jnp.concatenate([q_turned.reshape(rows, qcols), summed[:, qcols:]], 1)
    got = spread(sent, "wout")
    qrot = got[:, :, :qcols].reshape(wouts, rows, own, head)
    qrot = qrot.transpose(1, 0, 2, 3).reshape(rows, heads, head)
    fresh = got[:, :, qcols:].transpose(1, 0, 2).reshape(rows, 2 * head)
    newkey = turn(fresh[:, :head].astype(wide), cosine, sine).astype(narrow)
    newval = fresh[:, head:]

    scores = jnp.einsum("rhd,rtd->rht", qrot, key_cache, preferred_element_type=wide) * scale
    valid = (me * slots + jnp.arange(slots))[None, :] < lengths[:, None]
    scores = jnp.where(valid[:, None, :], scores, -1e30)
    self_score = jnp.sum(qrot.astype(wide) * newkey.astype(wide)[:, None, :], -1) * scale
    self_score = jnp.where(me == 0, self_score, -1e30)
    top = jnp.maximum(jnp.max(scores, -1), self_score)
    weights = jnp.where(valid[:, None, :], jnp.exp(scores - top[..., None]), 0.0)
    self_weight = jnp.where(me == 0, jnp.exp(self_score - top), 0.0)
    total = jnp.sum(weights, -1) + self_weight
    acc = jnp.einsum("rht,rtd->rhd", weights.astype(narrow), value_cache, preferred_element_type=wide)
    acc = acc + self_weight[..., None] * newval.astype(wide)[:, None, :]

    stats = jnp.concatenate(
        [
            jnp.broadcast_to(top[..., None], (rows, heads, 64)),
            jnp.broadcast_to(total[..., None], (rows, heads, 64)),
        ],
        -1,
    )
    parts = jnp.concatenate([acc, stats], -1).reshape(rows, wouts, own, head + 128)
    parts = parts.transpose(1, 0, 2, 3).reshape(wouts, rows * own, head + 128)
    parts = exchange(parts, "wout")
    tops = parts[:, :, head : head + 1]
    totals = parts[:, :, head + 64 : head + 65]
    factors = jnp.exp(tops - jnp.max(tops, 0, keepdims=True))
    total = jnp.sum(totals * factors, 0)
    acc = jnp.sum(parts[:, :, :head] * factors, 0)
    attended = (acc / total).reshape(rows, qcols).astype(narrow)

    whole = spread(attended, "win").reshape(wins * rows, qcols)
    mixed = jnp.dot(whole, w_out, preferred_element_type=wide).astype(narrow)
    mixed = exchange(mixed.reshape(wouts, -1, mixed.shape[1]), "wout")
    return jnp.sum(mixed.astype(wide), 0).astype(narrow)


def solution(mesh):
    placed = (
        P(None, "win"),
        P("win", "wout"),
        P("win", "wout"),
        P("wout", "win"),
        P("win", "wout", None),
        P("win", "wout", None),
        P("win"),
        P("win"),
    )
    return jax.shard_map(
        body, mesh=mesh, in_specs=placed, out_specs=P("wout", "win"), check_vma=False
    )
```

```python
import functools

import jax
import jax.numpy as jnp
from jax import lax
from jax.experimental import pallas as pl
from jax.experimental.pallas import tpu as pltpu
from jax.sharding import Mesh
from jax.sharding import PartitionSpec as P

WIDE = jnp.float32
NARROW = jnp.bfloat16
AXES = ("zlo", "y", "core", "x", "zh")
SIZES = (4, 8, 2, 4, 4)
WIN = ("zlo", "y", "core")
CHIP = ("zlo", "y")
WOUT = ("x", "zh")
NONE = -1e30
STATS = 128
TALL = 16
VMEM = pl.BlockSpec(memory_space=pltpu.VMEM)
SMEM = pl.BlockSpec(memory_space=pltpu.SMEM)


def exchange(pieces, axis):
    return lax.all_to_all(pieces, axis, 0, 0, tiled=True)


def turn(first, second, cosine, sine):
    return first * cosine - second * sine, first * sine + second * cosine


def own_queries(head, own, rows, pieces_ref, cos_ref, sin_ref, out_ref):
    half = head // 2
    total = jnp.sum(pieces_ref[...].astype(WIDE), 0).astype(NARROW)
    cosine, sine = cos_ref[:rows, :], sin_ref[:rows, :]
    for h in range(own):
        start = h * head
        first = total[:, start : start + half].astype(WIDE)
        second = total[:, start + half : start + head].astype(WIDE)
        first, second = turn(first, second, cosine, sine)
        for peer in range(out_ref.shape[0]):
            out_ref[peer, :, start : start + half] = first.astype(NARROW)
            out_ref[peer, :, start + half : start + head] = second.astype(NARROW)
    for peer in range(out_ref.shape[0]):
        out_ref[peer, :, own * head :] = total[:, own * head :]


def partial_attention(head, own, rows, slots, scale, blocks, peers, len_ref, at_ref, got_ref, cos_ref, sin_ref, *refs):
    kv_refs = refs[:blocks]
    out_ref, q_scr, fresh_scr, out_scr = refs[blocks:]
    half = head // 2
    count = peers * TALL
    width = got_ref.shape[2] - own * head
    wouts = got_ref.shape[0]
    x, zh = at_ref[0], at_ref[1]
    q_scr[...] = jnp.zeros_like(q_scr)
    for z in range(peers):
        for h in range(own):
            at = z * TALL + h * rows
            q_scr[at : at + rows, :] = got_ref[x * peers + z, :, h * head : (h + 1) * head].astype(WIDE)
    q = q_scr[...].astype(NARROW)

    for o in range(wouts):
        fresh_scr[o * rows : (o + 1) * rows, :] = got_ref[o, :, own * head :].astype(WIDE)
    iota = functools.partial(lax.broadcasted_iota, jnp.int32)
    copies = iota((width, wouts * width), 1) % width == iota((width, wouts * width), 0)
    fresh = jnp.dot(fresh_scr[...].astype(NARROW), copies.astype(WIDE).astype(NARROW), preferred_element_type=WIDE)
    wide = (wouts * rows, wouts * width)
    fresh = jnp.where(iota(wide, 1) // width == iota(wide, 0) // rows, fresh, 0.0).astype(NARROW)
    pick = iota((TALL, wouts * rows), 1) % rows == iota((TALL, wouts * rows), 0)
    fresh = jnp.dot(pick.astype(WIDE).astype(NARROW), fresh, preferred_element_type=WIDE)
    first, second = turn(fresh[:, :half], fresh[:, half:head], cos_ref[...], sin_ref[...])
    newkey = jnp.concatenate([first, second], 1).astype(NARROW)
    newval = fresh[:, head:].astype(NARROW)

    def against(keys):
        return lax.dot_general(q, keys, (((1,), (1,)), ((), ())), preferred_element_type=WIDE)

    row = iota((count, slots), 0) % rows
    lane = iota((count, slots), 1)
    length = jnp.zeros((count, slots), jnp.int32)
    for r in range(rows):
        length = jnp.where(row == r, len_ref[r], length)
    scores, valids = [], []
    for b in range(blocks):
        part = lax.rem(x + (blocks - b), blocks)
        valid = (part * peers + zh) * slots + lane < length
        s = jnp.zeros((count, slots), WIDE)
        for r in range(rows):
            s = jnp.where(row == r, against(kv_refs[b][0, r]), s)
        scores.append(jnp.where(valid, s * scale, NONE))
        valids.append(valid)
    own_slot = (count, TALL)
    self_valid = jnp.logical_and(iota(own_slot, 0) % rows == iota(own_slot, 1), zh == 0)
    self_score = jnp.where(self_valid, against(newkey) * scale, NONE)

    top = jnp.max(functools.reduce(jnp.maximum, scores), -1, keepdims=True)
    top = jnp.maximum(top, jnp.max(self_score, -1, keepdims=True))
    top_hi = top.astype(NARROW).astype(WIDE)
    top_lo = (top - top_hi).astype(NARROW).astype(WIDE)
    top = top_hi + top_lo
    weights = [jnp.where(v, jnp.exp(s - top), 0.0) for s, v in zip(scores, valids)]
    self_weight = jnp.where(self_valid, jnp.exp(self_score - top), 0.0)
    total = jnp.sum(functools.reduce(jnp.add, weights), -1, keepdims=True)
    total = total + jnp.sum(self_weight, -1, keepdims=True)
    total_hi = total.astype(NARROW).astype(WIDE)
    acc = jnp.dot(self_weight.astype(NARROW), newval, preferred_element_type=WIDE)
    for b in range(blocks):
        for r in range(rows):
            w = jnp.where(row == r, weights[b], 0.0).astype(NARROW)
            acc = acc + jnp.dot(w, kv_refs[b][1, r], preferred_element_type=WIDE)
    out_scr[:, :head] = acc
    part = iota((count, STATS), 1) // (STATS // 4)
    out_scr[:, head:] = jnp.where(
        part == 0, top_hi, jnp.where(part == 1, top_lo, jnp.where(part == 2, total_hi, total - total_hi))
    )
    out_ref[...] = out_scr[...].astype(NARROW).reshape(out_ref.shape)


def merged(head, own, rows, parts_ref, out_ref):
    peers = parts_ref.shape[0]
    parts = parts_ref[...].astype(WIDE)
    span = STATS // 4
    stat = [parts[:, :, head + i * span : head + i * span + 1] for i in range(4)]
    tops, totals = stat[0] + stat[1], stat[2] + stat[3]
    top = jnp.max(tops, 0)
    total = jnp.zeros_like(top)
    acc = jnp.zeros(parts.shape[1:2] + (head,), WIDE)
    for z in range(peers):
        factor = jnp.exp(tops[z] - top)
        total = total + factor * totals[z]
        acc = acc + factor * parts[z, :, :head]
    attended = acc / total
    for h in range(own):
        piece = attended[h * rows : (h + 1) * rows, :].astype(NARROW)
        for peer in range(out_ref.shape[0]):
            out_ref[peer, :, h * head : (h + 1) * head] = piece


def limit(mib):
    return pltpu.CompilerParams(vmem_limit_bytes=mib * 2**20)


def body(inputs, w_query, w_keyval, w_out, key_cache, value_cache, lengths, positions):
    rows, slots, head = key_cache.shape
    qcols = w_query.shape[1]
    own = qcols // head
    wins = lax.axis_size(WIN)
    chips = lax.axis_size(CHIP)
    peers = lax.axis_size("zh")
    wouts = lax.axis_size(WOUT)
    blocks = lax.axis_size("x")
    core = lax.axis_index("core")
    scale = head ** (-0.5)

    half = head // 2
    freq = 10000.0 ** (-(2.0 * jnp.arange(half, dtype=WIDE)) / head)
    place = jnp.pad(positions, (0, TALL - rows)).astype(WIDE)
    angle = place[:, None] * freq
    cosine = jnp.cos(angle)
    sine = jnp.sin(angle)

    def projected(value):
        return jnp.concatenate(
            [
                jnp.dot(value, w_query, preferred_element_type=WIDE),
                jnp.dot(value, w_keyval, preferred_element_type=WIDE),
            ],
            1,
        )

    halves = inputs.reshape(chips, 2, rows, -1)
    theirs = jnp.where(core == 0, halves[:, 1], halves[:, 0]).reshape(chips * rows, -1)
    ours = jnp.where(core == 0, halves[:, 0], halves[:, 1]).reshape(chips * rows, -1)
    theirs = lax.ppermute(projected(theirs).astype(NARROW), "core", [(0, 1), (1, 0)])
    partial = (projected(ours) + theirs.astype(WIDE)).astype(NARROW).reshape(chips, rows, -1)
    group = CHIP

    def around(value):
        return [value] + [
            lax.ppermute(value, "x", [(i, (i + k) % blocks) for i in range(blocks)])
            for k in range(1, blocks)
        ]

    held = lax.optimization_barrier((partial, key_cache, value_cache))
    partial = held[0]
    caches = around(jnp.stack(held[1:]))
    pieces = exchange(partial, group)
    message = pl.pallas_call(
        functools.partial(own_queries, head, own, rows),
        out_shape=jax.ShapeDtypeStruct((wouts,) + pieces.shape[1:], NARROW),
        in_specs=[VMEM] * 3,
        out_specs=VMEM,
        compiler_params=limit(4),
        name="own_queries",
    )(pieces, cosine, sine)
    got = exchange(message, WOUT)
    at = jnp.stack([lax.axis_index("x"), lax.axis_index("zh")]).astype(jnp.int32)
    count = peers * TALL
    message = pl.pallas_call(
        functools.partial(partial_attention, head, own, rows, slots, scale, blocks, peers),
        out_shape=jax.ShapeDtypeStruct((peers, TALL, head + STATS), NARROW),
        in_specs=[SMEM, SMEM] + [VMEM] * (3 + blocks),
        out_specs=VMEM,
        scratch_shapes=[
            pltpu.VMEM((count, head), WIDE),
            pltpu.VMEM((wouts * rows, w_keyval.shape[1]), WIDE),
            pltpu.VMEM((count, head + STATS), WIDE),
        ],
        compiler_params=limit(8),
        name="partial_attention",
    )(lengths, at, got, cosine, sine, *caches)
    parts = exchange(message, "zh")
    attended = pl.pallas_call(
        functools.partial(merged, head, own, rows),
        out_shape=jax.ShapeDtypeStruct((chips, rows, qcols), NARROW),
        in_specs=[VMEM],
        out_specs=VMEM,
        compiler_params=limit(4),
        name="merged",
    )(parts)

    mine = exchange(attended, CHIP)
    other = lax.ppermute(mine, "core", [(0, 1), (1, 0)])
    mixed = [
        jnp.dot(part.reshape(chips * rows, qcols), w_out, preferred_element_type=WIDE)
        .astype(NARROW)
        .reshape(wouts, -1, w_out.shape[1])
        for part in (mine, other)
    ]
    mixed = exchange(jnp.concatenate(mixed, 1), WOUT)
    mixed = jnp.sum(mixed.astype(WIDE), 0).reshape(2, -1, rows, w_out.shape[1])
    mixed = jnp.where(core == 0, mixed, mixed[::-1])
    return mixed.transpose(1, 0, 2, 3).reshape(-1, w_out.shape[1]).astype(NARROW)


def solution(mesh):
    parted = Mesh(mesh.devices.reshape(SIZES), AXES)
    placed = (
        P(None, WIN),
        P(WIN, WOUT),
        P(WIN, WOUT),
        P(WOUT, WIN),
        P(WIN, WOUT, None),
        P(WIN, WOUT, None),
        P(WIN),
        P(WIN),
    )
    return jax.shard_map(
        body, mesh=parted, in_specs=placed, out_specs=P(WOUT, WIN), check_vma=False
    )
```

```python
import functools

import jax
import jax.numpy as jnp
from jax import lax
from jax.experimental import pallas as pl
from jax.experimental.pallas import tpu as pltpu
from jax.sharding import Mesh
from jax.sharding import PartitionSpec as P

WIDE = jnp.float32
NARROW = jnp.bfloat16
AXES = ("zlo", "y", "core", "x", "zh")
SIZES = (4, 8, 2, 4, 4)
WIN = ("zlo", "y", "core")
CHIP = ("zlo", "y")
WOUT = ("x", "zh")
NONE = -1e30
STATS = 128
TALL = 16
CORES = [(0, 1), (1, 0)]
VMEM = pl.BlockSpec(memory_space=pltpu.VMEM)
SMEM = pl.BlockSpec(memory_space=pltpu.SMEM)


def exchange(pieces, axis):
    return lax.all_to_all(pieces, axis, 0, 0, tiled=True)


def turn(first, second, cosine, sine):
    return first * cosine - second * sine, first * sine + second * cosine


def projected(rows, core_ref, x_ref, q_ref, kv_ref, ours_ref, theirs_ref):
    first = core_ref[0] == 0
    cols = q_ref.shape[1]
    step = 256
    for start in range(0, cols + 1, step):
        if start < cols:
            terms = lax.dot_general(
                x_ref[...], q_ref[:, start : start + step], (((0,), (0,)), ((), ())), preferred_element_type=WIDE
            )
        else:
            terms = lax.dot_general(
                x_ref[...], kv_ref[...], (((0,), (1,)), ((), ())), preferred_element_type=WIDE
            )
        terms = terms.reshape(-1, 2 * rows, terms.shape[1])
        low, high = terms[:, :rows], terms[:, rows:]
        ours_ref[:, :, start : start + terms.shape[2]] = jnp.where(first, low, high)
        theirs_ref[:, :, start : start + terms.shape[2]] = jnp.where(first, high, low).astype(NARROW)


def mixed_parts(core_ref, rows_ref, own_ref, other_ref, out_ref):
    core = core_ref[0]
    rows = rows_ref[...].reshape(-1, rows_ref.shape[2])
    for at, w_ref in ((core, own_ref), (1 - core, other_ref)):
        part = lax.dot_general(rows, w_ref[...], (((1,), (1,)), ((), ())), preferred_element_type=WIDE)
        out_ref[at] = part.reshape(out_ref.shape[1:]).astype(NARROW)


def own_queries(head, own, rows, pieces_ref, cos_ref, sin_ref, out_ref):
    half = head // 2
    total = jnp.sum(pieces_ref[...].astype(WIDE), 0).astype(NARROW)
    cosine, sine = cos_ref[:rows, :], sin_ref[:rows, :]
    for h in range(own):
        start = h * head
        first = total[:, start : start + half].astype(WIDE)
        second = total[:, start + half : start + head].astype(WIDE)
        first, second = turn(first, second, cosine, sine)
        for peer in range(out_ref.shape[0]):
            out_ref[peer, :, start : start + half] = first.astype(NARROW)
            out_ref[peer, :, start + half : start + head] = second.astype(NARROW)
    for peer in range(out_ref.shape[0]):
        out_ref[peer, :, own * head :] = total[:, own * head :]


def partial_attention(head, own, rows, slots, scale, blocks, peers, len_ref, at_ref, got_ref, cos_ref, sin_ref, *refs):
    kv_refs = refs[:blocks]
    out_ref, q_scr, fresh_scr, out_scr = refs[blocks:]
    half = head // 2
    count = peers * TALL
    width = got_ref.shape[2] - own * head
    wouts = got_ref.shape[0]
    x, zh = at_ref[0], at_ref[1]
    q_scr[...] = jnp.zeros_like(q_scr)
    for z in range(peers):
        for h in range(own):
            at = z * TALL + h * rows
            q_scr[at : at + rows, :] = got_ref[x * peers + z, :, h * head : (h + 1) * head].astype(WIDE)
    q = q_scr[...].astype(NARROW)

    for o in range(wouts):
        fresh_scr[o * rows : (o + 1) * rows, :] = got_ref[o, :, own * head :].astype(WIDE)
    iota = functools.partial(lax.broadcasted_iota, jnp.int32)
    copies = iota((width, wouts * width), 1) % width == iota((width, wouts * width), 0)
    fresh = jnp.dot(fresh_scr[...].astype(NARROW), copies.astype(WIDE).astype(NARROW), preferred_element_type=WIDE)
    wide = (wouts * rows, wouts * width)
    fresh = jnp.where(iota(wide, 1) // width == iota(wide, 0) // rows, fresh, 0.0).astype(NARROW)
    pick = iota((TALL, wouts * rows), 1) % rows == iota((TALL, wouts * rows), 0)
    fresh = jnp.dot(pick.astype(WIDE).astype(NARROW), fresh, preferred_element_type=WIDE)
    first, second = turn(fresh[:, :half], fresh[:, half:head], cos_ref[...], sin_ref[...])
    newkey = jnp.concatenate([first, second], 1).astype(NARROW)
    newval = fresh[:, head:].astype(NARROW)

    def against(keys):
        return lax.dot_general(q, keys, (((1,), (1,)), ((), ())), preferred_element_type=WIDE)

    row = iota((count, slots), 0) % rows
    lane = iota((count, slots), 1)
    length = jnp.zeros((count, slots), jnp.int32)
    for r in range(rows):
        length = jnp.where(row == r, len_ref[r], length)
    scores, valids = [], []
    for b in range(blocks):
        part = lax.rem(x + (blocks - b), blocks)
        valid = (part * peers + zh) * slots + lane < length
        s = jnp.zeros((count, slots), WIDE)
        for r in range(rows):
            s = jnp.where(row == r, against(kv_refs[b][0, r]), s)
        scores.append(jnp.where(valid, s * scale, NONE))
        valids.append(valid)
    own_slot = (count, TALL)
    self_valid = jnp.logical_and(iota(own_slot, 0) % rows == iota(own_slot, 1), zh == 0)
    self_score = jnp.where(self_valid, against(newkey) * scale, NONE)

    top = jnp.max(functools.reduce(jnp.maximum, scores), -1, keepdims=True)
    top = jnp.maximum(top, jnp.max(self_score, -1, keepdims=True))
    top_hi = top.astype(NARROW).astype(WIDE)
    top_lo = (top - top_hi).astype(NARROW).astype(WIDE)
    top = top_hi + top_lo
    weights = [jnp.where(v, jnp.exp(s - top), 0.0) for s, v in zip(scores, valids)]
    self_weight = jnp.where(self_valid, jnp.exp(self_score - top), 0.0)
    total = jnp.sum(functools.reduce(jnp.add, weights), -1, keepdims=True)
    total = total + jnp.sum(self_weight, -1, keepdims=True)
    total_hi = total.astype(NARROW).astype(WIDE)
    acc = jnp.dot(self_weight.astype(NARROW), newval, preferred_element_type=WIDE)
    for b in range(blocks):
        for r in range(rows):
            w = jnp.where(row == r, weights[b], 0.0).astype(NARROW)
            acc = acc + jnp.dot(w, kv_refs[b][1, r], preferred_element_type=WIDE)
    out_scr[:, :head] = acc
    part = iota((count, STATS), 1) // (STATS // 4)
    out_scr[:, head:] = jnp.where(
        part == 0, top_hi, jnp.where(part == 1, top_lo, jnp.where(part == 2, total_hi, total - total_hi))
    )
    out_ref[...] = out_scr[...].astype(NARROW).reshape(out_ref.shape)


def merged(head, own, rows, parts_ref, out_ref):
    peers = parts_ref.shape[0]
    parts = parts_ref[...].astype(WIDE)
    span = STATS // 4
    stat = [parts[:, :, head + i * span : head + i * span + 1] for i in range(4)]
    tops, totals = stat[0] + stat[1], stat[2] + stat[3]
    top = jnp.max(tops, 0)
    total = jnp.zeros_like(top)
    acc = jnp.zeros(parts.shape[1:2] + (head,), WIDE)
    for z in range(peers):
        factor = jnp.exp(tops[z] - top)
        total = total + factor * totals[z]
        acc = acc + factor * parts[z, :, :head]
    attended = acc / total
    for h in range(own):
        piece = attended[h * rows : (h + 1) * rows, :].astype(NARROW)
        for peer in range(out_ref.shape[0]):
            out_ref[peer, :, h * head : (h + 1) * head] = piece


def limit(mib):
    return pltpu.CompilerParams(vmem_limit_bytes=mib * 2**20)


def body(inputs, w_query, w_keyval, w_out, key_cache, value_cache, lengths, positions):
    rows, slots, head = key_cache.shape
    qcols = w_query.shape[1]
    own = qcols // head
    chips = lax.axis_size(CHIP)
    peers = lax.axis_size("zh")
    wouts = lax.axis_size(WOUT)
    blocks = lax.axis_size("x")
    core = lax.axis_index("core")
    scale = head ** (-0.5)

    half = head // 2
    freq = 10000.0 ** (-(2.0 * jnp.arange(half, dtype=WIDE)) / head)
    place = jnp.pad(positions, (0, TALL - rows)).astype(WIDE)
    angle = place[:, None] * freq
    cosine = jnp.cos(angle)
    sine = jnp.sin(angle)

    ours, theirs = pl.pallas_call(
        functools.partial(projected, rows),
        out_shape=(
            jax.ShapeDtypeStruct((chips, rows, qcols + w_keyval.shape[1]), WIDE),
            jax.ShapeDtypeStruct((chips, rows, qcols + w_keyval.shape[1]), NARROW),
        ),
        in_specs=[SMEM] + [VMEM] * 3,
        out_specs=(VMEM, VMEM),
        compiler_params=limit(8),
        name="projected",
    )(core.reshape(1).astype(jnp.int32), inputs.T, w_query, w_keyval.T)
    theirs = lax.ppermute(theirs, "core", CORES)
    partial = (ours + theirs.astype(WIDE)).astype(NARROW)

    def around(value):
        return [value] + [
            lax.ppermute(value, "x", [(i, (i + k) % blocks) for i in range(blocks)])
            for k in range(1, blocks)
        ]

    partial, keys, values, w_turned = lax.optimization_barrier((partial, key_cache, value_cache, w_out.T))
    caches = around(jnp.stack([keys, values]))
    w_other = lax.ppermute(w_turned, "core", CORES)
    pieces = exchange(partial, CHIP)
    message = pl.pallas_call(
        functools.partial(own_queries, head, own, rows),
        out_shape=jax.ShapeDtypeStruct((wouts,) + pieces.shape[1:], NARROW),
        in_specs=[VMEM] * 3,
        out_specs=VMEM,
        compiler_params=limit(4),
        name="own_queries",
    )(pieces, cosine, sine)
    got = exchange(message, WOUT)
    at = jnp.stack([lax.axis_index("x"), lax.axis_index("zh")]).astype(jnp.int32)
    count = peers * TALL
    message = pl.pallas_call(
        functools.partial(partial_attention, head, own, rows, slots, scale, blocks, peers),
        out_shape=jax.ShapeDtypeStruct((peers, TALL, head + STATS), NARROW),
        in_specs=[SMEM, SMEM] + [VMEM] * (3 + blocks),
        out_specs=VMEM,
        scratch_shapes=[
            pltpu.VMEM((count, head), WIDE),
            pltpu.VMEM((wouts * rows, w_keyval.shape[1]), WIDE),
            pltpu.VMEM((count, head + STATS), WIDE),
        ],
        compiler_params=limit(8),
        name="partial_attention",
    )(lengths, at, got, cosine, sine, *caches)
    parts = exchange(message, "zh")
    attended = pl.pallas_call(
        functools.partial(merged, head, own, rows),
        out_shape=jax.ShapeDtypeStruct((chips, rows, qcols), NARROW),
        in_specs=[VMEM],
        out_specs=VMEM,
        compiler_params=limit(4),
        name="merged",
    )(parts)

    whole = exchange(attended, CHIP)
    mixed = pl.pallas_call(
        mixed_parts,
        out_shape=jax.ShapeDtypeStruct((2, wouts, 2 * rows, w_out.shape[1]), NARROW),
        in_specs=[SMEM] + [VMEM] * 3,
        out_specs=VMEM,
        compiler_params=limit(8),
        name="mixed_parts",
    )(core.reshape(1).astype(jnp.int32), whole, w_turned, w_other)
    mixed = exchange(mixed.reshape((2 * wouts,) + mixed.shape[2:]), ("core",) + WOUT)
    mixed = jnp.sum(mixed.reshape(2, wouts, 2, rows, -1).astype(WIDE), 1)
    return mixed.transpose(1, 0, 2, 3).reshape(-1, w_out.shape[1]).astype(NARROW)


def solution(mesh):
    parted = Mesh(mesh.devices.reshape(SIZES), AXES)
    placed = (
        P(None, WIN),
        P(WIN, WOUT),
        P(WIN, WOUT),
        P(WOUT, WIN),
        P(WIN, WOUT, None),
        P(WIN, WOUT, None),
        P(WIN),
        P(WIN),
    )
    return jax.shard_map(
        body, mesh=parted, in_specs=placed, out_specs=P(WOUT, WIN), check_vma=False
    )
```

```python
import functools

import jax
import jax.numpy as jnp
from jax import lax
from jax.experimental import pallas as pl
from jax.experimental.pallas import tpu as pltpu
from jax.sharding import Mesh
from jax.sharding import PartitionSpec as P

WIDE = jnp.float32
NARROW = jnp.bfloat16
AXES = ("zlo", "y", "core", "x", "zh")
SIZES = (4, 8, 2, 4, 4)
WIN = ("zlo", "y", "core")
CHIP = ("zlo", "y")
WOUT = ("x", "zh")
NONE = -1e30
STATS = 128
TALL = 16
CORES = [(0, 1), (1, 0)]
VMEM = pl.BlockSpec(memory_space=pltpu.VMEM)
SMEM = pl.BlockSpec(memory_space=pltpu.SMEM)


ZLO_ORDER = (2, 0, 1, 3)
ZH_ORDER = (3, 0, 1, 2)
CHIP_GROUP = [[zlo * SIZES[1] + y for zlo in ZLO_ORDER for y in range(SIZES[1])]]
ZH_GROUP = [list(ZH_ORDER)]
WOUT_ORDER = [x * SIZES[4] + zh for x in range(SIZES[3]) for zh in ZH_ORDER]
CORE_WOUT_GROUP = [[core * len(WOUT_ORDER) + o for core in range(2) for o in WOUT_ORDER]]


def exchange(pieces, axis, group):
    return lax.all_to_all(pieces, axis, 0, 0, axis_index_groups=group, tiled=True)


def turn(first, second, cosine, sine):
    return first * cosine - second * sine, first * sine + second * cosine


def projected(rows, core_ref, x_hbm, q_hbm, kv_hbm, ours_ref, theirs_ref, x_ref, q_ref, kv_ref, sems):
    pairs = ((x_hbm, x_ref), (q_hbm, q_ref), (kv_hbm, kv_ref))
    copies = [pltpu.make_async_copy(there, here, sems.at[i]) for i, (there, here) in enumerate(pairs)]
    for copy in copies:
        copy.start()
    for copy in copies:
        copy.wait()
    first = core_ref[0] == 0
    cols = q_ref.shape[1]
    step = 256
    for start in range(0, cols + 1, step):
        if start < cols:
            terms = lax.dot_general(
                x_ref[...], q_ref[:, start : start + step], (((0,), (0,)), ((), ())), preferred_element_type=WIDE
            )
        else:
            terms = lax.dot_general(
                x_ref[...], kv_ref[...], (((0,), (1,)), ((), ())), preferred_element_type=WIDE
            )
        terms = terms.reshape(-1, 2 * rows, terms.shape[1])
        terms = jnp.concatenate([terms[z * SIZES[1] : (z + 1) * SIZES[1]] for z in ZLO_ORDER], 0)
        low, high = terms[:, :rows], terms[:, rows:]
        ours_ref[:, :, start : start + terms.shape[2]] = jnp.where(first, low, high)
        theirs_ref[:, :, start : start + terms.shape[2]] = jnp.where(first, high, low).astype(NARROW)


def mixed_parts(core_ref, rows_ref, own_ref, other_ref, out_ref):
    core = core_ref[0]
    span = SIZES[1]
    blocks = [rows_ref[ZLO_ORDER.index(z) * span : (ZLO_ORDER.index(z) + 1) * span] for z in range(SIZES[0])]
    rows = jnp.concatenate(blocks, 0).reshape(-1, rows_ref.shape[2])
    for at, w_ref in ((core, own_ref), (1 - core, other_ref)):
        part = lax.dot_general(rows, w_ref[...], (((1,), (1,)), ((), ())), preferred_element_type=WIDE)
        part = part.reshape(out_ref.shape[1:]).astype(NARROW)
        for o, place in enumerate(WOUT_ORDER):
            out_ref[at, o] = part[place]


def own_queries(head, own, rows, pieces_ref, cos_ref, sin_ref, out_ref):
    half = head // 2
    total = jnp.sum(pieces_ref[...].astype(WIDE), 0).astype(NARROW)
    cosine, sine = cos_ref[:rows, :], sin_ref[:rows, :]
    for h in range(own):
        start = h * head
        first = total[:, start : start + half].astype(WIDE)
        second = total[:, start + half : start + head].astype(WIDE)
        first, second = turn(first, second, cosine, sine)
        for peer in range(out_ref.shape[0]):
            out_ref[peer, :, start : start + half] = first.astype(NARROW)
            out_ref[peer, :, start + half : start + head] = second.astype(NARROW)
    for peer in range(out_ref.shape[0]):
        out_ref[peer, :, own * head :] = total[:, own * head :]


def partial_attention(head, own, rows, slots, scale, blocks, peers, len_ref, at_ref, got_ref, cos_ref, sin_ref, *refs):
    kv_refs = refs[:blocks]
    out_ref, q_scr, fresh_scr, out_scr = refs[blocks:]
    half = head // 2
    count = peers * TALL
    width = got_ref.shape[2] - own * head
    wouts = got_ref.shape[0]
    x, zh = at_ref[0], at_ref[1]
    q_scr[...] = jnp.zeros_like(q_scr)
    for z in range(peers):
        for h in range(own):
            at = z * TALL + h * rows
            q_scr[at : at + rows, :] = got_ref[x * peers + z, :, h * head : (h + 1) * head].astype(WIDE)
    q = q_scr[...].astype(NARROW)

    for o in range(wouts):
        fresh_scr[o * rows : (o + 1) * rows, :] = got_ref[o, :, own * head :].astype(WIDE)
    iota = functools.partial(lax.broadcasted_iota, jnp.int32)
    copies = iota((width, wouts * width), 1) % width == iota((width, wouts * width), 0)
    fresh = jnp.dot(fresh_scr[...].astype(NARROW), copies.astype(WIDE).astype(NARROW), preferred_element_type=WIDE)
    wide = (wouts * rows, wouts * width)
    piece = iota(wide, 0) // rows
    piece = piece // peers * peers + (piece + ZH_ORDER[0]) % peers
    fresh = jnp.where(iota(wide, 1) // width == piece, fresh, 0.0).astype(NARROW)
    pick = iota((TALL, wouts * rows), 1) % rows == iota((TALL, wouts * rows), 0)
    fresh = jnp.dot(pick.astype(WIDE).astype(NARROW), fresh, preferred_element_type=WIDE)
    first, second = turn(fresh[:, :half], fresh[:, half:head], cos_ref[...], sin_ref[...])
    newkey = jnp.concatenate([first, second], 1).astype(NARROW)
    newval = fresh[:, head:].astype(NARROW)

    def against(keys):
        return lax.dot_general(q, keys, (((1,), (1,)), ((), ())), preferred_element_type=WIDE)

    row = iota((count, slots), 0) % rows
    lane = iota((count, slots), 1)
    length = jnp.zeros((count, slots), jnp.int32)
    for r in range(rows):
        length = jnp.where(row == r, len_ref[r], length)
    scores, valids = [], []
    for b in range(blocks):
        part = lax.rem(x + (blocks - b), blocks)
        valid = (part * peers + zh) * slots + lane < length
        s = jnp.zeros((count, slots), WIDE)
        for r in range(rows):
            s = jnp.where(row == r, against(kv_refs[b][0, r]), s)
        scores.append(jnp.where(valid, s * scale, NONE))
        valids.append(valid)
    own_slot = (count, TALL)
    self_valid = jnp.logical_and(iota(own_slot, 0) % rows == iota(own_slot, 1), zh == 0)
    self_score = jnp.where(self_valid, against(newkey) * scale, NONE)

    top = jnp.max(functools.reduce(jnp.maximum, scores), -1, keepdims=True)
    top = jnp.maximum(top, jnp.max(self_score, -1, keepdims=True))
    top_hi = top.astype(NARROW).astype(WIDE)
    top_lo = (top - top_hi).astype(NARROW).astype(WIDE)
    top = top_hi + top_lo
    weights = [jnp.where(v, jnp.exp(s - top), 0.0) for s, v in zip(scores, valids)]
    self_weight = jnp.where(self_valid, jnp.exp(self_score - top), 0.0)
    total = jnp.sum(functools.reduce(jnp.add, weights), -1, keepdims=True)
    total = total + jnp.sum(self_weight, -1, keepdims=True)
    total_hi = total.astype(NARROW).astype(WIDE)
    acc = jnp.dot(self_weight.astype(NARROW), newval, preferred_element_type=WIDE)
    for b in range(blocks):
        for r in range(rows):
            w = jnp.where(row == r, weights[b], 0.0).astype(NARROW)
            acc = acc + jnp.dot(w, kv_refs[b][1, r], preferred_element_type=WIDE)
    out_scr[:, :head] = acc
    part = iota((count, STATS), 1) // (STATS // 4)
    out_scr[:, head:] = jnp.where(
        part == 0, top_hi, jnp.where(part == 1, top_lo, jnp.where(part == 2, total_hi, total - total_hi))
    )
    out_ref[...] = out_scr[...].astype(NARROW).reshape(out_ref.shape)


def merged(head, own, rows, parts_ref, out_ref):
    peers = parts_ref.shape[0]
    parts = parts_ref[...].astype(WIDE)
    span = STATS // 4
    stat = [parts[:, :, head + i * span : head + i * span + 1] for i in range(4)]
    tops, totals = stat[0] + stat[1], stat[2] + stat[3]
    top = jnp.max(tops, 0)
    total = jnp.zeros_like(top)
    acc = jnp.zeros(parts.shape[1:2] + (head,), WIDE)
    for z in range(peers):
        factor = jnp.exp(tops[z] - top)
        total = total + factor * totals[z]
        acc = acc + factor * parts[z, :, :head]
    attended = acc / total
    for h in range(own):
        piece = attended[h * rows : (h + 1) * rows, :].astype(NARROW)
        for peer in range(out_ref.shape[0]):
            out_ref[peer, :, h * head : (h + 1) * head] = piece


def limit(mib):
    return pltpu.CompilerParams(vmem_limit_bytes=mib * 2**20)


def body(inputs, w_query, w_keyval, w_out, key_cache, value_cache, lengths, positions):
    rows, slots, head = key_cache.shape
    qcols = w_query.shape[1]
    own = qcols // head
    chips = lax.axis_size(CHIP)
    peers = lax.axis_size("zh")
    wouts = lax.axis_size(WOUT)
    blocks = lax.axis_size("x")
    core = lax.axis_index("core")
    scale = head ** (-0.5)

    half = head // 2
    freq = 10000.0 ** (-(2.0 * jnp.arange(half, dtype=WIDE)) / head)
    place = jnp.pad(positions, (0, TALL - rows)).astype(WIDE)
    angle = place[:, None] * freq
    cosine = jnp.cos(angle)
    sine = jnp.sin(angle)

    ours, theirs = pl.pallas_call(
        functools.partial(projected, rows),
        out_shape=(
            jax.ShapeDtypeStruct((chips, rows, qcols + w_keyval.shape[1]), WIDE),
            jax.ShapeDtypeStruct((chips, rows, qcols + w_keyval.shape[1]), NARROW),
        ),
        in_specs=[SMEM] + [pl.BlockSpec(memory_space=pl.ANY)] * 3,
        out_specs=(VMEM, VMEM),
        scratch_shapes=[
            pltpu.VMEM(inputs.shape[::-1], NARROW),
            pltpu.VMEM(w_query.shape, NARROW),
            pltpu.VMEM(w_keyval.shape[::-1], NARROW),
            pltpu.SemaphoreType.DMA((3,)),
        ],
        compiler_params=limit(56),
        name="projected",
    )(core.reshape(1).astype(jnp.int32), inputs.T, w_query, w_keyval.T)
    theirs = lax.ppermute(theirs, "core", CORES)
    partial = (ours + theirs.astype(WIDE)).astype(NARROW)

    def around(value):
        return [value] + [
            lax.ppermute(value, "x", [(i, (i + k) % blocks) for i in range(blocks)])
            for k in range(1, blocks)
        ]

    partial, keys, values, w_turned = lax.optimization_barrier((partial, key_cache, value_cache, w_out.T))
    caches = around(jnp.stack([keys, values]))
    w_other = lax.ppermute(w_turned, "core", CORES)
    pieces = exchange(partial, CHIP, CHIP_GROUP)
    message = pl.pallas_call(
        functools.partial(own_queries, head, own, rows),
        out_shape=jax.ShapeDtypeStruct((wouts,) + pieces.shape[1:], NARROW),
        in_specs=[VMEM] * 3,
        out_specs=VMEM,
        compiler_params=limit(4),
        name="own_queries",
    )(pieces, cosine, sine)
    message, w_other = lax.optimization_barrier((message, w_other))
    got = exchange(message, WOUT, [WOUT_ORDER])
    at = jnp.stack([lax.axis_index("x"), lax.axis_index("zh")]).astype(jnp.int32)
    count = peers * TALL
    message = pl.pallas_call(
        functools.partial(partial_attention, head, own, rows, slots, scale, blocks, peers),
        out_shape=jax.ShapeDtypeStruct((peers, TALL, head + STATS), NARROW),
        in_specs=[SMEM, SMEM] + [VMEM] * (3 + blocks),
        out_specs=VMEM,
        scratch_shapes=[
            pltpu.VMEM((count, head), WIDE),
            pltpu.VMEM((wouts * rows, w_keyval.shape[1]), WIDE),
            pltpu.VMEM((count, head + STATS), WIDE),
        ],
        compiler_params=limit(8),
        name="partial_attention",
    )(lengths, at, got, cosine, sine, *caches)
    parts = exchange(message, "zh", ZH_GROUP)
    attended = pl.pallas_call(
        functools.partial(merged, head, own, rows),
        out_shape=jax.ShapeDtypeStruct((chips, rows, qcols), NARROW),
        in_specs=[VMEM],
        out_specs=VMEM,
        compiler_params=limit(4),
        name="merged",
    )(parts)

    whole = exchange(attended, CHIP, CHIP_GROUP)
    mixed = pl.pallas_call(
        mixed_parts,
        out_shape=jax.ShapeDtypeStruct((2, wouts, 2 * rows, w_out.shape[1]), NARROW),
        in_specs=[SMEM] + [VMEM] * 3,
        out_specs=VMEM,
        compiler_params=limit(8),
        name="mixed_parts",
    )(core.reshape(1).astype(jnp.int32), whole, w_turned, w_other)
    mixed = exchange(mixed.reshape((2 * wouts,) + mixed.shape[2:]), ("core",) + WOUT, CORE_WOUT_GROUP)
    mixed = jnp.sum(mixed.reshape(2, wouts, 2, rows, -1).astype(WIDE), 1)
    return mixed.transpose(1, 0, 2, 3).reshape(-1, w_out.shape[1]).astype(NARROW)


def solution(mesh):
    parted = Mesh(mesh.devices.reshape(SIZES), AXES)
    placed = (
        P(None, WIN),
        P(WIN, WOUT),
        P(WIN, WOUT),
        P(WOUT, WIN),
        P(WIN, WOUT, None),
        P(WIN, WOUT, None),
        P(WIN),
        P(WIN),
    )
    return jax.shard_map(
        body, mesh=parted, in_specs=placed, out_specs=P(WOUT, WIN), check_vma=False
    )
```

```python
import functools

import jax
import jax.numpy as jnp
from jax import lax
from jax.experimental import pallas as pl
from jax.experimental.pallas import tpu as pltpu
from jax.sharding import Mesh
from jax.sharding import PartitionSpec as P

WIDE = jnp.float32
NARROW = jnp.bfloat16
AXES = ("zlo", "y", "core", "x", "zh")
SIZES = (4, 8, 2, 4, 4)
WIN = ("zlo", "y", "core")
CHIP = ("zlo", "y")
WOUT = ("x", "zh")
NONE = -1e30
STATS = 128
TALL = 16
CORES = [(0, 1), (1, 0)]
VMEM = pl.BlockSpec(memory_space=pltpu.VMEM)
SMEM = pl.BlockSpec(memory_space=pltpu.SMEM)


ZLO_ORDER = (2, 0, 1, 3)
ZH_ORDER = (3, 0, 1, 2)
CHIP_GROUP = [[zlo * SIZES[1] + y for zlo in ZLO_ORDER for y in range(SIZES[1])]]
ZH_GROUP = [list(ZH_ORDER)]
WOUT_ORDER = [x * SIZES[4] + zh for x in range(SIZES[3]) for zh in ZH_ORDER]
CORE_WOUT_GROUP = [[core * len(WOUT_ORDER) + o for core in range(2) for o in WOUT_ORDER]]


def exchange(pieces, axis, group):
    return lax.all_to_all(pieces, axis, 0, 0, axis_index_groups=group, tiled=True)


def turn(first, second, cosine, sine):
    return first * cosine - second * sine, first * sine + second * cosine


def mixed_parts(core_ref, rows_ref, own_ref, other_ref, out_ref):
    core = core_ref[0]
    span = SIZES[1]
    blocks = [rows_ref[ZLO_ORDER.index(z) * span : (ZLO_ORDER.index(z) + 1) * span] for z in range(SIZES[0])]
    rows = jnp.concatenate(blocks, 0).reshape(-1, rows_ref.shape[2])
    for at, w_ref in ((core, own_ref), (1 - core, other_ref)):
        part = lax.dot_general(rows, w_ref[...], (((1,), (1,)), ((), ())), preferred_element_type=WIDE)
        part = part.reshape(out_ref.shape[1:]).astype(NARROW)
        for o, place in enumerate(WOUT_ORDER):
            out_ref[at, o] = part[place]


def own_queries(head, own, rows, pieces_ref, cos_ref, sin_ref, out_ref):
    half = head // 2
    total = jnp.sum(pieces_ref[...].astype(WIDE), 0).astype(NARROW)
    cosine, sine = cos_ref[:rows, :], sin_ref[:rows, :]
    for h in range(own):
        start = h * head
        first = total[:, start : start + half].astype(WIDE)
        second = total[:, start + half : start + head].astype(WIDE)
        first, second = turn(first, second, cosine, sine)
        for peer in range(out_ref.shape[0]):
            out_ref[peer, :, start : start + half] = first.astype(NARROW)
            out_ref[peer, :, start + half : start + head] = second.astype(NARROW)
    for peer in range(out_ref.shape[0]):
        out_ref[peer, :, own * head :] = total[:, own * head :]


def partial_attention(head, own, rows, slots, scale, blocks, peers, len_ref, at_ref, got_ref, cos_ref, sin_ref, *refs):
    keys_ref, values_ref, out_ref, q_scr, fresh_scr, out_scr = refs
    half = head // 2
    count = peers * TALL
    width = got_ref.shape[2] - own * head
    wouts = got_ref.shape[0]
    x, zh = at_ref[0], at_ref[1]
    q_scr[...] = jnp.zeros_like(q_scr)
    for z in range(peers):
        for h in range(own):
            at = z * TALL + h * rows
            q_scr[at : at + rows, :] = got_ref[x * peers + z, :, h * head : (h + 1) * head].astype(WIDE)
    q = q_scr[...].astype(NARROW)

    for o in range(wouts):
        fresh_scr[o * rows : (o + 1) * rows, :] = got_ref[o, :, own * head :].astype(WIDE)
    iota = functools.partial(lax.broadcasted_iota, jnp.int32)
    copies = iota((width, wouts * width), 1) % width == iota((width, wouts * width), 0)
    fresh = jnp.dot(fresh_scr[...].astype(NARROW), copies.astype(WIDE).astype(NARROW), preferred_element_type=WIDE)
    wide = (wouts * rows, wouts * width)
    piece = iota(wide, 0) // rows
    piece = piece // peers * peers + (piece + ZH_ORDER[0]) % peers
    fresh = jnp.where(iota(wide, 1) // width == piece, fresh, 0.0).astype(NARROW)
    pick = iota((TALL, wouts * rows), 1) % rows == iota((TALL, wouts * rows), 0)
    fresh = jnp.dot(pick.astype(WIDE).astype(NARROW), fresh, preferred_element_type=WIDE)
    first, second = turn(fresh[:, :half], fresh[:, half:head], cos_ref[...], sin_ref[...])
    newkey = jnp.concatenate([first, second], 1).astype(NARROW)
    newval = fresh[:, head:].astype(NARROW)

    def against(keys):
        return lax.dot_general(q, keys, (((1,), (1,)), ((), ())), preferred_element_type=WIDE)

    row = iota((count, slots), 0) % rows
    lane = iota((count, slots), 1)
    length = jnp.zeros((count, slots), jnp.int32)
    for r in range(rows):
        length = jnp.where(row == r, len_ref[r], length)
    scores, valids = [], []
    for b in range(blocks):
        valid = (b * peers + zh) * slots + lane < length
        s = jnp.zeros((count, slots), WIDE)
        for r in range(rows):
            s = jnp.where(row == r, against(keys_ref[b, r]), s)
        scores.append(jnp.where(valid, s * scale, NONE))
        valids.append(valid)
    own_slot = (count, TALL)
    self_valid = jnp.logical_and(iota(own_slot, 0) % rows == iota(own_slot, 1), zh == 0)
    self_score = jnp.where(self_valid, against(newkey) * scale, NONE)

    top = jnp.max(functools.reduce(jnp.maximum, scores), -1, keepdims=True)
    top = jnp.maximum(top, jnp.max(self_score, -1, keepdims=True))
    top_hi = top.astype(NARROW).astype(WIDE)
    top_lo = (top - top_hi).astype(NARROW).astype(WIDE)
    top = top_hi + top_lo
    weights = [jnp.where(v, jnp.exp(s - top), 0.0) for s, v in zip(scores, valids)]
    self_weight = jnp.where(self_valid, jnp.exp(self_score - top), 0.0)
    total = jnp.sum(functools.reduce(jnp.add, weights), -1, keepdims=True)
    total = total + jnp.sum(self_weight, -1, keepdims=True)
    total_hi = total.astype(NARROW).astype(WIDE)
    acc = jnp.dot(self_weight.astype(NARROW), newval, preferred_element_type=WIDE)
    for b in range(blocks):
        for r in range(rows):
            w = jnp.where(row == r, weights[b], 0.0).astype(NARROW)
            acc = acc + jnp.dot(w, values_ref[b, r], preferred_element_type=WIDE)
    out_scr[:, :head] = acc
    part = iota((count, STATS), 1) // (STATS // 4)
    out_scr[:, head:] = jnp.where(
        part == 0, top_hi, jnp.where(part == 1, top_lo, jnp.where(part == 2, total_hi, total - total_hi))
    )
    out_ref[...] = out_scr[...].astype(NARROW).reshape(out_ref.shape)


def merged(head, own, rows, parts_ref, out_ref):
    peers = parts_ref.shape[0]
    parts = parts_ref[...].astype(WIDE)
    span = STATS // 4
    stat = [parts[:, :, head + i * span : head + i * span + 1] for i in range(4)]
    tops, totals = stat[0] + stat[1], stat[2] + stat[3]
    top = jnp.max(tops, 0)
    total = jnp.zeros_like(top)
    acc = jnp.zeros(parts.shape[1:2] + (head,), WIDE)
    for z in range(peers):
        factor = jnp.exp(tops[z] - top)
        total = total + factor * totals[z]
        acc = acc + factor * parts[z, :, :head]
    attended = acc / total
    for h in range(own):
        piece = attended[h * rows : (h + 1) * rows, :].astype(NARROW)
        for peer in range(out_ref.shape[0]):
            out_ref[peer, :, h * head : (h + 1) * head] = piece


def limit(mib):
    return pltpu.CompilerParams(vmem_limit_bytes=mib * 2**20)


def body(inputs, w_query, w_keyval, w_out, key_cache, value_cache, lengths, positions):
    rows, slots, head = key_cache.shape
    qcols = w_query.shape[1]
    own = qcols // head
    chips = lax.axis_size(CHIP)
    peers = lax.axis_size("zh")
    wouts = lax.axis_size(WOUT)
    blocks = lax.axis_size("x")
    core = lax.axis_index("core")
    scale = head ** (-0.5)

    half = head // 2
    freq = 10000.0 ** (-(2.0 * jnp.arange(half, dtype=WIDE)) / head)
    place = jnp.pad(positions, (0, TALL - rows)).astype(WIDE)
    angle = place[:, None] * freq
    cosine = jnp.cos(angle)
    sine = jnp.sin(angle)

    def projected(value):
        return jnp.concatenate(
            [
                jnp.dot(value, w_query, preferred_element_type=WIDE),
                jnp.dot(value, w_keyval, preferred_element_type=WIDE),
            ],
            1,
        )

    halves = inputs.reshape(SIZES[:3] + (rows, -1))
    halves = jnp.concatenate([halves[z] for z in ZLO_ORDER], 0)
    theirs = jnp.where(core == 0, halves[:, 1], halves[:, 0]).reshape(chips * rows, -1)
    ours = jnp.where(core == 0, halves[:, 0], halves[:, 1]).reshape(chips * rows, -1)
    theirs = lax.ppermute(projected(theirs).astype(NARROW), "core", CORES)
    partial = (projected(ours) + theirs.astype(WIDE)).astype(NARROW).reshape(chips, rows, -1)

    caches = [lax.all_gather(cache, "x") for cache in (key_cache, value_cache)]
    pieces = exchange(partial, CHIP, CHIP_GROUP)
    message = pl.pallas_call(
        functools.partial(own_queries, head, own, rows),
        out_shape=jax.ShapeDtypeStruct((wouts,) + pieces.shape[1:], NARROW),
        in_specs=[VMEM] * 3,
        out_specs=VMEM,
        compiler_params=limit(4),
        name="own_queries",
    )(pieces, cosine, sine)
    got = exchange(message, WOUT, [WOUT_ORDER])
    got, w_turned = lax.optimization_barrier((got, w_out.T))
    w_other = lax.ppermute(w_turned, "core", CORES)
    at = jnp.stack([lax.axis_index("x"), lax.axis_index("zh")]).astype(jnp.int32)
    count = peers * TALL
    message = pl.pallas_call(
        functools.partial(partial_attention, head, own, rows, slots, scale, blocks, peers),
        out_shape=jax.ShapeDtypeStruct((peers, TALL, head + STATS), NARROW),
        in_specs=[SMEM, SMEM] + [VMEM] * 5,
        out_specs=VMEM,
        scratch_shapes=[
            pltpu.VMEM((count, head), WIDE),
            pltpu.VMEM((wouts * rows, w_keyval.shape[1]), WIDE),
            pltpu.VMEM((count, head + STATS), WIDE),
        ],
        compiler_params=limit(8),
        name="partial_attention",
    )(lengths, at, got, cosine, sine, *caches)
    parts = exchange(message, "zh", ZH_GROUP)
    parts, w_other = lax.optimization_barrier((parts, w_other))
    attended = pl.pallas_call(
        functools.partial(merged, head, own, rows),
        out_shape=jax.ShapeDtypeStruct((chips, rows, qcols), NARROW),
        in_specs=[VMEM],
        out_specs=VMEM,
        compiler_params=limit(4),
        name="merged",
    )(parts)

    whole = exchange(attended, CHIP, CHIP_GROUP)
    mixed = pl.pallas_call(
        mixed_parts,
        out_shape=jax.ShapeDtypeStruct((2, wouts, 2 * rows, w_out.shape[1]), NARROW),
        in_specs=[SMEM] + [VMEM] * 3,
        out_specs=VMEM,
        compiler_params=limit(8),
        name="mixed_parts",
    )(core.reshape(1).astype(jnp.int32), whole, w_turned, w_other)
    mixed = exchange(mixed.reshape((2 * wouts,) + mixed.shape[2:]), ("core",) + WOUT, CORE_WOUT_GROUP)
    mixed = jnp.sum(mixed.reshape(2, wouts, 2, rows, -1).astype(WIDE), 1)
    return mixed.transpose(1, 0, 2, 3).reshape(-1, w_out.shape[1]).astype(NARROW)


def solution(mesh):
    parted = Mesh(mesh.devices.reshape(SIZES), AXES)
    placed = (
        P(None, WIN),
        P(WIN, WOUT),
        P(WIN, WOUT),
        P(WOUT, WIN),
        P(WIN, WOUT, None),
        P(WIN, WOUT, None),
        P(WIN),
        P(WIN),
    )
    return jax.shard_map(
        body, mesh=parted, in_specs=placed, out_specs=P(WOUT, WIN), check_vma=False
    )
```

```python
import functools

import jax
import jax.numpy as jnp
from jax import lax
from jax.experimental import pallas as pl
from jax.experimental.pallas import tpu as pltpu
from jax.sharding import Mesh
from jax.sharding import PartitionSpec as P

WIDE = jnp.float32
NARROW = jnp.bfloat16
AXES = ("zlo", "y", "core", "x", "zh")
SIZES = (4, 8, 2, 4, 4)
WIN = ("zlo", "y", "core")
CHIP = ("zlo", "y")
WOUT = ("x", "zh")
NONE = -1e30
TALL = 16
CORES = [(0, 1), (1, 0)]
VMEM = pl.BlockSpec(memory_space=pltpu.VMEM)
SMEM = pl.BlockSpec(memory_space=pltpu.SMEM)


ZLO_ORDER = (2, 0, 1, 3)
ZH_ORDER = (3, 0, 1, 2)
CHIP_GROUP = [[zlo * SIZES[1] + y for zlo in ZLO_ORDER for y in range(SIZES[1])]]
WOUT_ORDER = [x * SIZES[4] + zh for x in range(SIZES[3]) for zh in ZH_ORDER]
CORE_WOUT_GROUP = [[core * len(WOUT_ORDER) + o for core in range(2) for o in WOUT_ORDER]]


def exchange(pieces, axis, group):
    return lax.all_to_all(pieces, axis, 0, 0, axis_index_groups=group, tiled=True)


def turn(first, second, cosine, sine):
    return first * cosine - second * sine, first * sine + second * cosine


def mixed_parts(core_ref, rows_ref, own_ref, other_ref, out_ref):
    core = core_ref[0]
    span = SIZES[1]
    blocks = [rows_ref[ZLO_ORDER.index(z) * span : (ZLO_ORDER.index(z) + 1) * span] for z in range(SIZES[0])]
    rows = jnp.concatenate(blocks, 0).reshape(-1, rows_ref.shape[2])
    for at, w_ref in ((core, own_ref), (1 - core, other_ref)):
        part = lax.dot_general(rows, w_ref[...], (((1,), (1,)), ((), ())), preferred_element_type=WIDE)
        part = part.reshape(out_ref.shape[1:]).astype(NARROW)
        for o, place in enumerate(WOUT_ORDER):
            out_ref[at, o] = part[place]


def own_queries(head, own, rows, pieces_ref, cos_ref, sin_ref, out_ref):
    half = head // 2
    total = jnp.sum(pieces_ref[...].astype(WIDE), 0).astype(NARROW)
    cosine, sine = cos_ref[:rows, :], sin_ref[:rows, :]
    for h in range(own):
        start = h * head
        first = total[:, start : start + half].astype(WIDE)
        second = total[:, start + half : start + head].astype(WIDE)
        first, second = turn(first, second, cosine, sine)
        for peer in range(out_ref.shape[0]):
            out_ref[peer, :, start : start + half] = first.astype(NARROW)
            out_ref[peer, :, start + half : start + head] = second.astype(NARROW)
    for peer in range(out_ref.shape[0]):
        out_ref[peer, :, own * head :] = total[:, own * head :]


def partial_attention(head, own, rows, slots, scale, len_ref, at_ref, got_ref, cos_ref, sin_ref, keys_ref, values_ref, out_ref, q_scr, fresh_scr):
    half = head // 2
    wouts, _, width = got_ref.shape
    width = width - own * head
    count = wouts * TALL
    here = at_ref[0]
    q_scr[...] = jnp.zeros_like(q_scr)
    for o in range(wouts):
        for h in range(own):
            at = o * TALL + h * rows
            q_scr[at : at + rows, :] = got_ref[o, :, h * head : (h + 1) * head].astype(WIDE)
    q = q_scr[...].astype(NARROW)

    for o in range(wouts):
        fresh_scr[o * rows : (o + 1) * rows, :] = got_ref[o, :, own * head :].astype(WIDE)
    iota = functools.partial(lax.broadcasted_iota, jnp.int32)
    copies = iota((width, wouts * width), 1) % width == iota((width, wouts * width), 0)
    fresh = jnp.dot(fresh_scr[...].astype(NARROW), copies.astype(WIDE).astype(NARROW), preferred_element_type=WIDE)
    wide = (wouts * rows, wouts * width)
    piece = iota(wide, 0) // rows
    piece = piece // SIZES[4] * SIZES[4] + (piece + ZH_ORDER[0]) % SIZES[4]
    fresh = jnp.where(iota(wide, 1) // width == piece, fresh, 0.0).astype(NARROW)
    pick = iota((TALL, wouts * rows), 1) % rows == iota((TALL, wouts * rows), 0)
    fresh = jnp.dot(pick.astype(WIDE).astype(NARROW), fresh, preferred_element_type=WIDE)
    first, second = turn(fresh[:, :half], fresh[:, half:head], cos_ref[...], sin_ref[...])
    newkey = jnp.concatenate([first, second], 1).astype(NARROW)
    newval = fresh[:, head:].astype(NARROW)

    def against(keys):
        return lax.dot_general(q, keys, (((1,), (1,)), ((), ())), preferred_element_type=WIDE)

    row = iota((count, slots), 0) % rows
    length = jnp.zeros((count, slots), jnp.int32)
    scores = jnp.zeros((count, slots), WIDE)
    for r in range(rows):
        length = jnp.where(row == r, len_ref[r], length)
        scores = jnp.where(row == r, against(keys_ref[r]), scores)
    valid = here * slots + iota((count, slots), 1) < length
    scores = jnp.where(valid, scores * scale, NONE)
    own_slot = (count, TALL)
    self_valid = jnp.logical_and(iota(own_slot, 0) % rows == iota(own_slot, 1), here == 0)
    self_score = jnp.where(self_valid, against(newkey) * scale, NONE)

    top = jnp.maximum(jnp.max(scores, -1, keepdims=True), jnp.max(self_score, -1, keepdims=True))
    top_hi = top.astype(NARROW).astype(WIDE)
    top_lo = (top - top_hi).astype(NARROW).astype(WIDE)
    top = top_hi + top_lo
    weights = jnp.where(valid, jnp.exp(scores - top), 0.0)
    self_weight = jnp.where(self_valid, jnp.exp(self_score - top), 0.0)
    total = jnp.sum(weights, -1, keepdims=True) + jnp.sum(self_weight, -1, keepdims=True)
    total_hi = total.astype(NARROW).astype(WIDE)
    acc = jnp.dot(self_weight.astype(NARROW), newval, preferred_element_type=WIDE)
    for r in range(rows):
        w = jnp.where(row == r, weights, 0.0).astype(NARROW)
        acc = acc + jnp.dot(w, values_ref[r], preferred_element_type=WIDE)

    shape = (wouts, TALL, head)
    at_row, at_lane = iota(shape, 1), iota(shape, 2)
    message = acc.reshape(shape)
    for i, stat in enumerate((top_hi, top_lo, total_hi, total - total_hi)):
        line = jnp.where(at_row == at_lane, stat.reshape(wouts, TALL, 1), 0.0)
        message = jnp.where(at_row == own * rows + i, jnp.sum(line, 1, keepdims=True), message)
    out_ref[...] = message.astype(NARROW)


def merged(head, own, rows, parts_ref, out_ref):
    wouts = parts_ref.shape[0]
    parts = parts_ref[...].astype(WIDE)
    shape = parts.shape
    diagonal = lax.broadcasted_iota(jnp.int32, shape, 1) == lax.broadcasted_iota(jnp.int32, shape, 2)

    def column(i):
        line = parts[:, own * rows + i : own * rows + i + 1, :] + parts[:, own * rows + i + 1 : own * rows + i + 2, :]
        return jnp.sum(jnp.where(diagonal, line, 0.0), -1, keepdims=True)

    tops, totals = column(0), column(2)
    factors = jnp.exp(tops - jnp.max(tops, 0, keepdims=True))
    total = jnp.sum(factors * totals, 0)
    attended = jnp.sum(factors * parts, 0) / total
    for h in range(own):
        piece = attended[h * rows : (h + 1) * rows, :].astype(NARROW)
        for peer in range(out_ref.shape[0]):
            out_ref[peer, :, h * head : (h + 1) * head] = piece


def limit(mib):
    return pltpu.CompilerParams(vmem_limit_bytes=mib * 2**20)


def body(inputs, w_query, w_keyval, w_out, key_cache, value_cache, lengths, positions):
    rows, slots, head = key_cache.shape
    qcols = w_query.shape[1]
    own = qcols // head
    chips = lax.axis_size(CHIP)
    wouts = lax.axis_size(WOUT)
    core = lax.axis_index("core")
    scale = head ** (-0.5)

    half = head // 2
    freq = 10000.0 ** (-(2.0 * jnp.arange(half, dtype=WIDE)) / head)
    place = jnp.pad(positions, (0, TALL - rows)).astype(WIDE)
    angle = place[:, None] * freq
    cosine = jnp.cos(angle)
    sine = jnp.sin(angle)

    def projected(value):
        return jnp.concatenate(
            [
                jnp.dot(value, w_query, preferred_element_type=WIDE),
                jnp.dot(value, w_keyval, preferred_element_type=WIDE),
            ],
            1,
        )

    halves = inputs.reshape(SIZES[:3] + (rows, -1))
    halves = jnp.concatenate([halves[z] for z in ZLO_ORDER], 0)
    theirs = jnp.where(core == 0, halves[:, 1], halves[:, 0]).reshape(chips * rows, -1)
    ours = jnp.where(core == 0, halves[:, 0], halves[:, 1]).reshape(chips * rows, -1)
    theirs = lax.ppermute(projected(theirs).astype(NARROW), "core", CORES)
    partial = (projected(ours) + theirs.astype(WIDE)).astype(NARROW).reshape(chips, rows, -1)

    partial, w_turned = lax.optimization_barrier((partial, w_out.T))
    w_other = lax.ppermute(w_turned, "core", CORES)
    pieces = exchange(partial, CHIP, CHIP_GROUP)
    message = pl.pallas_call(
        functools.partial(own_queries, head, own, rows),
        out_shape=jax.ShapeDtypeStruct((wouts,) + pieces.shape[1:], NARROW),
        in_specs=[VMEM] * 3,
        out_specs=VMEM,
        compiler_params=limit(4),
        name="own_queries",
    )(pieces, cosine, sine)
    message, w_other = lax.optimization_barrier((message, w_other))
    got = exchange(message, WOUT, [WOUT_ORDER])
    at = lax.axis_index(WOUT).reshape(1).astype(jnp.int32)
    message = pl.pallas_call(
        functools.partial(partial_attention, head, own, rows, slots, scale),
        out_shape=jax.ShapeDtypeStruct((wouts, TALL, head), NARROW),
        in_specs=[SMEM, SMEM] + [VMEM] * 5,
        out_specs=VMEM,
        scratch_shapes=[
            pltpu.VMEM((wouts * TALL, head), WIDE),
            pltpu.VMEM((wouts * rows, w_keyval.shape[1]), WIDE),
        ],
        compiler_params=limit(8),
        name="partial_attention",
    )(lengths, at, got, cosine, sine, key_cache, value_cache)
    parts = exchange(message, WOUT, [WOUT_ORDER])
    attended = pl.pallas_call(
        functools.partial(merged, head, own, rows),
        out_shape=jax.ShapeDtypeStruct((chips, rows, qcols), NARROW),
        in_specs=[VMEM],
        out_specs=VMEM,
        compiler_params=limit(4),
        name="merged",
    )(parts)

    whole = exchange(attended, CHIP, CHIP_GROUP)
    mixed = pl.pallas_call(
        mixed_parts,
        out_shape=jax.ShapeDtypeStruct((2, wouts, 2 * rows, w_out.shape[1]), NARROW),
        in_specs=[SMEM] + [VMEM] * 3,
        out_specs=VMEM,
        compiler_params=limit(8),
        name="mixed_parts",
    )(core.reshape(1).astype(jnp.int32), whole, w_turned, w_other)
    mixed = exchange(mixed.reshape((2 * wouts,) + mixed.shape[2:]), ("core",) + WOUT, CORE_WOUT_GROUP)
    mixed = jnp.sum(mixed.reshape(2, wouts, 2, rows, -1).astype(WIDE), 1)
    return mixed.transpose(1, 0, 2, 3).reshape(-1, w_out.shape[1]).astype(NARROW)


def solution(mesh):
    parted = Mesh(mesh.devices.reshape(SIZES), AXES)
    placed = (
        P(None, WIN),
        P(WIN, WOUT),
        P(WIN, WOUT),
        P(WOUT, WIN),
        P(WIN, WOUT, None),
        P(WIN, WOUT, None),
        P(WIN),
        P(WIN),
    )
    return jax.shard_map(
        body, mesh=parted, in_specs=placed, out_specs=P(WOUT, WIN), check_vma=False
    )
```

```python
import functools

import jax
import jax.numpy as jnp
from jax import lax
from jax.experimental import pallas as pl
from jax.experimental.pallas import tpu as pltpu
from jax.sharding import Mesh
from jax.sharding import PartitionSpec as P

WIDE = jnp.float32
NARROW = jnp.bfloat16
AXES = ("zlo", "y", "core", "x", "zh")
SIZES = (4, 8, 2, 4, 4)
WIN = ("zlo", "y", "core")
CHIP = ("zlo", "y")
WOUT = ("x", "zh")
NONE = -1e30
TALL = 16
CORES = [(0, 1), (1, 0)]
VMEM = pl.BlockSpec(memory_space=pltpu.VMEM)
SMEM = pl.BlockSpec(memory_space=pltpu.SMEM)


ZLO_FIRST = 2
ZH_ORDER = (3, 0, 1, 2)
CHIP_GROUP = [[(ZLO_FIRST + z) % SIZES[0] * SIZES[1] + y for z in range(SIZES[0]) for y in range(SIZES[1])]]
WOUT_ORDER = [x * SIZES[4] + zh for x in range(SIZES[3]) for zh in ZH_ORDER]
CORE_WOUT_GROUP = [[core * len(WOUT_ORDER) + o for core in range(2) for o in WOUT_ORDER]]


def exchange(pieces, axis, group):
    return lax.all_to_all(pieces, axis, 0, 0, axis_index_groups=group, tiled=True)


def turn(first, second, cosine, sine):
    return first * cosine - second * sine, first * sine + second * cosine


def mixed_parts(core_ref, rows_ref, own_ref, other_ref, out_ref):
    core = core_ref[0]
    split = rows_ref.shape[0] - ZLO_FIRST * SIZES[1]
    rows = jnp.concatenate([rows_ref[split:], rows_ref[:split]], 0).reshape(-1, rows_ref.shape[2])
    for at, w_ref in ((core, own_ref), (1 - core, other_ref)):
        part = lax.dot_general(rows, w_ref[...], (((1,), (1,)), ((), ())), preferred_element_type=WIDE)
        part = part.reshape(out_ref.shape[1:]).astype(NARROW)
        for o, place in enumerate(WOUT_ORDER):
            out_ref[at, o] = part[place]


def own_queries(head, own, rows, pieces_ref, cos_ref, sin_ref, out_ref, scr):
    half = head // 2
    total = jnp.sum(pieces_ref[...].astype(WIDE), 0).astype(NARROW).astype(WIDE)
    cosine, sine = cos_ref[:rows, :], sin_ref[:rows, :]
    scr[...] = jnp.zeros_like(scr)
    for h in range(own):
        start = h * head
        first, second = turn(total[:, start : start + half], total[:, start + half : start + head], cosine, sine)
        scr[h * rows : (h + 1) * rows, :half] = first
        scr[h * rows : (h + 1) * rows, half:] = second
    fresh = total[:, own * head :]
    scr[own * rows : (own + 1) * rows, : fresh.shape[1]] = fresh
    out_ref[...] = jnp.broadcast_to(scr[...].astype(NARROW)[None], out_ref.shape)


def partial_attention(head, own, rows, slots, scale, len_ref, at_ref, got_ref, cos_ref, sin_ref, keys_ref, values_ref, out_ref):
    half = head // 2
    wouts = got_ref.shape[0]
    width = 2 * head // wouts
    count = wouts * TALL
    here = at_ref[0]
    q = got_ref[...].reshape(count, head)

    iota = functools.partial(lax.broadcasted_iota, jnp.int32)
    wide = (count, wouts * width)
    copies = iota((head, wouts * width), 1) % width == iota((head, wouts * width), 0)
    fresh = jnp.dot(q, copies.astype(WIDE).astype(NARROW), preferred_element_type=WIDE)
    piece = iota(wide, 0) // TALL
    piece = piece // SIZES[4] * SIZES[4] + (piece + ZH_ORDER[0]) % SIZES[4]
    fresh = jnp.where(iota(wide, 1) // width == piece, fresh, 0.0).astype(NARROW)
    pick = iota((TALL, count), 1) % TALL == iota((TALL, count), 0) + own * rows
    fresh = jnp.dot(pick.astype(WIDE).astype(NARROW), fresh, preferred_element_type=WIDE)
    first, second = turn(fresh[:, :half], fresh[:, half:head], cos_ref[...], sin_ref[...])
    newkey = jnp.concatenate([first, second], 1).astype(NARROW)
    newval = fresh[:, head:].astype(NARROW)

    def against(keys):
        return lax.dot_general(q, keys, (((1,), (1,)), ((), ())), preferred_element_type=WIDE)

    row = iota((count, slots), 0) % rows
    length = jnp.zeros((count, slots), jnp.int32)
    scores = jnp.zeros((count, slots), WIDE)
    for r in range(rows):
        length = jnp.where(row == r, len_ref[r], length)
        scores = jnp.where(row == r, against(keys_ref[r]), scores)
    valid = here * slots + iota((count, slots), 1) < length
    scores = jnp.where(valid, scores * scale, NONE)
    own_slot = (count, TALL)
    self_valid = jnp.logical_and(iota(own_slot, 0) % rows == iota(own_slot, 1), here == 0)
    self_score = jnp.where(self_valid, against(newkey) * scale, NONE)

    top = jnp.maximum(jnp.max(scores, -1, keepdims=True), jnp.max(self_score, -1, keepdims=True))
    top_hi = top.astype(NARROW).astype(WIDE)
    top_lo = (top - top_hi).astype(NARROW).astype(WIDE)
    top = top_hi + top_lo
    weights = jnp.where(valid, jnp.exp(scores - top), 0.0)
    self_weight = jnp.where(self_valid, jnp.exp(self_score - top), 0.0)
    total = jnp.sum(weights, -1, keepdims=True) + jnp.sum(self_weight, -1, keepdims=True)
    total_hi = total.astype(NARROW).astype(WIDE)
    acc = jnp.dot(self_weight.astype(NARROW), newval, preferred_element_type=WIDE)
    for r in range(rows):
        w = jnp.where(row == r, weights, 0.0).astype(NARROW)
        acc = acc + jnp.dot(w, values_ref[r], preferred_element_type=WIDE)

    shape = (wouts, TALL, head)
    at_row, at_lane = iota(shape, 1), iota(shape, 2)
    message = acc.reshape(shape)
    for i, stat in enumerate((top_hi, top_lo, total_hi, total - total_hi)):
        line = jnp.where(at_row == at_lane, stat.reshape(wouts, TALL, 1), 0.0)
        message = jnp.where(at_row == own * rows + i, jnp.sum(line, 1, keepdims=True), message)
    out_ref[...] = message.astype(NARROW)


def merged(head, own, rows, parts_ref, out_ref):
    wouts = parts_ref.shape[0]
    parts = parts_ref[...].astype(WIDE)
    shape = parts.shape
    diagonal = lax.broadcasted_iota(jnp.int32, shape, 1) == lax.broadcasted_iota(jnp.int32, shape, 2)

    def column(i):
        line = parts[:, own * rows + i : own * rows + i + 1, :] + parts[:, own * rows + i + 1 : own * rows + i + 2, :]
        return jnp.sum(jnp.where(diagonal, line, 0.0), -1, keepdims=True)

    tops, totals = column(0), column(2)
    factors = jnp.exp(tops - jnp.max(tops, 0, keepdims=True))
    total = jnp.sum(factors * totals, 0)
    attended = jnp.sum(factors * parts, 0) / total
    for h in range(own):
        piece = attended[h * rows : (h + 1) * rows, :].astype(NARROW)
        for peer in range(out_ref.shape[0]):
            out_ref[peer, :, h * head : (h + 1) * head] = piece


def limit(mib):
    return pltpu.CompilerParams(vmem_limit_bytes=mib * 2**20)


def body(inputs, w_query, w_keyval, w_out, key_cache, value_cache, lengths, positions):
    rows, slots, head = key_cache.shape
    qcols = w_query.shape[1]
    own = qcols // head
    chips = lax.axis_size(CHIP)
    wouts = lax.axis_size(WOUT)
    core = lax.axis_index("core")
    scale = head ** (-0.5)

    half = head // 2
    freq = 10000.0 ** (-(2.0 * jnp.arange(half, dtype=WIDE)) / head)
    place = jnp.pad(positions, (0, TALL - rows)).astype(WIDE)
    angle = place[:, None] * freq
    cosine = jnp.cos(angle)
    sine = jnp.sin(angle)

    def projected(value):
        return jnp.concatenate(
            [
                jnp.dot(value, w_query, preferred_element_type=WIDE),
                jnp.dot(value, w_keyval, preferred_element_type=WIDE),
            ],
            1,
        )

    split = ZLO_FIRST * SIZES[1] * 2 * rows
    halves = jnp.concatenate([inputs[split:], inputs[:split]], 0).reshape(chips, 2, rows, -1)
    theirs = jnp.where(core == 0, halves[:, 1], halves[:, 0]).reshape(chips * rows, -1)
    ours = jnp.where(core == 0, halves[:, 0], halves[:, 1]).reshape(chips * rows, -1)
    theirs = lax.ppermute(projected(theirs).astype(NARROW), "core", CORES)
    partial = (projected(ours) + theirs.astype(WIDE)).astype(NARROW).reshape(chips, rows, -1)

    at = lax.axis_index(WOUT).reshape(1).astype(jnp.int32)
    partial, w_turned, at = lax.optimization_barrier((partial, w_out.T, at))
    w_other = lax.ppermute(w_turned, "core", CORES)
    pieces = exchange(partial, CHIP, CHIP_GROUP)
    message = pl.pallas_call(
        functools.partial(own_queries, head, own, rows),
        out_shape=jax.ShapeDtypeStruct((wouts, TALL, head), NARROW),
        in_specs=[VMEM] * 3,
        out_specs=VMEM,
        scratch_shapes=[pltpu.VMEM((TALL, head), WIDE)],
        compiler_params=limit(4),
        name="own_queries",
    )(pieces, cosine, sine)
    message, w_other = lax.optimization_barrier((message, w_other))
    got = exchange(message, WOUT, [WOUT_ORDER])
    message = pl.pallas_call(
        functools.partial(partial_attention, head, own, rows, slots, scale),
        out_shape=jax.ShapeDtypeStruct((wouts, TALL, head), NARROW),
        in_specs=[SMEM, SMEM] + [VMEM] * 5,
        out_specs=VMEM,
        compiler_params=limit(8),
        name="partial_attention",
    )(lengths, at, got, cosine, sine, key_cache, value_cache)
    parts = exchange(message, WOUT, [WOUT_ORDER])
    attended = pl.pallas_call(
        functools.partial(merged, head, own, rows),
        out_shape=jax.ShapeDtypeStruct((chips, rows, qcols), NARROW),
        in_specs=[VMEM],
        out_specs=VMEM,
        compiler_params=limit(4),
        name="merged",
    )(parts)

    whole = exchange(attended, CHIP, CHIP_GROUP)
    mixed = pl.pallas_call(
        mixed_parts,
        out_shape=jax.ShapeDtypeStruct((2, wouts, 2 * rows, w_out.shape[1]), NARROW),
        in_specs=[SMEM] + [VMEM] * 3,
        out_specs=VMEM,
        compiler_params=limit(8),
        name="mixed_parts",
    )(core.reshape(1).astype(jnp.int32), whole, w_turned, w_other)
    mixed = exchange(mixed.reshape((2 * wouts,) + mixed.shape[2:]), ("core",) + WOUT, CORE_WOUT_GROUP)
    mixed = jnp.sum(mixed.reshape(2, wouts, 2, rows, -1).astype(WIDE), 1)
    return mixed.transpose(1, 0, 2, 3).reshape(-1, w_out.shape[1]).astype(NARROW)


def solution(mesh):
    parted = Mesh(mesh.devices.reshape(SIZES), AXES)
    placed = (
        P(None, WIN),
        P(WIN, WOUT),
        P(WIN, WOUT),
        P(WOUT, WIN),
        P(WIN, WOUT, None),
        P(WIN, WOUT, None),
        P(WIN),
        P(WIN),
    )
    return jax.shard_map(
        body, mesh=parted, in_specs=placed, out_specs=P(WOUT, WIN), check_vma=False
    )
```

```python
import functools

import jax
import jax.numpy as jnp
from jax import lax
from jax.experimental import pallas as pl
from jax.experimental.pallas import tpu as pltpu
from jax.sharding import Mesh
from jax.sharding import PartitionSpec as P

WIDE = jnp.float32
NARROW = jnp.bfloat16
AXES = ("zlo", "y", "core", "x", "zh")
SIZES = (4, 8, 2, 4, 4)
WIN = ("zlo", "y", "core")
CHIP = ("zlo", "y")
WOUT = ("x", "zh")
NONE = -1e30
TALL = 16
SELF_INDEX = 9
CORES = [(0, 1), (1, 0)]
VMEM = pl.BlockSpec(memory_space=pltpu.VMEM)
SMEM = pl.BlockSpec(memory_space=pltpu.SMEM)


ZLO_FIRST = 2
ZH_ORDER = (3, 0, 1, 2)
CHIP_GROUP = [[(ZLO_FIRST + z) % SIZES[0] * SIZES[1] + y for z in range(SIZES[0]) for y in range(SIZES[1])]]
WOUT_ORDER = [x * SIZES[4] + zh for x in range(SIZES[3]) for zh in ZH_ORDER]


def exchange(pieces, axis, group):
    return lax.all_to_all(pieces, axis, 0, 0, axis_index_groups=group, tiled=True)


def turn(first, second, cosine, sine):
    return first * cosine - second * sine, first * sine + second * cosine


def mixed_parts(core_ref, rows_ref, own_ref, other_ref, out_ref):
    core = core_ref[0]
    split = rows_ref.shape[0] - ZLO_FIRST * SIZES[1]
    rows = jnp.concatenate([rows_ref[split:], rows_ref[:split]], 0).reshape(-1, rows_ref.shape[2])
    for at, w_ref in ((core, own_ref), (1 - core, other_ref)):
        part = lax.dot_general(rows, w_ref[...], (((1,), (1,)), ((), ())), preferred_element_type=WIDE)
        part = part.reshape(out_ref.shape[:1] + out_ref.shape[2:]).astype(NARROW)
        for o, place in enumerate(WOUT_ORDER):
            out_ref[o, at] = part[place]


def own_sums(core_ref, parts_ref, keep_ref, send_ref):
    core = core_ref[0]
    sums = jnp.sum(parts_ref[...].astype(WIDE), 0)
    half = sums.shape[0] // 2
    low, high = sums[:half], sums[half:]
    keep_ref[...] = jnp.where(core == 0, low, high).astype(NARROW)
    send_ref[...] = jnp.where(core == 0, high, low).astype(NARROW)


def all_rows(rows, core_ref, keep_ref, got_ref, out_ref):
    core = core_ref[0]
    keep, got = keep_ref[...].astype(WIDE), got_ref[...].astype(WIDE)
    sides = jnp.where(core == 0, keep, got), jnp.where(core == 0, got, keep)
    pieces = [side[chip * rows : (chip + 1) * rows] for chip in range(2) for side in sides]
    out_ref[...] = jnp.concatenate(pieces, 0).astype(NARROW)


def own_queries(head, own, rows, pieces_ref, cos_ref, sin_ref, out_ref, scr):
    half = head // 2
    total = jnp.sum(pieces_ref[...].astype(WIDE), 0).astype(NARROW).astype(WIDE)
    cosine, sine = cos_ref[:rows, :], sin_ref[:rows, :]
    scr[...] = jnp.zeros_like(scr)
    for h in range(own):
        start = h * head
        first, second = turn(total[:, start : start + half], total[:, start + half : start + head], cosine, sine)
        scr[h * rows : (h + 1) * rows, :half] = first
        scr[h * rows : (h + 1) * rows, half:] = second
    fresh = total[:, own * head :]
    scr[own * rows : (own + 1) * rows, : fresh.shape[1]] = fresh
    out_ref[...] = jnp.broadcast_to(scr[...].astype(NARROW)[None], out_ref.shape)


def partial_attention(head, own, rows, slots, scale, len_ref, at_ref, got_ref, cos_ref, sin_ref, keys_ref, values_ref, out_ref, self_scr, value_scr):
    half = head // 2
    wouts = got_ref.shape[0]
    width = 2 * head // wouts
    count = wouts * TALL
    here = at_ref[0]
    q = got_ref[...].reshape(count, head)

    iota = functools.partial(lax.broadcasted_iota, jnp.int32)

    def against(keys):
        return lax.dot_general(q, keys, (((1,), (1,)), ((), ())), preferred_element_type=WIDE)

    own_slot = (count, TALL)
    self_valid = jnp.logical_and(iota(own_slot, 0) % rows == iota(own_slot, 1), here == SELF_INDEX)
    self_scr[...] = jnp.full(own_slot, NONE, WIDE)
    value_scr[...] = jnp.zeros_like(value_scr)

    @pl.when(here == SELF_INDEX)
    def _():
        wide = (count, wouts * width)
        copies = iota((head, wouts * width), 1) % width == iota((head, wouts * width), 0)
        fresh = jnp.dot(q, copies.astype(WIDE).astype(NARROW), preferred_element_type=WIDE)
        piece = iota(wide, 0) // TALL
        piece = piece // SIZES[4] * SIZES[4] + (piece + ZH_ORDER[0]) % SIZES[4]
        fresh = jnp.where(iota(wide, 1) // width == piece, fresh, 0.0).astype(NARROW)
        pick = iota((TALL, count), 1) % TALL == iota((TALL, count), 0) + own * rows
        fresh = jnp.dot(pick.astype(WIDE).astype(NARROW), fresh, preferred_element_type=WIDE)
        first, second = turn(fresh[:, :half], fresh[:, half:head], cos_ref[...], sin_ref[...])
        newkey = jnp.concatenate([first, second], 1).astype(NARROW)
        self_scr[...] = jnp.where(self_valid, against(newkey) * scale, NONE)
        value_scr[...] = fresh[:, head:].astype(NARROW)

    row = iota((count, slots), 0) % rows
    length = jnp.zeros((count, slots), jnp.int32)
    scores = jnp.zeros((count, slots), WIDE)
    for r in range(rows):
        length = jnp.where(row == r, len_ref[r], length)
        scores = jnp.where(row == r, against(keys_ref[r]), scores)
    valid = here * slots + iota((count, slots), 1) < length
    scores = jnp.where(valid, scores * scale, NONE)
    self_score = self_scr[...]

    top = jnp.maximum(jnp.max(scores, -1, keepdims=True), jnp.max(self_score, -1, keepdims=True))
    top_hi = top.astype(NARROW).astype(WIDE)
    top_lo = (top - top_hi).astype(NARROW).astype(WIDE)
    top = top_hi + top_lo
    weights = jnp.where(valid, jnp.exp(scores - top), 0.0)
    self_weight = jnp.where(self_valid, jnp.exp(self_score - top), 0.0)
    total = jnp.sum(weights, -1, keepdims=True) + jnp.sum(self_weight, -1, keepdims=True)
    total_hi = total.astype(NARROW).astype(WIDE)
    acc = jnp.dot(self_weight.astype(NARROW), value_scr[...], preferred_element_type=WIDE)
    for r in range(rows):
        w = jnp.where(row == r, weights, 0.0).astype(NARROW)
        acc = acc + jnp.dot(w, values_ref[r], preferred_element_type=WIDE)

    shape = (wouts, TALL, head)
    at_row, at_lane = iota(shape, 1), iota(shape, 2)
    message = acc.reshape(shape)
    for i, stat in enumerate((top_hi, top_lo, total_hi, total - total_hi)):
        line = jnp.where(at_row == at_lane, stat.reshape(wouts, TALL, 1), 0.0)
        message = jnp.where(at_row == own * rows + i, jnp.sum(line, 1, keepdims=True), message)
    out_ref[...] = message.astype(NARROW)


def merged(head, own, rows, parts_ref, out_ref):
    wouts = parts_ref.shape[0]
    parts = parts_ref[...].astype(WIDE)
    shape = parts.shape
    diagonal = lax.broadcasted_iota(jnp.int32, shape, 1) == lax.broadcasted_iota(jnp.int32, shape, 2)

    def column(i):
        line = parts[:, own * rows + i : own * rows + i + 1, :] + parts[:, own * rows + i + 1 : own * rows + i + 2, :]
        return jnp.sum(jnp.where(diagonal, line, 0.0), -1, keepdims=True)

    tops, totals = column(0), column(2)
    factors = jnp.exp(tops - jnp.max(tops, 0, keepdims=True))
    total = jnp.sum(factors * totals, 0)
    attended = jnp.sum(factors * parts, 0) / total
    for h in range(own):
        piece = attended[h * rows : (h + 1) * rows, :].astype(NARROW)
        for peer in range(out_ref.shape[0]):
            out_ref[peer, :, h * head : (h + 1) * head] = piece


def limit(mib):
    return pltpu.CompilerParams(vmem_limit_bytes=mib * 2**20)


def body(inputs, w_query, w_keyval, w_out, key_cache, value_cache, lengths, positions):
    rows, slots, head = key_cache.shape
    qcols = w_query.shape[1]
    own = qcols // head
    chips = lax.axis_size(CHIP)
    wouts = lax.axis_size(WOUT)
    core = lax.axis_index("core")
    scale = head ** (-0.5)

    half = head // 2
    freq = 10000.0 ** (-(2.0 * jnp.arange(half, dtype=WIDE)) / head)
    place = jnp.pad(positions, (0, TALL - rows)).astype(WIDE)
    angle = place[:, None] * freq
    cosine = jnp.cos(angle)
    sine = jnp.sin(angle)

    def projected(value):
        return jnp.concatenate(
            [
                jnp.dot(value, w_query, preferred_element_type=WIDE),
                jnp.dot(value, w_keyval, preferred_element_type=WIDE),
            ],
            1,
        )

    split = ZLO_FIRST * SIZES[1] * 2 * rows
    halves = jnp.concatenate([inputs[split:], inputs[:split]], 0).reshape(chips, 2, rows, -1)
    theirs = jnp.where(core == 0, halves[:, 1], halves[:, 0]).reshape(chips * rows, -1)
    ours = jnp.where(core == 0, halves[:, 0], halves[:, 1]).reshape(chips * rows, -1)
    theirs = lax.ppermute(projected(theirs).astype(NARROW), "core", CORES)
    partial = (projected(ours) + theirs.astype(WIDE)).astype(NARROW).reshape(chips, rows, -1)

    at = lax.axis_index(WOUT).reshape(1).astype(jnp.int32)
    core_at = core.reshape(1).astype(jnp.int32)
    partial, w_turned, at, core_at = lax.optimization_barrier((partial, w_out.T, at, core_at))
    w_other = lax.ppermute(w_turned, "core", CORES)
    pieces = exchange(partial, CHIP, CHIP_GROUP)
    message = pl.pallas_call(
        functools.partial(own_queries, head, own, rows),
        out_shape=jax.ShapeDtypeStruct((wouts, TALL, head), NARROW),
        in_specs=[VMEM] * 3,
        out_specs=VMEM,
        scratch_shapes=[pltpu.VMEM((TALL, head), WIDE)],
        compiler_params=limit(4),
        name="own_queries",
    )(pieces, cosine, sine)
    message, w_other = lax.optimization_barrier((message, w_other))
    got = exchange(message, WOUT, [WOUT_ORDER])
    message = pl.pallas_call(
        functools.partial(partial_attention, head, own, rows, slots, scale),
        out_shape=jax.ShapeDtypeStruct((wouts, TALL, head), NARROW),
        in_specs=[SMEM, SMEM] + [VMEM] * 5,
        out_specs=VMEM,
        scratch_shapes=[pltpu.VMEM((wouts * TALL, TALL), WIDE), pltpu.VMEM((TALL, head), NARROW)],
        compiler_params=limit(8),
        name="partial_attention",
    )(lengths, at, got, cosine, sine, key_cache, value_cache)
    parts = exchange(message, WOUT, [WOUT_ORDER])
    attended = pl.pallas_call(
        functools.partial(merged, head, own, rows),
        out_shape=jax.ShapeDtypeStruct((chips, rows, qcols), NARROW),
        in_specs=[VMEM],
        out_specs=VMEM,
        compiler_params=limit(4),
        name="merged",
    )(parts)

    whole = exchange(attended, CHIP, CHIP_GROUP)
    mixed = pl.pallas_call(
        mixed_parts,
        out_shape=jax.ShapeDtypeStruct((wouts, 2, 2 * rows, w_out.shape[1]), NARROW),
        in_specs=[SMEM] + [VMEM] * 3,
        out_specs=VMEM,
        compiler_params=limit(8),
        name="mixed_parts",
    )(core_at, whole, w_turned, w_other)
    mixed = exchange(mixed.reshape(wouts, 4 * rows, -1), WOUT, [WOUT_ORDER])
    side = jax.ShapeDtypeStruct((2 * rows, w_out.shape[1]), NARROW)
    keep, send = pl.pallas_call(
        own_sums,
        out_shape=(side, side),
        in_specs=[SMEM, VMEM],
        out_specs=(VMEM, VMEM),
        compiler_params=limit(8),
        name="own_sums",
    )(core_at, mixed)
    return pl.pallas_call(
        functools.partial(all_rows, rows),
        out_shape=jax.ShapeDtypeStruct((4 * rows, w_out.shape[1]), NARROW),
        in_specs=[SMEM] + [VMEM] * 2,
        out_specs=VMEM,
        compiler_params=limit(8),
        name="all_rows",
    )(core_at, keep, lax.ppermute(send, "core", CORES))


def solution(mesh):
    parted = Mesh(mesh.devices.reshape(SIZES), AXES)
    placed = (
        P(None, WIN),
        P(WIN, WOUT),
        P(WIN, WOUT),
        P(WOUT, WIN),
        P(WIN, WOUT, None),
        P(WIN, WOUT, None),
        P(WIN),
        P(WIN),
    )
    return jax.shard_map(
        body, mesh=parted, in_specs=placed, out_specs=P(WOUT, WIN), check_vma=False
    )
```

```python
import functools

import jax
import jax.numpy as jnp
from jax import lax
from jax.experimental import pallas as pl
from jax.experimental.pallas import tpu as pltpu
from jax.sharding import Mesh
from jax.sharding import PartitionSpec as P

WIDE = jnp.float32
NARROW = jnp.bfloat16
AXES = ("zlo", "y", "core", "x", "zh")
SIZES = (4, 8, 2, 4, 4)
WIN = ("zlo", "y", "core")
CHIP = ("zlo", "y")
WOUT = ("x", "zh")
NONE = -1e30
TALL = 16
SELF_INDEX = 9
CORES = [(0, 1), (1, 0)]
VMEM = pl.BlockSpec(memory_space=pltpu.VMEM)
SMEM = pl.BlockSpec(memory_space=pltpu.SMEM)


ZLO_FIRST = 2
ZH_ORDER = (3, 0, 1, 2)
CHIP_GROUP = [[(ZLO_FIRST + z) % SIZES[0] * SIZES[1] + y for z in range(SIZES[0]) for y in range(SIZES[1])]]
WOUT_ORDER = [x * SIZES[4] + zh for x in range(SIZES[3]) for zh in ZH_ORDER]
CORE_WOUT_GROUP = [[core * len(WOUT_ORDER) + o for core in range(2) for o in WOUT_ORDER]]


def exchange(pieces, axis, group):
    return lax.all_to_all(pieces, axis, 0, 0, axis_index_groups=group, tiled=True)


def turn(first, second, cosine, sine):
    return first * cosine - second * sine, first * sine + second * cosine


def projected(rows, core_ref, x_ref, q_ref, kv_ref, ours_ref, theirs_ref):
    first = core_ref[0] == 0
    cols = q_ref.shape[1]
    step = 256
    for start in range(0, cols + 1, step):
        if start < cols:
            terms = lax.dot_general(
                x_ref[...], q_ref[:, start : start + step], (((0,), (0,)), ((), ())), preferred_element_type=WIDE
            )
        else:
            terms = lax.dot_general(
                x_ref[...], kv_ref[...], (((0,), (1,)), ((), ())), preferred_element_type=WIDE
            )
        terms = terms.reshape(-1, 2 * rows, terms.shape[1])
        low, high = terms[:, :rows], terms[:, rows:]
        ours_ref[:, :, start : start + terms.shape[2]] = jnp.where(first, low, high)
        theirs_ref[:, :, start : start + terms.shape[2]] = jnp.where(first, high, low).astype(NARROW)


def mixed_parts(core_ref, rows_ref, own_ref, other_ref, out_ref):
    core = core_ref[0]
    split = rows_ref.shape[0] - ZLO_FIRST * SIZES[1]
    rows = jnp.concatenate([rows_ref[split:], rows_ref[:split]], 0).reshape(-1, rows_ref.shape[2])
    for at, w_ref in ((core, own_ref), (1 - core, other_ref)):
        part = lax.dot_general(rows, w_ref[...], (((1,), (1,)), ((), ())), preferred_element_type=WIDE)
        part = part.reshape(out_ref.shape[1:]).astype(NARROW)
        for o, place in enumerate(WOUT_ORDER):
            out_ref[at, o] = part[place]


def own_rows(rows, parts_ref, out_ref):
    half = parts_ref.shape[0] // 2
    sums = [jnp.sum(parts_ref[c * half : (c + 1) * half].astype(WIDE), 0) for c in range(2)]
    pieces = [sums[c][chip * rows : (chip + 1) * rows] for chip in range(2) for c in range(2)]
    out_ref[...] = jnp.concatenate(pieces, 0).astype(NARROW)


def own_queries(head, own, rows, pieces_ref, cos_ref, sin_ref, out_ref, scr):
    half = head // 2
    total = jnp.sum(pieces_ref[...].astype(WIDE), 0).astype(NARROW).astype(WIDE)
    cosine, sine = cos_ref[:rows, :], sin_ref[:rows, :]
    scr[...] = jnp.zeros_like(scr)
    for h in range(own):
        start = h * head
        first, second = turn(total[:, start : start + half], total[:, start + half : start + head], cosine, sine)
        scr[h * rows : (h + 1) * rows, :half] = first
        scr[h * rows : (h + 1) * rows, half:] = second
    fresh = total[:, own * head :]
    scr[own * rows : (own + 1) * rows, : fresh.shape[1]] = fresh
    out_ref[...] = jnp.broadcast_to(scr[...].astype(NARROW)[None], out_ref.shape)


def partial_attention(head, own, rows, slots, scale, len_ref, at_ref, got_ref, cos_ref, sin_ref, keys_ref, values_ref, out_ref, self_scr, value_scr):
    half = head // 2
    wouts = got_ref.shape[0]
    width = 2 * head // wouts
    count = wouts * TALL
    here = at_ref[0]
    q = got_ref[...].reshape(count, head)

    iota = functools.partial(lax.broadcasted_iota, jnp.int32)

    def against(keys):
        return lax.dot_general(q, keys, (((1,), (1,)), ((), ())), preferred_element_type=WIDE)

    own_slot = (count, TALL)
    self_valid = jnp.logical_and(iota(own_slot, 0) % rows == iota(own_slot, 1), here == SELF_INDEX)
    self_scr[...] = jnp.full(own_slot, NONE, WIDE)
    value_scr[...] = jnp.zeros_like(value_scr)

    @pl.when(here == SELF_INDEX)
    def _():
        wide = (count, wouts * width)
        copies = iota((head, wouts * width), 1) % width == iota((head, wouts * width), 0)
        fresh = jnp.dot(q, copies.astype(WIDE).astype(NARROW), preferred_element_type=WIDE)
        piece = iota(wide, 0) // TALL
        piece = piece // SIZES[4] * SIZES[4] + (piece + ZH_ORDER[0]) % SIZES[4]
        fresh = jnp.where(iota(wide, 1) // width == piece, fresh, 0.0).astype(NARROW)
        pick = iota((TALL, count), 1) % TALL == iota((TALL, count), 0) + own * rows
        fresh = jnp.dot(pick.astype(WIDE).astype(NARROW), fresh, preferred_element_type=WIDE)
        first, second = turn(fresh[:, :half], fresh[:, half:head], cos_ref[...], sin_ref[...])
        newkey = jnp.concatenate([first, second], 1).astype(NARROW)
        self_scr[...] = jnp.where(self_valid, against(newkey) * scale, NONE)
        value_scr[...] = fresh[:, head:].astype(NARROW)

    row = iota((count, slots), 0) % rows
    length = jnp.zeros((count, slots), jnp.int32)
    scores = jnp.zeros((count, slots), WIDE)
    for r in range(rows):
        length = jnp.where(row == r, len_ref[r], length)
        scores = jnp.where(row == r, against(keys_ref[r]), scores)
    valid = here * slots + iota((count, slots), 1) < length
    scores = jnp.where(valid, scores * scale, NONE)
    self_score = self_scr[...]

    top = jnp.maximum(jnp.max(scores, -1, keepdims=True), jnp.max(self_score, -1, keepdims=True))
    top_hi = top.astype(NARROW).astype(WIDE)
    top_lo = (top - top_hi).astype(NARROW).astype(WIDE)
    top = top_hi + top_lo
    weights = jnp.where(valid, jnp.exp(scores - top), 0.0)
    self_weight = jnp.where(self_valid, jnp.exp(self_score - top), 0.0)
    total = jnp.sum(weights, -1, keepdims=True) + jnp.sum(self_weight, -1, keepdims=True)
    total_hi = total.astype(NARROW).astype(WIDE)
    acc = jnp.dot(self_weight.astype(NARROW), value_scr[...], preferred_element_type=WIDE)
    for r in range(rows):
        w = jnp.where(row == r, weights, 0.0).astype(NARROW)
        acc = acc + jnp.dot(w, values_ref[r], preferred_element_type=WIDE)

    shape = (wouts, TALL, head)
    at_row, at_lane = iota(shape, 1), iota(shape, 2)
    message = acc.reshape(shape)
    for i, stat in enumerate((top_hi, top_lo, total_hi, total - total_hi)):
        line = jnp.where(at_row == at_lane, stat.reshape(wouts, TALL, 1), 0.0)
        message = jnp.where(at_row == own * rows + i, jnp.sum(line, 1, keepdims=True), message)
    out_ref[...] = message.astype(NARROW)


def merged(head, own, rows, parts_ref, out_ref):
    wouts = parts_ref.shape[0]
    parts = parts_ref[...].astype(WIDE)
    shape = parts.shape
    diagonal = lax.broadcasted_iota(jnp.int32, shape, 1) == lax.broadcasted_iota(jnp.int32, shape, 2)

    def column(i):
        line = parts[:, own * rows + i : own * rows + i + 1, :] + parts[:, own * rows + i + 1 : own * rows + i + 2, :]
        return jnp.sum(jnp.where(diagonal, line, 0.0), -1, keepdims=True)

    tops, totals = column(0), column(2)
    factors = jnp.exp(tops - jnp.max(tops, 0, keepdims=True))
    total = jnp.sum(factors * totals, 0)
    attended = jnp.sum(factors * parts, 0) / total
    for h in range(own):
        piece = attended[h * rows : (h + 1) * rows, :].astype(NARROW)
        for peer in range(out_ref.shape[0]):
            out_ref[peer, :, h * head : (h + 1) * head] = piece


def limit(mib):
    return pltpu.CompilerParams(vmem_limit_bytes=mib * 2**20)


def body(inputs, w_query, w_keyval, w_out, key_cache, value_cache, lengths, positions):
    rows, slots, head = key_cache.shape
    qcols = w_query.shape[1]
    own = qcols // head
    chips = lax.axis_size(CHIP)
    wouts = lax.axis_size(WOUT)
    core = lax.axis_index("core")
    scale = head ** (-0.5)

    half = head // 2
    freq = 10000.0 ** (-(2.0 * jnp.arange(half, dtype=WIDE)) / head)
    place = jnp.pad(positions, (0, TALL - rows)).astype(WIDE)
    angle = place[:, None] * freq
    cosine = jnp.cos(angle)
    sine = jnp.sin(angle)

    split = ZLO_FIRST * SIZES[1] * 2 * rows
    rolled = jnp.concatenate([inputs[split:], inputs[:split]], 0)
    core_at = core.reshape(1).astype(jnp.int32)
    shape = (chips, rows, qcols + w_keyval.shape[1])
    ours, theirs = pl.pallas_call(
        functools.partial(projected, rows),
        out_shape=(jax.ShapeDtypeStruct(shape, WIDE), jax.ShapeDtypeStruct(shape, NARROW)),
        in_specs=[SMEM] + [VMEM] * 3,
        out_specs=(VMEM, VMEM),
        compiler_params=limit(8),
        name="projected",
    )(core_at, rolled.T, w_query, w_keyval.T)
    theirs = lax.ppermute(theirs, "core", CORES)
    partial = (ours + theirs.astype(WIDE)).astype(NARROW)

    at = lax.axis_index(WOUT).reshape(1).astype(jnp.int32)
    partial, w_turned, at = lax.optimization_barrier((partial, w_out.T, at))
    w_other = lax.ppermute(w_turned, "core", CORES)
    pieces = exchange(partial, CHIP, CHIP_GROUP)
    message = pl.pallas_call(
        functools.partial(own_queries, head, own, rows),
        out_shape=jax.ShapeDtypeStruct((wouts, TALL, head), NARROW),
        in_specs=[VMEM] * 3,
        out_specs=VMEM,
        scratch_shapes=[pltpu.VMEM((TALL, head), WIDE)],
        compiler_params=limit(4),
        name="own_queries",
    )(pieces, cosine, sine)
    message, w_other = lax.optimization_barrier((message, w_other))
    got = exchange(message, WOUT, [WOUT_ORDER])
    message = pl.pallas_call(
        functools.partial(partial_attention, head, own, rows, slots, scale),
        out_shape=jax.ShapeDtypeStruct((wouts, TALL, head), NARROW),
        in_specs=[SMEM, SMEM] + [VMEM] * 5,
        out_specs=VMEM,
        scratch_shapes=[pltpu.VMEM((wouts * TALL, TALL), WIDE), pltpu.VMEM((TALL, head), NARROW)],
        compiler_params=limit(8),
        name="partial_attention",
    )(lengths, at, got, cosine, sine, key_cache, value_cache)
    parts = exchange(message, WOUT, [WOUT_ORDER])
    attended = pl.pallas_call(
        functools.partial(merged, head, own, rows),
        out_shape=jax.ShapeDtypeStruct((chips, rows, qcols), NARROW),
        in_specs=[VMEM],
        out_specs=VMEM,
        compiler_params=limit(4),
        name="merged",
    )(parts)

    whole = exchange(attended, CHIP, CHIP_GROUP)
    mixed = pl.pallas_call(
        mixed_parts,
        out_shape=jax.ShapeDtypeStruct((2, wouts, 2 * rows, w_out.shape[1]), NARROW),
        in_specs=[SMEM] + [VMEM] * 3,
        out_specs=VMEM,
        compiler_params=limit(8),
        name="mixed_parts",
    )(core_at, whole, w_turned, w_other)
    mixed = exchange(mixed.reshape((2 * wouts,) + mixed.shape[2:]), ("core",) + WOUT, CORE_WOUT_GROUP)
    return pl.pallas_call(
        functools.partial(own_rows, rows),
        out_shape=jax.ShapeDtypeStruct((4 * rows, mixed.shape[2]), NARROW),
        in_specs=[VMEM],
        out_specs=VMEM,
        compiler_params=limit(8),
        name="own_rows",
    )(mixed)


def solution(mesh):
    parted = Mesh(mesh.devices.reshape(SIZES), AXES)
    placed = (
        P(None, WIN),
        P(WIN, WOUT),
        P(WIN, WOUT),
        P(WOUT, WIN),
        P(WIN, WOUT, None),
        P(WIN, WOUT, None),
        P(WIN),
        P(WIN),
    )
    return jax.shard_map(
        body, mesh=parted, in_specs=placed, out_specs=P(WOUT, WIN), check_vma=False
    )
```

```python
import functools

import jax
import jax.numpy as jnp
from jax import lax
from jax.experimental import pallas as pl
from jax.experimental.pallas import tpu as pltpu
from jax.sharding import Mesh
from jax.sharding import PartitionSpec as P

WIDE = jnp.float32
NARROW = jnp.bfloat16
AXES = ("zlo", "y", "core", "x", "zh")
SIZES = (4, 8, 2, 4, 4)
WIN = ("zlo", "y", "core")
CHIP = ("zlo", "y")
WOUT = ("x", "zh")
NONE = -1e30
TALL = 16
SELF_INDEX = 9
CORES = [(0, 1), (1, 0)]
VMEM = pl.BlockSpec(memory_space=pltpu.VMEM)
SMEM = pl.BlockSpec(memory_space=pltpu.SMEM)


ZLO_FIRST = 2
ZH_ORDER = (3, 0, 1, 2)
CHIP_GROUP = [[(ZLO_FIRST + z) % SIZES[0] * SIZES[1] + y for z in range(SIZES[0]) for y in range(SIZES[1])]]
WOUT_ORDER = [x * SIZES[4] + zh for x in range(SIZES[3]) for zh in ZH_ORDER]
CORE_WOUT_GROUP = [[core * len(WOUT_ORDER) + o for core in range(2) for o in WOUT_ORDER]]


def exchange(pieces, axis, group):
    return lax.all_to_all(pieces, axis, 0, 0, axis_index_groups=group, tiled=True)


def turn(first, second, cosine, sine):
    return first * cosine - second * sine, first * sine + second * cosine


def projected(rows, ours, core_ref, x_ref, q_ref, kv_hbm, out_ref, kv_ref, sem):
    copy = pltpu.make_async_copy(kv_hbm, kv_ref, sem)
    copy.start()
    first = (core_ref[0] == 0) == ours
    cols = q_ref.shape[1]
    step = 256
    for start in range(0, cols + 1, step):
        if start < cols:
            terms = lax.dot_general(
                x_ref[...], q_ref[:, start : start + step], (((0,), (0,)), ((), ())), preferred_element_type=WIDE
            )
        else:
            copy.wait()
            terms = lax.dot_general(
                x_ref[...], kv_ref[...], (((0,), (1,)), ((), ())), preferred_element_type=WIDE
            )
        terms = terms.reshape(-1, 2 * rows, terms.shape[1])
        terms = jnp.where(first, terms[:, :rows], terms[:, rows:])
        out_ref[:, :, start : start + terms.shape[2]] = terms.astype(out_ref.dtype)


def mixed_parts(core_ref, rows_ref, own_ref, other_ref, out_ref):
    core = core_ref[0]
    split = rows_ref.shape[0] - ZLO_FIRST * SIZES[1]
    rows = jnp.concatenate([rows_ref[split:], rows_ref[:split]], 0).reshape(-1, rows_ref.shape[2])
    for at, w_ref in ((core, own_ref), (1 - core, other_ref)):
        part = lax.dot_general(rows, w_ref[...], (((1,), (1,)), ((), ())), preferred_element_type=WIDE)
        part = part.reshape(out_ref.shape[1:]).astype(NARROW)
        for o, place in enumerate(WOUT_ORDER):
            out_ref[at, o] = part[place]


def own_rows(rows, parts_ref, out_ref):
    half = parts_ref.shape[0] // 2
    sums = [jnp.sum(parts_ref[c * half : (c + 1) * half].astype(WIDE), 0) for c in range(2)]
    pieces = [sums[c][chip * rows : (chip + 1) * rows] for chip in range(2) for c in range(2)]
    out_ref[...] = jnp.concatenate(pieces, 0).astype(NARROW)


def own_queries(head, own, rows, pieces_ref, cos_ref, sin_ref, out_ref, scr):
    half = head // 2
    total = jnp.sum(pieces_ref[...].astype(WIDE), 0).astype(NARROW).astype(WIDE)
    cosine, sine = cos_ref[:rows, :], sin_ref[:rows, :]
    scr[...] = jnp.zeros_like(scr)
    for h in range(own):
        start = h * head
        first, second = turn(total[:, start : start + half], total[:, start + half : start + head], cosine, sine)
        scr[h * rows : (h + 1) * rows, :half] = first
        scr[h * rows : (h + 1) * rows, half:] = second
    fresh = total[:, own * head :]
    scr[own * rows : (own + 1) * rows, : fresh.shape[1]] = fresh
    out_ref[...] = jnp.broadcast_to(scr[...].astype(NARROW)[None], out_ref.shape)


def partial_attention(head, own, rows, slots, scale, len_ref, at_ref, got_ref, cos_ref, sin_ref, keys_ref, values_ref, out_ref, self_scr, value_scr):
    half = head // 2
    wouts = got_ref.shape[0]
    width = 2 * head // wouts
    count = wouts * TALL
    here = at_ref[0]
    q = got_ref[...].reshape(count, head)

    iota = functools.partial(lax.broadcasted_iota, jnp.int32)

    def against(keys):
        return lax.dot_general(q, keys, (((1,), (1,)), ((), ())), preferred_element_type=WIDE)

    own_slot = (count, TALL)
    self_valid = jnp.logical_and(iota(own_slot, 0) % rows == iota(own_slot, 1), here == SELF_INDEX)
    self_scr[...] = jnp.full(own_slot, NONE, WIDE)
    value_scr[...] = jnp.zeros_like(value_scr)

    @pl.when(here == SELF_INDEX)
    def _():
        wide = (count, wouts * width)
        copies = iota((head, wouts * width), 1) % width == iota((head, wouts * width), 0)
        fresh = jnp.dot(q, copies.astype(WIDE).astype(NARROW), preferred_element_type=WIDE)
        piece = iota(wide, 0) // TALL
        piece = piece // SIZES[4] * SIZES[4] + (piece + ZH_ORDER[0]) % SIZES[4]
        fresh = jnp.where(iota(wide, 1) // width == piece, fresh, 0.0).astype(NARROW)
        pick = iota((TALL, count), 1) % TALL == iota((TALL, count), 0) + own * rows
        fresh = jnp.dot(pick.astype(WIDE).astype(NARROW), fresh, preferred_element_type=WIDE)
        first, second = turn(fresh[:, :half], fresh[:, half:head], cos_ref[...], sin_ref[...])
        newkey = jnp.concatenate([first, second], 1).astype(NARROW)
        self_scr[...] = jnp.where(self_valid, against(newkey) * scale, NONE)
        value_scr[...] = fresh[:, head:].astype(NARROW)

    row = iota((count, slots), 0) % rows
    length = jnp.zeros((count, slots), jnp.int32)
    scores = jnp.zeros((count, slots), WIDE)
    for r in range(rows):
        length = jnp.where(row == r, len_ref[r], length)
        scores = jnp.where(row == r, against(keys_ref[r]), scores)
    valid = here * slots + iota((count, slots), 1) < length
    scores = jnp.where(valid, scores * scale, NONE)
    self_score = self_scr[...]

    top = jnp.maximum(jnp.max(scores, -1, keepdims=True), jnp.max(self_score, -1, keepdims=True))
    top_hi = top.astype(NARROW).astype(WIDE)
    top_lo = (top - top_hi).astype(NARROW).astype(WIDE)
    top = top_hi + top_lo
    weights = jnp.where(valid, jnp.exp(scores - top), 0.0)
    self_weight = jnp.where(self_valid, jnp.exp(self_score - top), 0.0)
    total = jnp.sum(weights, -1, keepdims=True) + jnp.sum(self_weight, -1, keepdims=True)
    total_hi = total.astype(NARROW).astype(WIDE)
    acc = jnp.dot(self_weight.astype(NARROW), value_scr[...], preferred_element_type=WIDE)
    for r in range(rows):
        w = jnp.where(row == r, weights, 0.0).astype(NARROW)
        acc = acc + jnp.dot(w, values_ref[r], preferred_element_type=WIDE)

    shape = (wouts, TALL, head)
    at_row, at_lane = iota(shape, 1), iota(shape, 2)
    message = acc.reshape(shape)
    for i, stat in enumerate((top_hi, top_lo, total_hi, total - total_hi)):
        line = jnp.where(at_row == at_lane, stat.reshape(wouts, TALL, 1), 0.0)
        message = jnp.where(at_row == own * rows + i, jnp.sum(line, 1, keepdims=True), message)
    out_ref[...] = message.astype(NARROW)


def merged(head, own, rows, parts_ref, out_ref):
    wouts = parts_ref.shape[0]
    parts = parts_ref[...].astype(WIDE)
    shape = parts.shape
    diagonal = lax.broadcasted_iota(jnp.int32, shape, 1) == lax.broadcasted_iota(jnp.int32, shape, 2)

    def column(i):
        line = parts[:, own * rows + i : own * rows + i + 1, :] + parts[:, own * rows + i + 1 : own * rows + i + 2, :]
        return jnp.sum(jnp.where(diagonal, line, 0.0), -1, keepdims=True)

    tops, totals = column(0), column(2)
    factors = jnp.exp(tops - jnp.max(tops, 0, keepdims=True))
    total = jnp.sum(factors * totals, 0)
    attended = jnp.sum(factors * parts, 0) / total
    for h in range(own):
        piece = attended[h * rows : (h + 1) * rows, :].astype(NARROW)
        for peer in range(out_ref.shape[0]):
            out_ref[peer, :, h * head : (h + 1) * head] = piece


def limit(mib):
    return pltpu.CompilerParams(vmem_limit_bytes=mib * 2**20)


def body(inputs, w_query, w_keyval, w_out, key_cache, value_cache, lengths, positions):
    rows, slots, head = key_cache.shape
    qcols = w_query.shape[1]
    own = qcols // head
    chips = lax.axis_size(CHIP)
    wouts = lax.axis_size(WOUT)
    core = lax.axis_index("core")
    scale = head ** (-0.5)

    half = head // 2
    freq = 10000.0 ** (-(2.0 * jnp.arange(half, dtype=WIDE)) / head)
    place = jnp.pad(positions, (0, TALL - rows)).astype(WIDE)
    angle = place[:, None] * freq
    cosine = jnp.cos(angle)
    sine = jnp.sin(angle)

    split = ZLO_FIRST * SIZES[1] * 2 * rows
    rolled = jnp.concatenate([inputs[split:], inputs[:split]], 0)
    core_at = core.reshape(1).astype(jnp.int32)
    shape = (chips, rows, qcols + w_keyval.shape[1])

    def terms(own_rows, dtype, name):
        return pl.pallas_call(
            functools.partial(projected, rows, own_rows),
            out_shape=jax.ShapeDtypeStruct(shape, dtype),
            in_specs=[SMEM, VMEM, VMEM, pl.BlockSpec(memory_space=pl.ANY)],
            out_specs=VMEM,
            scratch_shapes=[pltpu.VMEM(w_keyval.shape[::-1], NARROW), pltpu.SemaphoreType.DMA],
            compiler_params=limit(8),
            cost_estimate=pl.CostEstimate(flops=120_000_000, bytes_accessed=1_000_000, transcendentals=0),
            name=name,
        )(core_at, rolled.T, w_query, w_keyval.T)

    theirs = terms(False, NARROW, "theirs")
    ours = terms(True, WIDE, "ours")
    theirs, w_turned = lax.optimization_barrier((theirs, w_out.T))
    theirs = lax.ppermute(theirs, "core", CORES)
    w_other = lax.ppermute(w_turned, "core", CORES)
    partial = (ours + theirs.astype(WIDE)).astype(NARROW)
    at = lax.axis_index(WOUT).reshape(1).astype(jnp.int32)
    partial, w_other, at, cosine, sine = lax.optimization_barrier((partial, w_other, at, cosine, sine))
    pieces = exchange(partial, CHIP, CHIP_GROUP)
    message = pl.pallas_call(
        functools.partial(own_queries, head, own, rows),
        out_shape=jax.ShapeDtypeStruct((wouts, TALL, head), NARROW),
        in_specs=[VMEM] * 3,
        out_specs=VMEM,
        scratch_shapes=[pltpu.VMEM((TALL, head), WIDE)],
        compiler_params=limit(4),
        name="own_queries",
    )(pieces, cosine, sine)
    got = exchange(message, WOUT, [WOUT_ORDER])
    message = pl.pallas_call(
        functools.partial(partial_attention, head, own, rows, slots, scale),
        out_shape=jax.ShapeDtypeStruct((wouts, TALL, head), NARROW),
        in_specs=[SMEM, SMEM] + [VMEM] * 5,
        out_specs=VMEM,
        scratch_shapes=[pltpu.VMEM((wouts * TALL, TALL), WIDE), pltpu.VMEM((TALL, head), NARROW)],
        compiler_params=limit(8),
        name="partial_attention",
    )(lengths, at, got, cosine, sine, key_cache, value_cache)
    parts = exchange(message, WOUT, [WOUT_ORDER])
    attended = pl.pallas_call(
        functools.partial(merged, head, own, rows),
        out_shape=jax.ShapeDtypeStruct((chips, rows, qcols), NARROW),
        in_specs=[VMEM],
        out_specs=VMEM,
        compiler_params=limit(4),
        name="merged",
    )(parts)

    whole = exchange(attended, CHIP, CHIP_GROUP)
    mixed = pl.pallas_call(
        mixed_parts,
        out_shape=jax.ShapeDtypeStruct((2, wouts, 2 * rows, w_out.shape[1]), NARROW),
        in_specs=[SMEM] + [VMEM] * 3,
        out_specs=VMEM,
        compiler_params=limit(8),
        name="mixed_parts",
    )(core_at, whole, w_turned, w_other)
    mixed = exchange(mixed.reshape((2 * wouts,) + mixed.shape[2:]), ("core",) + WOUT, CORE_WOUT_GROUP)
    return pl.pallas_call(
        functools.partial(own_rows, rows),
        out_shape=jax.ShapeDtypeStruct((4 * rows, mixed.shape[2]), NARROW),
        in_specs=[VMEM],
        out_specs=VMEM,
        compiler_params=limit(8),
        name="own_rows",
    )(mixed)


def solution(mesh):
    parted = Mesh(mesh.devices.reshape(SIZES), AXES)
    placed = (
        P(None, WIN),
        P(WIN, WOUT),
        P(WIN, WOUT),
        P(WOUT, WIN),
        P(WIN, WOUT, None),
        P(WIN, WOUT, None),
        P(WIN),
        P(WIN),
    )
    return jax.shard_map(
        body, mesh=parted, in_specs=placed, out_specs=P(WOUT, WIN), check_vma=False
    )
```

```python
import functools

import jax
import jax.numpy as jnp
from jax import lax
from jax.experimental import pallas as pl
from jax.experimental.pallas import tpu as pltpu
from jax.sharding import Mesh
from jax.sharding import PartitionSpec as P

WIDE = jnp.float32
NARROW = jnp.bfloat16
AXES = ("zlo", "y", "core", "x", "zh")
SIZES = (4, 8, 2, 4, 4)
WIN = ("zlo", "y", "core")
CHIP = ("zlo", "y")
WOUT = ("x", "zh")
NONE = -1e30
TALL = 16
SELF_INDEX = 9
CORES = [(0, 1), (1, 0)]
VMEM = pl.BlockSpec(memory_space=pltpu.VMEM)
SMEM = pl.BlockSpec(memory_space=pltpu.SMEM)


def ring(a, b, size):
    return min((a - b) % size, (b - a) % size)


def far_first(first, members, hops):
    rest = [m for m in members if m != first]
    return [first] + sorted(rest, key=lambda m: -hops(m))


CHIP_ORDER = far_first(
    2 * SIZES[1],
    range(SIZES[0] * SIZES[1]),
    lambda m: abs(m // SIZES[1] - 2) + ring(m % SIZES[1], 0, SIZES[1]),
)
WOUT_ORDER = far_first(
    SIZES[4] - 1,
    range(SIZES[3] * SIZES[4]),
    lambda m: ring(m // SIZES[4], 0, SIZES[3]) + 4 * ring(m % SIZES[4], SIZES[4] - 1, SIZES[4]),
)
CHIP_GROUP = [CHIP_ORDER]
CORE_WOUT_GROUP = [[core * len(WOUT_ORDER) + o for o in WOUT_ORDER for core in range(2)]]


def exchange(pieces, axis, group):
    return lax.all_to_all(pieces, axis, 0, 0, axis_index_groups=group, tiled=True)


def turn(first, second, cosine, sine):
    return first * cosine - second * sine, first * sine + second * cosine


def projected(rows, core_ref, x_ref, q_ref, kv_ref, ours_ref, theirs_ref):
    first = core_ref[0] == 0
    cols = q_ref.shape[1]
    step = 256
    for start in range(0, cols + 1, step):
        if start < cols:
            terms = lax.dot_general(
                x_ref[...], q_ref[:, start : start + step], (((0,), (0,)), ((), ())), preferred_element_type=WIDE
            )
        else:
            terms = lax.dot_general(
                x_ref[...], kv_ref[...], (((0,), (1,)), ((), ())), preferred_element_type=WIDE
            )
        terms = terms.reshape(-1, 2 * rows, terms.shape[1])
        low, high = terms[:, :rows], terms[:, rows:]
        ours = jnp.where(first, low, high)
        theirs = jnp.where(first, high, low).astype(NARROW)
        for k, chip in enumerate(CHIP_ORDER):
            at = (chip + len(CHIP_ORDER) // 2) % len(CHIP_ORDER)
            ours_ref[k, :, start : start + terms.shape[2]] = ours[at]
            theirs_ref[k, :, start : start + terms.shape[2]] = theirs[at]


def mixed_parts(core_ref, rows_ref, own_ref, other_ref, out_ref):
    core = core_ref[0]
    whole = rows_ref[...]
    rows = jnp.stack([whole[CHIP_ORDER.index(chip)] for chip in range(len(CHIP_ORDER))])
    rows = rows.reshape(-1, whole.shape[2])
    for at, w_ref in ((core, own_ref), (1 - core, other_ref)):
        part = lax.dot_general(rows, w_ref[...], (((1,), (1,)), ((), ())), preferred_element_type=WIDE)
        part = part.reshape(out_ref.shape[:1] + out_ref.shape[2:]).astype(NARROW)
        for o, place in enumerate(WOUT_ORDER):
            out_ref[o, at] = part[place]


def own_rows(rows, parts_ref, out_ref):
    parts = parts_ref[...].astype(WIDE)
    parts = parts.reshape((parts.shape[0] // 2, 2) + parts.shape[1:])
    sums = [jnp.sum(parts[:, c], 0) for c in range(2)]
    pieces = [sums[c][chip * rows : (chip + 1) * rows] for chip in range(2) for c in range(2)]
    out_ref[...] = jnp.concatenate(pieces, 0).astype(NARROW)


def own_queries(head, own, rows, pieces_ref, cos_ref, sin_ref, out_ref, scr):
    half = head // 2
    total = jnp.sum(pieces_ref[...].astype(WIDE), 0).astype(NARROW).astype(WIDE)
    cosine, sine = cos_ref[:rows, :], sin_ref[:rows, :]
    scr[...] = jnp.zeros_like(scr)
    for h in range(own):
        start = h * head
        first, second = turn(total[:, start : start + half], total[:, start + half : start + head], cosine, sine)
        scr[h * rows : (h + 1) * rows, :half] = first
        scr[h * rows : (h + 1) * rows, half:] = second
    fresh = total[:, own * head :]
    scr[own * rows : (own + 1) * rows, : fresh.shape[1]] = fresh
    out_ref[...] = jnp.broadcast_to(scr[...].astype(NARROW)[None], out_ref.shape)


def partial_attention(head, own, rows, slots, scale, len_ref, at_ref, got_ref, cos_ref, sin_ref, keys_ref, values_ref, out_ref, self_scr, value_scr):
    half = head // 2
    wouts = got_ref.shape[0]
    width = 2 * head // wouts
    count = wouts * TALL
    here = at_ref[0]
    q = got_ref[...].reshape(count, head)

    iota = functools.partial(lax.broadcasted_iota, jnp.int32)

    def against(keys):
        return lax.dot_general(q, keys, (((1,), (1,)), ((), ())), preferred_element_type=WIDE)

    own_slot = (count, TALL)
    self_valid = jnp.logical_and(iota(own_slot, 0) % rows == iota(own_slot, 1), here == SELF_INDEX)
    self_scr[...] = jnp.full(own_slot, NONE, WIDE)
    value_scr[...] = jnp.zeros_like(value_scr)

    @pl.when(here == SELF_INDEX)
    def _():
        wide = (count, wouts * width)
        copies = iota((head, wouts * width), 1) % width == iota((head, wouts * width), 0)
        fresh = jnp.dot(q, copies.astype(WIDE).astype(NARROW), preferred_element_type=WIDE)
        block = iota((count, 1), 0) // TALL
        piece = jnp.zeros_like(block)
        for k, o in enumerate(WOUT_ORDER):
            piece = jnp.where(block == k, o, piece)
        fresh = jnp.where(iota(wide, 1) // width == piece, fresh, 0.0).astype(NARROW)
        pick = iota((TALL, count), 1) % TALL == iota((TALL, count), 0) + own * rows
        fresh = jnp.dot(pick.astype(WIDE).astype(NARROW), fresh, preferred_element_type=WIDE)
        first, second = turn(fresh[:, :half], fresh[:, half:head], cos_ref[...], sin_ref[...])
        newkey = jnp.concatenate([first, second], 1).astype(NARROW)
        self_scr[...] = jnp.where(self_valid, against(newkey) * scale, NONE)
        value_scr[...] = fresh[:, head:].astype(NARROW)

    row = iota((count, slots), 0) % rows
    length = jnp.zeros((count, slots), jnp.int32)
    scores = jnp.zeros((count, slots), WIDE)
    for r in range(rows):
        length = jnp.where(row == r, len_ref[r], length)
        scores = jnp.where(row == r, against(keys_ref[r]), scores)
    valid = here * slots + iota((count, slots), 1) < length
    scores = jnp.where(valid, scores * scale, NONE)
    self_score = self_scr[...]

    top = jnp.maximum(jnp.max(scores, -1, keepdims=True), jnp.max(self_score, -1, keepdims=True))
    top_hi = top.astype(NARROW).astype(WIDE)
    top_lo = (top - top_hi).astype(NARROW).astype(WIDE)
    top = top_hi + top_lo
    weights = jnp.where(valid, jnp.exp(scores - top), 0.0)
    self_weight = jnp.where(self_valid, jnp.exp(self_score - top), 0.0)
    total = jnp.sum(weights, -1, keepdims=True) + jnp.sum(self_weight, -1, keepdims=True)
    total_hi = total.astype(NARROW).astype(WIDE)
    acc = jnp.dot(self_weight.astype(NARROW), value_scr[...], preferred_element_type=WIDE)
    for r in range(rows):
        w = jnp.where(row == r, weights, 0.0).astype(NARROW)
        acc = acc + jnp.dot(w, values_ref[r], preferred_element_type=WIDE)

    shape = (wouts, TALL, head)
    at_row, at_lane = iota(shape, 1), iota(shape, 2)
    message = acc.reshape(shape)
    for i, stat in enumerate((top_hi, top_lo, total_hi, total - total_hi)):
        line = jnp.where(at_row == at_lane, stat.reshape(wouts, TALL, 1), 0.0)
        message = jnp.where(at_row == own * rows + i, jnp.sum(line, 1, keepdims=True), message)
    out_ref[...] = message.astype(NARROW)


def merged(head, own, rows, parts_ref, out_ref):
    wouts = parts_ref.shape[0]
    parts = parts_ref[...].astype(WIDE)
    shape = parts.shape
    diagonal = lax.broadcasted_iota(jnp.int32, shape, 1) == lax.broadcasted_iota(jnp.int32, shape, 2)

    def column(i):
        line = parts[:, own * rows + i : own * rows + i + 1, :] + parts[:, own * rows + i + 1 : own * rows + i + 2, :]
        return jnp.sum(jnp.where(diagonal, line, 0.0), -1, keepdims=True)

    tops, totals = column(0), column(2)
    factors = jnp.exp(tops - jnp.max(tops, 0, keepdims=True))
    total = jnp.sum(factors * totals, 0)
    attended = jnp.sum(factors * parts, 0) / total
    for h in range(own):
        piece = attended[h * rows : (h + 1) * rows, :].astype(NARROW)
        for peer in range(out_ref.shape[0]):
            out_ref[peer, :, h * head : (h + 1) * head] = piece


def limit(mib):
    return pltpu.CompilerParams(vmem_limit_bytes=mib * 2**20)


def body(inputs, w_query, w_keyval, w_out, key_cache, value_cache, lengths, positions):
    rows, slots, head = key_cache.shape
    qcols = w_query.shape[1]
    own = qcols // head
    chips = lax.axis_size(CHIP)
    wouts = lax.axis_size(WOUT)
    core = lax.axis_index("core")
    scale = head ** (-0.5)

    half = head // 2
    freq = 10000.0 ** (-(2.0 * jnp.arange(half, dtype=WIDE)) / head)
    place = jnp.pad(positions, (0, TALL - rows)).astype(WIDE)
    angle = place[:, None] * freq
    cosine = jnp.cos(angle)
    sine = jnp.sin(angle)

    split = inputs.shape[0] // 2
    rolled = jnp.concatenate([inputs[split:], inputs[:split]], 0)
    core_at = core.reshape(1).astype(jnp.int32)
    shape = (chips, rows, qcols + w_keyval.shape[1])
    ours, theirs = pl.pallas_call(
        functools.partial(projected, rows),
        out_shape=(jax.ShapeDtypeStruct(shape, WIDE), jax.ShapeDtypeStruct(shape, NARROW)),
        in_specs=[SMEM] + [VMEM] * 3,
        out_specs=(VMEM, VMEM),
        compiler_params=limit(8),
        name="projected",
    )(core_at, rolled.T, w_query, w_keyval.T)
    theirs = lax.ppermute(theirs, "core", CORES)
    partial = (ours + theirs.astype(WIDE)).astype(NARROW)

    at = lax.axis_index(WOUT).reshape(1).astype(jnp.int32)
    partial, w_turned, at = lax.optimization_barrier((partial, w_out.T, at))
    w_other = lax.ppermute(w_turned, "core", CORES)
    pieces = exchange(partial, CHIP, CHIP_GROUP)
    message = pl.pallas_call(
        functools.partial(own_queries, head, own, rows),
        out_shape=jax.ShapeDtypeStruct((wouts, TALL, head), NARROW),
        in_specs=[VMEM] * 3,
        out_specs=VMEM,
        scratch_shapes=[pltpu.VMEM((TALL, head), WIDE)],
        compiler_params=limit(4),
        name="own_queries",
    )(pieces, cosine, sine)
    message, w_other = lax.optimization_barrier((message, w_other))
    got = exchange(message, WOUT, [WOUT_ORDER])
    message = pl.pallas_call(
        functools.partial(partial_attention, head, own, rows, slots, scale),
        out_shape=jax.ShapeDtypeStruct((wouts, TALL, head), NARROW),
        in_specs=[SMEM, SMEM] + [VMEM] * 5,
        out_specs=VMEM,
        scratch_shapes=[pltpu.VMEM((wouts * TALL, TALL), WIDE), pltpu.VMEM((TALL, head), NARROW)],
        compiler_params=limit(8),
        name="partial_attention",
    )(lengths, at, got, cosine, sine, key_cache, value_cache)
    parts = exchange(message, WOUT, [WOUT_ORDER])
    attended = pl.pallas_call(
        functools.partial(merged, head, own, rows),
        out_shape=jax.ShapeDtypeStruct((chips, rows, qcols), NARROW),
        in_specs=[VMEM],
        out_specs=VMEM,
        compiler_params=limit(4),
        name="merged",
    )(parts)

    whole = exchange(attended, CHIP, CHIP_GROUP)
    mixed = pl.pallas_call(
        mixed_parts,
        out_shape=jax.ShapeDtypeStruct((wouts, 2, 2 * rows, w_out.shape[1]), NARROW),
        in_specs=[SMEM] + [VMEM] * 3,
        out_specs=VMEM,
        compiler_params=limit(8),
        name="mixed_parts",
    )(core_at, whole, w_turned, w_other)
    mixed = exchange(mixed.reshape((2 * wouts,) + mixed.shape[2:]), ("core",) + WOUT, CORE_WOUT_GROUP)
    return pl.pallas_call(
        functools.partial(own_rows, rows),
        out_shape=jax.ShapeDtypeStruct((4 * rows, mixed.shape[2]), NARROW),
        in_specs=[VMEM],
        out_specs=VMEM,
        compiler_params=limit(8),
        name="own_rows",
    )(mixed)


def solution(mesh):
    parted = Mesh(mesh.devices.reshape(SIZES), AXES)
    placed = (
        P(None, WIN),
        P(WIN, WOUT),
        P(WIN, WOUT),
        P(WOUT, WIN),
        P(WIN, WOUT, None),
        P(WIN, WOUT, None),
        P(WIN),
        P(WIN),
    )
    return jax.shard_map(
        body, mesh=parted, in_specs=placed, out_specs=P(WOUT, WIN), check_vma=False
    )
```

```python
import functools

import jax
import jax.numpy as jnp
from jax import lax
from jax.experimental import pallas as pl
from jax.experimental.pallas import tpu as pltpu
from jax.sharding import Mesh
from jax.sharding import PartitionSpec as P

WIDE = jnp.float32
NARROW = jnp.bfloat16
AXES = ("zlo", "y", "core", "x", "zh")
SIZES = (4, 8, 2, 4, 4)
WIN = ("zlo", "y", "core")
CHIP = ("zlo", "y")
WOUT = ("x", "zh")
NONE = -1e30
TALL = 16
SELF_INDEX = 9
CORES = [(0, 1), (1, 0)]
VMEM = pl.BlockSpec(memory_space=pltpu.VMEM)
SMEM = pl.BlockSpec(memory_space=pltpu.SMEM)


def ring(a, b, size):
    return min((a - b) % size, (b - a) % size)


def far_first(first, members, hops):
    rest = [m for m in members if m != first]
    return [first] + sorted(rest, key=lambda m: -hops(m))


CHIP_ORDER = far_first(
    2 * SIZES[1],
    range(SIZES[0] * SIZES[1]),
    lambda m: abs(m // SIZES[1] - 2) + ring(m % SIZES[1], 0, SIZES[1]),
)
WOUT_ORDER = [x * SIZES[4] + zh for x in range(SIZES[3]) for zh in (3, 0, 1, 2)]
CHIP_GROUP = [CHIP_ORDER]
CORE_WOUT_GROUP = [[core * len(WOUT_ORDER) + o for core in range(2) for o in WOUT_ORDER]]


def exchange(pieces, axis, group):
    return lax.all_to_all(pieces, axis, 0, 0, axis_index_groups=group, tiled=True)


def turn(first, second, cosine, sine):
    return first * cosine - second * sine, first * sine + second * cosine


def projected(rows, core_ref, x_ref, q_ref, kv_ref, ours_ref, theirs_ref):
    first = core_ref[0] == 0
    cols = q_ref.shape[1]
    step = 256
    for start in range(0, cols + 1, step):
        if start < cols:
            terms = lax.dot_general(
                x_ref[...], q_ref[:, start : start + step], (((0,), (0,)), ((), ())), preferred_element_type=WIDE
            )
        else:
            terms = lax.dot_general(
                x_ref[...], kv_ref[...], (((0,), (1,)), ((), ())), preferred_element_type=WIDE
            )
        terms = terms.reshape(-1, 2 * rows, terms.shape[1])
        low, high = terms[:, :rows], terms[:, rows:]
        ours = jnp.where(first, low, high)
        theirs = jnp.where(first, high, low).astype(NARROW)
        for k, chip in enumerate(CHIP_ORDER):
            at = (chip + len(CHIP_ORDER) // 2) % len(CHIP_ORDER)
            ours_ref[k, :, start : start + terms.shape[2]] = ours[at]
            theirs_ref[k, :, start : start + terms.shape[2]] = theirs[at]


def mixed_parts(core_ref, rows_ref, own_ref, other_ref, out_ref):
    core = core_ref[0]
    whole = rows_ref[...]
    rows = jnp.stack([whole[CHIP_ORDER.index(chip)] for chip in range(len(CHIP_ORDER))])
    rows = rows.reshape(-1, whole.shape[2])
    for at, w_ref in ((core, own_ref), (1 - core, other_ref)):
        part = lax.dot_general(rows, w_ref[...], (((1,), (1,)), ((), ())), preferred_element_type=WIDE)
        part = part.reshape(out_ref.shape[1:]).astype(NARROW)
        for o, place in enumerate(WOUT_ORDER):
            out_ref[at, o] = part[place]


def own_rows(rows, parts_ref, out_ref):
    half = parts_ref.shape[0] // 2
    sums = [jnp.sum(parts_ref[c * half : (c + 1) * half].astype(WIDE), 0) for c in range(2)]
    pieces = [sums[c][chip * rows : (chip + 1) * rows] for chip in range(2) for c in range(2)]
    out_ref[...] = jnp.concatenate(pieces, 0).astype(NARROW)


def own_queries(head, own, rows, pieces_ref, cos_ref, sin_ref, out_ref, scr):
    half = head // 2
    total = jnp.sum(pieces_ref[...].astype(WIDE), 0).astype(NARROW).astype(WIDE)
    cosine, sine = cos_ref[:rows, :], sin_ref[:rows, :]
    scr[...] = jnp.zeros_like(scr)
    for h in range(own):
        start = h * head
        first, second = turn(total[:, start : start + half], total[:, start + half : start + head], cosine, sine)
        scr[h * rows : (h + 1) * rows, :half] = first
        scr[h * rows : (h + 1) * rows, half:] = second
    fresh = total[:, own * head :]
    scr[own * rows : (own + 1) * rows, : fresh.shape[1]] = fresh
    out_ref[...] = jnp.broadcast_to(scr[...].astype(NARROW)[None], out_ref.shape)


def partial_attention(head, own, rows, slots, scale, len_ref, at_ref, got_ref, cos_ref, sin_ref, keys_ref, values_ref, out_ref, self_scr, value_scr):
    half = head // 2
    wouts = got_ref.shape[0]
    width = 2 * head // wouts
    count = wouts * TALL
    here = at_ref[0]
    q = got_ref[...].reshape(count, head)

    iota = functools.partial(lax.broadcasted_iota, jnp.int32)

    def against(keys):
        return lax.dot_general(q, keys, (((1,), (1,)), ((), ())), preferred_element_type=WIDE)

    own_slot = (count, TALL)
    self_valid = jnp.logical_and(iota(own_slot, 0) % rows == iota(own_slot, 1), here == SELF_INDEX)
    self_scr[...] = jnp.full(own_slot, NONE, WIDE)
    value_scr[...] = jnp.zeros_like(value_scr)

    @pl.when(here == SELF_INDEX)
    def _():
        wide = (count, wouts * width)
        copies = iota((head, wouts * width), 1) % width == iota((head, wouts * width), 0)
        fresh = jnp.dot(q, copies.astype(WIDE).astype(NARROW), preferred_element_type=WIDE)
        block = iota((count, 1), 0) // TALL
        piece = jnp.zeros_like(block)
        for k, o in enumerate(WOUT_ORDER):
            piece = jnp.where(block == k, o, piece)
        fresh = jnp.where(iota(wide, 1) // width == piece, fresh, 0.0).astype(NARROW)
        pick = iota((TALL, count), 1) % TALL == iota((TALL, count), 0) + own * rows
        fresh = jnp.dot(pick.astype(WIDE).astype(NARROW), fresh, preferred_element_type=WIDE)
        first, second = turn(fresh[:, :half], fresh[:, half:head], cos_ref[...], sin_ref[...])
        newkey = jnp.concatenate([first, second], 1).astype(NARROW)
        self_scr[...] = jnp.where(self_valid, against(newkey) * scale, NONE)
        value_scr[...] = fresh[:, head:].astype(NARROW)

    row = iota((count, slots), 0) % rows
    length = jnp.zeros((count, slots), jnp.int32)
    scores = jnp.zeros((count, slots), WIDE)
    for r in range(rows):
        length = jnp.where(row == r, len_ref[r], length)
        scores = jnp.where(row == r, against(keys_ref[r]), scores)
    valid = here * slots + iota((count, slots), 1) < length
    scores = jnp.where(valid, scores * scale, NONE)
    self_score = self_scr[...]

    top = jnp.maximum(jnp.max(scores, -1, keepdims=True), jnp.max(self_score, -1, keepdims=True))
    top_hi = top.astype(NARROW).astype(WIDE)
    top_lo = (top - top_hi).astype(NARROW).astype(WIDE)
    top = top_hi + top_lo
    weights = jnp.where(valid, jnp.exp(scores - top), 0.0)
    self_weight = jnp.where(self_valid, jnp.exp(self_score - top), 0.0)
    total = jnp.sum(weights, -1, keepdims=True) + jnp.sum(self_weight, -1, keepdims=True)
    total_hi = total.astype(NARROW).astype(WIDE)
    acc = jnp.dot(self_weight.astype(NARROW), value_scr[...], preferred_element_type=WIDE)
    for r in range(rows):
        w = jnp.where(row == r, weights, 0.0).astype(NARROW)
        acc = acc + jnp.dot(w, values_ref[r], preferred_element_type=WIDE)

    shape = (wouts, TALL, head)
    at_row, at_lane = iota(shape, 1), iota(shape, 2)
    message = acc.reshape(shape)
    for i, stat in enumerate((top_hi, top_lo, total_hi, total - total_hi)):
        line = jnp.where(at_row == at_lane, stat.reshape(wouts, TALL, 1), 0.0)
        message = jnp.where(at_row == own * rows + i, jnp.sum(line, 1, keepdims=True), message)
    out_ref[...] = message.astype(NARROW)


def merged(head, own, rows, parts_ref, out_ref):
    wouts = parts_ref.shape[0]
    parts = parts_ref[...].astype(WIDE)
    shape = parts.shape
    diagonal = lax.broadcasted_iota(jnp.int32, shape, 1) == lax.broadcasted_iota(jnp.int32, shape, 2)

    def column(i):
        line = parts[:, own * rows + i : own * rows + i + 1, :] + parts[:, own * rows + i + 1 : own * rows + i + 2, :]
        return jnp.sum(jnp.where(diagonal, line, 0.0), -1, keepdims=True)

    tops, totals = column(0), column(2)
    factors = jnp.exp(tops - jnp.max(tops, 0, keepdims=True))
    total = jnp.sum(factors * totals, 0)
    attended = jnp.sum(factors * parts, 0) / total
    for h in range(own):
        piece = attended[h * rows : (h + 1) * rows, :].astype(NARROW)
        for peer in range(out_ref.shape[0]):
            out_ref[peer, :, h * head : (h + 1) * head] = piece


def limit(mib):
    return pltpu.CompilerParams(vmem_limit_bytes=mib * 2**20)


def body(inputs, w_query, w_keyval, w_out, key_cache, value_cache, lengths, positions):
    rows, slots, head = key_cache.shape
    qcols = w_query.shape[1]
    own = qcols // head
    chips = lax.axis_size(CHIP)
    wouts = lax.axis_size(WOUT)
    core = lax.axis_index("core")
    scale = head ** (-0.5)

    half = head // 2
    freq = 10000.0 ** (-(2.0 * jnp.arange(half, dtype=WIDE)) / head)
    place = jnp.pad(positions, (0, TALL - rows)).astype(WIDE)
    angle = place[:, None] * freq
    cosine = jnp.cos(angle)
    sine = jnp.sin(angle)

    split = inputs.shape[0] // 2
    rolled = jnp.concatenate([inputs[split:], inputs[:split]], 0)
    core_at = core.reshape(1).astype(jnp.int32)
    shape = (chips, rows, qcols + w_keyval.shape[1])
    ours, theirs = pl.pallas_call(
        functools.partial(projected, rows),
        out_shape=(jax.ShapeDtypeStruct(shape, WIDE), jax.ShapeDtypeStruct(shape, NARROW)),
        in_specs=[SMEM] + [VMEM] * 3,
        out_specs=(VMEM, VMEM),
        compiler_params=limit(8),
        name="projected",
    )(core_at, rolled.T, w_query, w_keyval.T)
    theirs = lax.ppermute(theirs, "core", CORES)
    partial = (ours + theirs.astype(WIDE)).astype(NARROW)

    at = lax.axis_index(WOUT).reshape(1).astype(jnp.int32)
    partial, w_turned, at = lax.optimization_barrier((partial, w_out.T, at))
    w_other = lax.ppermute(w_turned, "core", CORES)
    pieces = exchange(partial, CHIP, CHIP_GROUP)
    message = pl.pallas_call(
        functools.partial(own_queries, head, own, rows),
        out_shape=jax.ShapeDtypeStruct((wouts, TALL, head), NARROW),
        in_specs=[VMEM] * 3,
        out_specs=VMEM,
        scratch_shapes=[pltpu.VMEM((TALL, head), WIDE)],
        compiler_params=limit(4),
        name="own_queries",
    )(pieces, cosine, sine)
    message, w_other = lax.optimization_barrier((message, w_other))
    got = exchange(message, WOUT, [WOUT_ORDER])
    message = pl.pallas_call(
        functools.partial(partial_attention, head, own, rows, slots, scale),
        out_shape=jax.ShapeDtypeStruct((wouts, TALL, head), NARROW),
        in_specs=[SMEM, SMEM] + [VMEM] * 5,
        out_specs=VMEM,
        scratch_shapes=[pltpu.VMEM((wouts * TALL, TALL), WIDE), pltpu.VMEM((TALL, head), NARROW)],
        compiler_params=limit(8),
        name="partial_attention",
    )(lengths, at, got, cosine, sine, key_cache, value_cache)
    parts = exchange(message, WOUT, [WOUT_ORDER])
    attended = pl.pallas_call(
        functools.partial(merged, head, own, rows),
        out_shape=jax.ShapeDtypeStruct((chips, rows, qcols), NARROW),
        in_specs=[VMEM],
        out_specs=VMEM,
        compiler_params=limit(4),
        name="merged",
    )(parts)

    whole = exchange(attended, CHIP, CHIP_GROUP)
    mixed = pl.pallas_call(
        mixed_parts,
        out_shape=jax.ShapeDtypeStruct((2, wouts, 2 * rows, w_out.shape[1]), NARROW),
        in_specs=[SMEM] + [VMEM] * 3,
        out_specs=VMEM,
        compiler_params=limit(8),
        name="mixed_parts",
    )(core_at, whole, w_turned, w_other)
    mixed = exchange(mixed.reshape((2 * wouts,) + mixed.shape[2:]), ("core",) + WOUT, CORE_WOUT_GROUP)
    return pl.pallas_call(
        functools.partial(own_rows, rows),
        out_shape=jax.ShapeDtypeStruct((4 * rows, mixed.shape[2]), NARROW),
        in_specs=[VMEM],
        out_specs=VMEM,
        compiler_params=limit(8),
        name="own_rows",
    )(mixed)


def solution(mesh):
    parted = Mesh(mesh.devices.reshape(SIZES), AXES)
    placed = (
        P(None, WIN),
        P(WIN, WOUT),
        P(WIN, WOUT),
        P(WOUT, WIN),
        P(WIN, WOUT, None),
        P(WIN, WOUT, None),
        P(WIN),
        P(WIN),
    )
    return jax.shard_map(
        body, mesh=parted, in_specs=placed, out_specs=P(WOUT, WIN), check_vma=False
    )
```

```python
import functools

import jax
import jax.numpy as jnp
from jax import lax
from jax.experimental import pallas as pl
from jax.experimental.pallas import tpu as pltpu
from jax.sharding import Mesh
from jax.sharding import PartitionSpec as P

WIDE = jnp.float32
NARROW = jnp.bfloat16
AXES = ("zlo", "y", "core", "x", "zh")
SIZES = (4, 8, 2, 4, 4)
WIN = ("zlo", "y", "core")
CHIP = ("zlo", "y")
WOUT = ("x", "zh")
NONE = -1e30
TALL = 16
SELF_INDEX = 9
CORES = [(0, 1), (1, 0)]
VMEM = pl.BlockSpec(memory_space=pltpu.VMEM)
SMEM = pl.BlockSpec(memory_space=pltpu.SMEM)


ZLO_FIRST = 2
ZH_ORDER = (3, 0, 1, 2)
CHIP_GROUP = [[(ZLO_FIRST + z) % SIZES[0] * SIZES[1] + y for z in range(SIZES[0]) for y in range(SIZES[1])]]
WOUT_ORDER = [x * SIZES[4] + zh for zh in ZH_ORDER for x in range(SIZES[3])]
CORE_WOUT_GROUP = [[core * len(WOUT_ORDER) + o for core in range(2) for o in WOUT_ORDER]]


def exchange(pieces, axis, group):
    return lax.all_to_all(pieces, axis, 0, 0, axis_index_groups=group, tiled=True)


def turn(first, second, cosine, sine):
    return first * cosine - second * sine, first * sine + second * cosine


def projected(rows, core_ref, x_ref, q_ref, kv_ref, ours_ref, theirs_ref):
    first = core_ref[0] == 0
    cols = q_ref.shape[1]
    step = 256
    for start in range(0, cols + 1, step):
        if start < cols:
            terms = lax.dot_general(
                x_ref[...], q_ref[:, start : start + step], (((0,), (0,)), ((), ())), preferred_element_type=WIDE
            )
        else:
            terms = lax.dot_general(
                x_ref[...], kv_ref[...], (((0,), (1,)), ((), ())), preferred_element_type=WIDE
            )
        terms = terms.reshape(-1, 2 * rows, terms.shape[1])
        low, high = terms[:, :rows], terms[:, rows:]
        ours_ref[:, :, start : start + terms.shape[2]] = jnp.where(first, low, high)
        theirs_ref[:, :, start : start + terms.shape[2]] = jnp.where(first, high, low).astype(NARROW)


def mixed_parts(core_ref, rows_ref, own_ref, other_ref, out_ref):
    core = core_ref[0]
    split = rows_ref.shape[0] - ZLO_FIRST * SIZES[1]
    rows = jnp.concatenate([rows_ref[split:], rows_ref[:split]], 0).reshape(-1, rows_ref.shape[2])
    for at, w_ref in ((core, own_ref), (1 - core, other_ref)):
        part = lax.dot_general(rows, w_ref[...], (((1,), (1,)), ((), ())), preferred_element_type=WIDE)
        part = part.reshape(out_ref.shape[1:]).astype(NARROW)
        for o, place in enumerate(WOUT_ORDER):
            out_ref[at, o] = part[place]


def own_rows(rows, parts_ref, out_ref):
    half = parts_ref.shape[0] // 2
    sums = [jnp.sum(parts_ref[c * half : (c + 1) * half].astype(WIDE), 0) for c in range(2)]
    pieces = [sums[c][chip * rows : (chip + 1) * rows] for chip in range(2) for c in range(2)]
    out_ref[...] = jnp.concatenate(pieces, 0).astype(NARROW)


def own_queries(head, own, rows, pieces_ref, cos_ref, sin_ref, out_ref, scr):
    half = head // 2
    total = jnp.sum(pieces_ref[...].astype(WIDE), 0).astype(NARROW).astype(WIDE)
    cosine, sine = cos_ref[:rows, :], sin_ref[:rows, :]
    scr[...] = jnp.zeros_like(scr)
    for h in range(own):
        start = h * head
        first, second = turn(total[:, start : start + half], total[:, start + half : start + head], cosine, sine)
        scr[h * rows : (h + 1) * rows, :half] = first
        scr[h * rows : (h + 1) * rows, half:] = second
    fresh = total[:, own * head :]
    scr[own * rows : (own + 1) * rows, : fresh.shape[1]] = fresh
    out_ref[...] = jnp.broadcast_to(scr[...].astype(NARROW)[None], out_ref.shape)


def partial_attention(head, own, rows, slots, scale, len_ref, at_ref, got_ref, cos_ref, sin_ref, keys_ref, values_ref, out_ref, self_scr, value_scr):
    half = head // 2
    wouts = got_ref.shape[0]
    width = 2 * head // wouts
    count = wouts * TALL
    here = at_ref[0]
    q = got_ref[...].reshape(count, head)

    iota = functools.partial(lax.broadcasted_iota, jnp.int32)

    def against(keys):
        return lax.dot_general(q, keys, (((1,), (1,)), ((), ())), preferred_element_type=WIDE)

    own_slot = (count, TALL)
    self_valid = jnp.logical_and(iota(own_slot, 0) % rows == iota(own_slot, 1), here == SELF_INDEX)
    self_scr[...] = jnp.full(own_slot, NONE, WIDE)
    value_scr[...] = jnp.zeros_like(value_scr)

    @pl.when(here == SELF_INDEX)
    def _():
        wide = (count, wouts * width)
        copies = iota((head, wouts * width), 1) % width == iota((head, wouts * width), 0)
        fresh = jnp.dot(q, copies.astype(WIDE).astype(NARROW), preferred_element_type=WIDE)
        piece = iota(wide, 0) // TALL
        piece = piece % SIZES[3] * SIZES[4] + (piece // SIZES[3] + ZH_ORDER[0]) % SIZES[4]
        fresh = jnp.where(iota(wide, 1) // width == piece, fresh, 0.0).astype(NARROW)
        pick = iota((TALL, count), 1) % TALL == iota((TALL, count), 0) + own * rows
        fresh = jnp.dot(pick.astype(WIDE).astype(NARROW), fresh, preferred_element_type=WIDE)
        first, second = turn(fresh[:, :half], fresh[:, half:head], cos_ref[...], sin_ref[...])
        newkey = jnp.concatenate([first, second], 1).astype(NARROW)
        self_scr[...] = jnp.where(self_valid, against(newkey) * scale, NONE)
        value_scr[...] = fresh[:, head:].astype(NARROW)

    row = iota((count, slots), 0) % rows
    length = jnp.zeros((count, slots), jnp.int32)
    scores = jnp.zeros((count, slots), WIDE)
    for r in range(rows):
        length = jnp.where(row == r, len_ref[r], length)
        scores = jnp.where(row == r, against(keys_ref[r]), scores)
    valid = here * slots + iota((count, slots), 1) < length
    scores = jnp.where(valid, scores * scale, NONE)
    self_score = self_scr[...]

    top = jnp.maximum(jnp.max(scores, -1, keepdims=True), jnp.max(self_score, -1, keepdims=True))
    top_hi = top.astype(NARROW).astype(WIDE)
    top_lo = (top - top_hi).astype(NARROW).astype(WIDE)
    top = top_hi + top_lo
    weights = jnp.where(valid, jnp.exp(scores - top), 0.0)
    self_weight = jnp.where(self_valid, jnp.exp(self_score - top), 0.0)
    total = jnp.sum(weights, -1, keepdims=True) + jnp.sum(self_weight, -1, keepdims=True)
    total_hi = total.astype(NARROW).astype(WIDE)
    acc = jnp.dot(self_weight.astype(NARROW), value_scr[...], preferred_element_type=WIDE)
    for r in range(rows):
        w = jnp.where(row == r, weights, 0.0).astype(NARROW)
        acc = acc + jnp.dot(w, values_ref[r], preferred_element_type=WIDE)

    shape = (wouts, TALL, head)
    at_row, at_lane = iota(shape, 1), iota(shape, 2)
    message = acc.reshape(shape)
    for i, stat in enumerate((top_hi, top_lo, total_hi, total - total_hi)):
        line = jnp.where(at_row == at_lane, stat.reshape(wouts, TALL, 1), 0.0)
        message = jnp.where(at_row == own * rows + i, jnp.sum(line, 1, keepdims=True), message)
    out_ref[...] = message.astype(NARROW)


def merged(head, own, rows, parts_ref, out_ref):
    wouts = parts_ref.shape[0]
    parts = parts_ref[...].astype(WIDE)
    shape = parts.shape
    diagonal = lax.broadcasted_iota(jnp.int32, shape, 1) == lax.broadcasted_iota(jnp.int32, shape, 2)

    def column(i):
        line = parts[:, own * rows + i : own * rows + i + 1, :] + parts[:, own * rows + i + 1 : own * rows + i + 2, :]
        return jnp.sum(jnp.where(diagonal, line, 0.0), -1, keepdims=True)

    tops, totals = column(0), column(2)
    factors = jnp.exp(tops - jnp.max(tops, 0, keepdims=True))
    total = jnp.sum(factors * totals, 0)
    attended = jnp.sum(factors * parts, 0) / total
    for h in range(own):
        piece = attended[h * rows : (h + 1) * rows, :].astype(NARROW)
        for peer in range(out_ref.shape[0]):
            out_ref[peer, :, h * head : (h + 1) * head] = piece


def limit(mib):
    return pltpu.CompilerParams(vmem_limit_bytes=mib * 2**20)


def body(inputs, w_query, w_keyval, w_out, key_cache, value_cache, lengths, positions):
    rows, slots, head = key_cache.shape
    qcols = w_query.shape[1]
    own = qcols // head
    chips = lax.axis_size(CHIP)
    wouts = lax.axis_size(WOUT)
    core = lax.axis_index("core")
    scale = head ** (-0.5)

    half = head // 2
    freq = 10000.0 ** (-(2.0 * jnp.arange(half, dtype=WIDE)) / head)
    place = jnp.pad(positions, (0, TALL - rows)).astype(WIDE)
    angle = place[:, None] * freq
    cosine = jnp.cos(angle)
    sine = jnp.sin(angle)

    split = ZLO_FIRST * SIZES[1] * 2 * rows
    rolled = jnp.concatenate([inputs[split:], inputs[:split]], 0)
    core_at = core.reshape(1).astype(jnp.int32)
    shape = (chips, rows, qcols + w_keyval.shape[1])
    ours, theirs = pl.pallas_call(
        functools.partial(projected, rows),
        out_shape=(jax.ShapeDtypeStruct(shape, WIDE), jax.ShapeDtypeStruct(shape, NARROW)),
        in_specs=[SMEM] + [VMEM] * 3,
        out_specs=(VMEM, VMEM),
        compiler_params=limit(8),
        name="projected",
    )(core_at, rolled.T, w_query, w_keyval.T)
    theirs = lax.ppermute(theirs, "core", CORES)
    partial = (ours + theirs.astype(WIDE)).astype(NARROW)

    at = lax.axis_index(WOUT).reshape(1).astype(jnp.int32)
    partial, w_turned, at = lax.optimization_barrier((partial, w_out.T, at))
    w_other = lax.ppermute(w_turned, "core", CORES)
    pieces = exchange(partial, CHIP, CHIP_GROUP)
    message = pl.pallas_call(
        functools.partial(own_queries, head, own, rows),
        out_shape=jax.ShapeDtypeStruct((wouts, TALL, head), NARROW),
        in_specs=[VMEM] * 3,
        out_specs=VMEM,
        scratch_shapes=[pltpu.VMEM((TALL, head), WIDE)],
        compiler_params=limit(4),
        name="own_queries",
    )(pieces, cosine, sine)
    message, w_other = lax.optimization_barrier((message, w_other))
    got = exchange(message, WOUT, [WOUT_ORDER])
    message = pl.pallas_call(
        functools.partial(partial_attention, head, own, rows, slots, scale),
        out_shape=jax.ShapeDtypeStruct((wouts, TALL, head), NARROW),
        in_specs=[SMEM, SMEM] + [VMEM] * 5,
        out_specs=VMEM,
        scratch_shapes=[pltpu.VMEM((wouts * TALL, TALL), WIDE), pltpu.VMEM((TALL, head), NARROW)],
        compiler_params=limit(8),
        name="partial_attention",
    )(lengths, at, got, cosine, sine, key_cache, value_cache)
    parts = exchange(message, WOUT, [WOUT_ORDER])
    attended = pl.pallas_call(
        functools.partial(merged, head, own, rows),
        out_shape=jax.ShapeDtypeStruct((chips, rows, qcols), NARROW),
        in_specs=[VMEM],
        out_specs=VMEM,
        compiler_params=limit(4),
        name="merged",
    )(parts)

    whole = exchange(attended, CHIP, CHIP_GROUP)
    mixed = pl.pallas_call(
        mixed_parts,
        out_shape=jax.ShapeDtypeStruct((2, wouts, 2 * rows, w_out.shape[1]), NARROW),
        in_specs=[SMEM] + [VMEM] * 3,
        out_specs=VMEM,
        compiler_params=limit(8),
        name="mixed_parts",
    )(core_at, whole, w_turned, w_other)
    mixed = exchange(mixed.reshape((2 * wouts,) + mixed.shape[2:]), ("core",) + WOUT, CORE_WOUT_GROUP)
    return pl.pallas_call(
        functools.partial(own_rows, rows),
        out_shape=jax.ShapeDtypeStruct((4 * rows, mixed.shape[2]), NARROW),
        in_specs=[VMEM],
        out_specs=VMEM,
        compiler_params=limit(8),
        name="own_rows",
    )(mixed)


def solution(mesh):
    parted = Mesh(mesh.devices.reshape(SIZES), AXES)
    placed = (
        P(None, WIN),
        P(WIN, WOUT),
        P(WIN, WOUT),
        P(WOUT, WIN),
        P(WIN, WOUT, None),
        P(WIN, WOUT, None),
        P(WIN),
        P(WIN),
    )
    return jax.shard_map(
        body, mesh=parted, in_specs=placed, out_specs=P(WOUT, WIN), check_vma=False
    )
```

```python
import functools

import jax
import jax.numpy as jnp
from jax import lax
from jax.experimental import pallas as pl
from jax.experimental.pallas import tpu as pltpu
from jax.sharding import Mesh
from jax.sharding import PartitionSpec as P

WIDE = jnp.float32
NARROW = jnp.bfloat16
AXES = ("zlo", "y", "core", "x", "zh")
SIZES = (4, 8, 2, 4, 4)
WIN = ("zlo", "y", "core")
CHIP = ("zlo", "y")
WOUT = ("x", "zh")
NONE = -1e30
TALL = 16
SELF_INDEX = 9
CORES = [(0, 1), (1, 0)]
VMEM = pl.BlockSpec(memory_space=pltpu.VMEM)
SMEM = pl.BlockSpec(memory_space=pltpu.SMEM)


ZLO_FIRST = 2
ZH_ORDER = (3, 0, 1, 2)
CHIP_GROUP = [[(ZLO_FIRST + z) % SIZES[0] * SIZES[1] + y for z in range(SIZES[0]) for y in range(SIZES[1])]]
WOUT_ORDER = [x * SIZES[4] + zh for x in range(SIZES[3]) for zh in ZH_ORDER]
CORE_WOUT_GROUP = [[core * len(WOUT_ORDER) + o for core in range(2) for o in WOUT_ORDER]]


def exchange(pieces, axis, group):
    return lax.all_to_all(pieces, axis, 0, 0, axis_index_groups=group, tiled=True)


def turn(first, second, cosine, sine):
    return first * cosine - second * sine, first * sine + second * cosine


def projected(rows, count, core_ref, both_ref, q_ref, ours_ref, theirs_ref):
    first = core_ref[0] == 0
    depth, cols = q_ref.shape
    x, kv = both_ref[:depth, :count], both_ref[depth:, :depth]
    step = 256
    for start in range(0, cols + 1, step):
        if start < cols:
            terms = lax.dot_general(
                x, q_ref[:, start : start + step], (((0,), (0,)), ((), ())), preferred_element_type=WIDE
            )
        else:
            terms = lax.dot_general(
                x, kv, (((0,), (1,)), ((), ())), preferred_element_type=WIDE
            )
        terms = terms.reshape(-1, 2 * rows, terms.shape[1])
        split = ZLO_FIRST * SIZES[1]
        terms = jnp.concatenate([terms[split:], terms[:split]], 0)
        low, high = terms[:, :rows], terms[:, rows:]
        ours_ref[:, :, start : start + terms.shape[2]] = jnp.where(first, low, high)
        theirs_ref[:, :, start : start + terms.shape[2]] = jnp.where(first, high, low).astype(NARROW)


def mixed_parts(core_ref, rows_ref, own_ref, other_ref, out_ref):
    core = core_ref[0]
    split = rows_ref.shape[0] - ZLO_FIRST * SIZES[1]
    rows = jnp.concatenate([rows_ref[split:], rows_ref[:split]], 0).reshape(-1, rows_ref.shape[2])
    for at, w_ref in ((core, own_ref), (1 - core, other_ref)):
        part = lax.dot_general(rows, w_ref[...], (((1,), (1,)), ((), ())), preferred_element_type=WIDE)
        part = part.reshape(out_ref.shape[1:]).astype(NARROW)
        for o, place in enumerate(WOUT_ORDER):
            out_ref[at, o] = part[place]


def own_rows(rows, parts_ref, out_ref):
    half = parts_ref.shape[0] // 2
    sums = [jnp.sum(parts_ref[c * half : (c + 1) * half].astype(WIDE), 0) for c in range(2)]
    pieces = [sums[c][chip * rows : (chip + 1) * rows] for chip in range(2) for c in range(2)]
    out_ref[...] = jnp.concatenate(pieces, 0).astype(NARROW)


def own_queries(head, own, rows, pieces_ref, cos_ref, sin_ref, out_ref, scr):
    half = head // 2
    total = jnp.sum(pieces_ref[...].astype(WIDE), 0).astype(NARROW).astype(WIDE)
    cosine, sine = cos_ref[:rows, :], sin_ref[:rows, :]
    scr[...] = jnp.zeros_like(scr)
    for h in range(own):
        start = h * head
        first, second = turn(total[:, start : start + half], total[:, start + half : start + head], cosine, sine)
        scr[h * rows : (h + 1) * rows, :half] = first
        scr[h * rows : (h + 1) * rows, half:] = second
    fresh = total[:, own * head :]
    scr[own * rows : (own + 1) * rows, : fresh.shape[1]] = fresh
    out_ref[...] = jnp.broadcast_to(scr[...].astype(NARROW)[None], out_ref.shape)


def partial_attention(head, own, rows, slots, scale, len_ref, at_ref, got_ref, cos_ref, sin_ref, keys_ref, values_ref, out_ref, self_scr, value_scr):
    half = head // 2
    wouts = got_ref.shape[0]
    width = 2 * head // wouts
    count = wouts * TALL
    here = at_ref[0]
    q = got_ref[...].reshape(count, head)

    iota = functools.partial(lax.broadcasted_iota, jnp.int32)

    def against(keys):
        return lax.dot_general(q, keys, (((1,), (1,)), ((), ())), preferred_element_type=WIDE)

    own_slot = (count, TALL)
    self_valid = jnp.logical_and(iota(own_slot, 0) % rows == iota(own_slot, 1), here == SELF_INDEX)
    self_scr[...] = jnp.full(own_slot, NONE, WIDE)
    value_scr[...] = jnp.zeros_like(value_scr)

    @pl.when(here == SELF_INDEX)
    def _():
        wide = (count, wouts * width)
        copies = iota((head, wouts * width), 1) % width == iota((head, wouts * width), 0)
        fresh = jnp.dot(q, copies.astype(WIDE).astype(NARROW), preferred_element_type=WIDE)
        piece = iota(wide, 0) // TALL
        piece = piece // SIZES[4] * SIZES[4] + (piece + ZH_ORDER[0]) % SIZES[4]
        fresh = jnp.where(iota(wide, 1) // width == piece, fresh, 0.0).astype(NARROW)
        pick = iota((TALL, count), 1) % TALL == iota((TALL, count), 0) + own * rows
        fresh = jnp.dot(pick.astype(WIDE).astype(NARROW), fresh, preferred_element_type=WIDE)
        first, second = turn(fresh[:, :half], fresh[:, half:head], cos_ref[...], sin_ref[...])
        newkey = jnp.concatenate([first, second], 1).astype(NARROW)
        self_scr[...] = jnp.where(self_valid, against(newkey) * scale, NONE)
        value_scr[...] = fresh[:, head:].astype(NARROW)

    row = iota((count, slots), 0) % rows
    length = jnp.zeros((count, slots), jnp.int32)
    scores = jnp.zeros((count, slots), WIDE)
    for r in range(rows):
        length = jnp.where(row == r, len_ref[r], length)
        scores = jnp.where(row == r, against(keys_ref[r]), scores)
    valid = here * slots + iota((count, slots), 1) < length
    scores = jnp.where(valid, scores * scale, NONE)
    self_score = self_scr[...]

    top = jnp.maximum(jnp.max(scores, -1, keepdims=True), jnp.max(self_score, -1, keepdims=True))
    top_hi = top.astype(NARROW).astype(WIDE)
    top_lo = (top - top_hi).astype(NARROW).astype(WIDE)
    top = top_hi + top_lo
    weights = jnp.where(valid, jnp.exp(scores - top), 0.0)
    self_weight = jnp.where(self_valid, jnp.exp(self_score - top), 0.0)
    total = jnp.sum(weights, -1, keepdims=True) + jnp.sum(self_weight, -1, keepdims=True)
    total_hi = total.astype(NARROW).astype(WIDE)
    acc = jnp.dot(self_weight.astype(NARROW), value_scr[...], preferred_element_type=WIDE)
    for r in range(rows):
        w = jnp.where(row == r, weights, 0.0).astype(NARROW)
        acc = acc + jnp.dot(w, values_ref[r], preferred_element_type=WIDE)

    shape = (wouts, TALL, head)
    at_row, at_lane = iota(shape, 1), iota(shape, 2)
    message = acc.reshape(shape)
    for i, stat in enumerate((top_hi, top_lo, total_hi, total - total_hi)):
        line = jnp.where(at_row == at_lane, stat.reshape(wouts, TALL, 1), 0.0)
        message = jnp.where(at_row == own * rows + i, jnp.sum(line, 1, keepdims=True), message)
    out_ref[...] = message.astype(NARROW)


def merged(head, own, rows, parts_ref, out_ref):
    wouts = parts_ref.shape[0]
    parts = parts_ref[...].astype(WIDE)
    shape = parts.shape
    diagonal = lax.broadcasted_iota(jnp.int32, shape, 1) == lax.broadcasted_iota(jnp.int32, shape, 2)

    def column(i):
        line = parts[:, own * rows + i : own * rows + i + 1, :] + parts[:, own * rows + i + 1 : own * rows + i + 2, :]
        return jnp.sum(jnp.where(diagonal, line, 0.0), -1, keepdims=True)

    tops, totals = column(0), column(2)
    factors = jnp.exp(tops - jnp.max(tops, 0, keepdims=True))
    total = jnp.sum(factors * totals, 0)
    attended = jnp.sum(factors * parts, 0) / total
    for h in range(own):
        piece = attended[h * rows : (h + 1) * rows, :].astype(NARROW)
        for peer in range(out_ref.shape[0]):
            out_ref[peer, :, h * head : (h + 1) * head] = piece


def limit(mib):
    return pltpu.CompilerParams(vmem_limit_bytes=mib * 2**20)


def body(inputs, w_query, w_keyval, w_out, key_cache, value_cache, lengths, positions):
    rows, slots, head = key_cache.shape
    qcols = w_query.shape[1]
    own = qcols // head
    chips = lax.axis_size(CHIP)
    wouts = lax.axis_size(WOUT)
    core = lax.axis_index("core")
    scale = head ** (-0.5)

    half = head // 2
    freq = 10000.0 ** (-(2.0 * jnp.arange(half, dtype=WIDE)) / head)
    place = jnp.pad(positions, (0, TALL - rows)).astype(WIDE)
    angle = place[:, None] * freq
    cosine = jnp.cos(angle)
    sine = jnp.sin(angle)

    count, depth = inputs.shape
    lanes = max(count, depth)
    both = [jnp.pad(part, ((0, 0), (0, lanes - part.shape[1]))) for part in (inputs.T, w_keyval.T)]
    both = jnp.concatenate(both, 0)
    core_at = core.reshape(1).astype(jnp.int32)
    shape = (chips, rows, qcols + w_keyval.shape[1])
    ours, theirs = pl.pallas_call(
        functools.partial(projected, rows, count),
        out_shape=(jax.ShapeDtypeStruct(shape, WIDE), jax.ShapeDtypeStruct(shape, NARROW)),
        in_specs=[SMEM] + [VMEM] * 2,
        out_specs=(VMEM, VMEM),
        compiler_params=limit(8),
        name="projected",
    )(core_at, both, w_query)
    theirs = lax.ppermute(theirs, "core", CORES)
    partial = (ours + theirs.astype(WIDE)).astype(NARROW)

    at = lax.axis_index(WOUT).reshape(1).astype(jnp.int32)
    partial, w_turned, at = lax.optimization_barrier((partial, w_out.T, at))
    w_other = lax.ppermute(w_turned, "core", CORES)
    pieces = exchange(partial, CHIP, CHIP_GROUP)
    message = pl.pallas_call(
        functools.partial(own_queries, head, own, rows),
        out_shape=jax.ShapeDtypeStruct((wouts, TALL, head), NARROW),
        in_specs=[VMEM] * 3,
        out_specs=VMEM,
        scratch_shapes=[pltpu.VMEM((TALL, head), WIDE)],
        compiler_params=limit(4),
        name="own_queries",
    )(pieces, cosine, sine)
    message, w_other = lax.optimization_barrier((message, w_other))
    got = exchange(message, WOUT, [WOUT_ORDER])
    message = pl.pallas_call(
        functools.partial(partial_attention, head, own, rows, slots, scale),
        out_shape=jax.ShapeDtypeStruct((wouts, TALL, head), NARROW),
        in_specs=[SMEM, SMEM] + [VMEM] * 5,
        out_specs=VMEM,
        scratch_shapes=[pltpu.VMEM((wouts * TALL, TALL), WIDE), pltpu.VMEM((TALL, head), NARROW)],
        compiler_params=limit(8),
        name="partial_attention",
    )(lengths, at, got, cosine, sine, key_cache, value_cache)
    parts = exchange(message, WOUT, [WOUT_ORDER])
    attended = pl.pallas_call(
        functools.partial(merged, head, own, rows),
        out_shape=jax.ShapeDtypeStruct((chips, rows, qcols), NARROW),
        in_specs=[VMEM],
        out_specs=VMEM,
        compiler_params=limit(4),
        name="merged",
    )(parts)

    whole = exchange(attended, CHIP, CHIP_GROUP)
    mixed = pl.pallas_call(
        mixed_parts,
        out_shape=jax.ShapeDtypeStruct((2, wouts, 2 * rows, w_out.shape[1]), NARROW),
        in_specs=[SMEM] + [VMEM] * 3,
        out_specs=VMEM,
        compiler_params=limit(8),
        name="mixed_parts",
    )(core_at, whole, w_turned, w_other)
    mixed = exchange(mixed.reshape((2 * wouts,) + mixed.shape[2:]), ("core",) + WOUT, CORE_WOUT_GROUP)
    return pl.pallas_call(
        functools.partial(own_rows, rows),
        out_shape=jax.ShapeDtypeStruct((4 * rows, mixed.shape[2]), NARROW),
        in_specs=[VMEM],
        out_specs=VMEM,
        compiler_params=limit(8),
        name="own_rows",
    )(mixed)


def solution(mesh):
    parted = Mesh(mesh.devices.reshape(SIZES), AXES)
    placed = (
        P(None, WIN),
        P(WIN, WOUT),
        P(WIN, WOUT),
        P(WOUT, WIN),
        P(WIN, WOUT, None),
        P(WIN, WOUT, None),
        P(WIN),
        P(WIN),
    )
    return jax.shard_map(
        body, mesh=parted, in_specs=placed, out_specs=P(WOUT, WIN), check_vma=False
    )
```

```python
import functools

import jax
import jax.numpy as jnp
from jax import lax
from jax.experimental import pallas as pl
from jax.experimental.pallas import tpu as pltpu
from jax.sharding import Mesh
from jax.sharding import PartitionSpec as P

WIDE = jnp.float32
NARROW = jnp.bfloat16
AXES = ("zlo", "y", "core", "x", "zh")
SIZES = (4, 8, 2, 4, 4)
WIN = ("zlo", "y", "core")
CHIP = ("zlo", "y")
WOUT = ("x", "zh")
NONE = -1e30
TALL = 16
SELF_INDEX = 9
CORES = [(0, 1), (1, 0)]
VMEM = pl.BlockSpec(memory_space=pltpu.VMEM)
SMEM = pl.BlockSpec(memory_space=pltpu.SMEM)


ZLO_FIRST = 2
ZH_ORDER = (3, 0, 1, 2)
CHIP_GROUP = [[(ZLO_FIRST + z) % SIZES[0] * SIZES[1] + y for z in range(SIZES[0]) for y in range(SIZES[1])]]
WOUT_ORDER = [x * SIZES[4] + zh for x in range(SIZES[3]) for zh in ZH_ORDER]
CORE_WOUT_GROUP = [[core * len(WOUT_ORDER) + o for core in range(2) for o in WOUT_ORDER]]


def exchange(pieces, axis, group):
    return lax.all_to_all(pieces, axis, 0, 0, axis_index_groups=group, tiled=True)


def turn(first, second, cosine, sine):
    return first * cosine - second * sine, first * sine + second * cosine


def projected(rows, core_ref, x_ref, q_ref, kv_ref, ours_ref, theirs_ref):
    first = core_ref[0] == 0
    cols = q_ref.shape[1]
    step = 256
    for start in range(0, cols + 1, step):
        if start < cols:
            terms = lax.dot_general(
                x_ref[...], q_ref[:, start : start + step], (((0,), (0,)), ((), ())), preferred_element_type=WIDE
            )
        else:
            terms = lax.dot_general(
                x_ref[...], kv_ref[...], (((0,), (1,)), ((), ())), preferred_element_type=WIDE
            )
        terms = terms.reshape(-1, 2 * rows, terms.shape[1])
        low, high = terms[:, :rows], terms[:, rows:]
        ours_ref[:, :, start : start + terms.shape[2]] = jnp.where(first, low, high)
        theirs_ref[:, :, start : start + terms.shape[2]] = jnp.where(first, high, low).astype(NARROW)


def mixed_parts(core_ref, rows_ref, own_ref, other_ref, out_ref):
    core = core_ref[0]
    split = rows_ref.shape[0] - ZLO_FIRST * SIZES[1]
    rows = jnp.concatenate([rows_ref[split:], rows_ref[:split]], 0).reshape(-1, rows_ref.shape[2])
    for at, w_ref in ((core, own_ref), (1 - core, other_ref)):
        part = lax.dot_general(rows, w_ref[...], (((1,), (1,)), ((), ())), preferred_element_type=WIDE)
        part = part.reshape(out_ref.shape[1:]).astype(NARROW)
        for o, place in enumerate(WOUT_ORDER):
            out_ref[at, o] = part[place]


def own_rows(rows, parts_ref, out_ref):
    half = parts_ref.shape[0] // 2
    sums = [jnp.sum(parts_ref[c * half : (c + 1) * half].astype(WIDE), 0) for c in range(2)]
    pieces = [sums[c][chip * rows : (chip + 1) * rows] for chip in range(2) for c in range(2)]
    out_ref[...] = jnp.concatenate(pieces, 0).astype(NARROW)


def own_queries(head, own, rows, pieces_ref, cos_ref, sin_ref, out_ref, scr):
    half = head // 2
    total = jnp.sum(pieces_ref[...].astype(WIDE), 0).astype(NARROW).astype(WIDE)
    cosine, sine = cos_ref[:rows, :], sin_ref[:rows, :]
    scr[...] = jnp.zeros_like(scr)
    for h in range(own):
        start = h * head
        first, second = turn(total[:, start : start + half], total[:, start + half : start + head], cosine, sine)
        scr[h * rows : (h + 1) * rows, :half] = first
        scr[h * rows : (h + 1) * rows, half:] = second
    fresh = total[:, own * head :]
    scr[own * rows : (own + 1) * rows, : fresh.shape[1]] = fresh
    out_ref[...] = jnp.broadcast_to(scr[...].astype(NARROW)[None], out_ref.shape)


def partial_attention(head, own, rows, slots, scale, len_ref, at_ref, got_ref, cos_ref, sin_ref, keys_ref, values_ref, out_ref, key_scr, value_scr, q_scr, stat_scr):
    half = head // 2
    wouts = got_ref.shape[0]
    width = 2 * head // wouts
    count = wouts * TALL
    here = at_ref[0]
    q = got_ref[...].reshape(count, head)

    iota = functools.partial(lax.broadcasted_iota, jnp.int32)

    key_scr[...] = jnp.zeros_like(key_scr)
    value_scr[...] = jnp.zeros_like(value_scr)

    @pl.when(here == SELF_INDEX)
    def _():
        wide = (count, wouts * width)
        copies = iota((head, wouts * width), 1) % width == iota((head, wouts * width), 0)
        fresh = jnp.dot(q, copies.astype(WIDE).astype(NARROW), preferred_element_type=WIDE)
        piece = iota(wide, 0) // TALL
        piece = piece // SIZES[4] * SIZES[4] + (piece + ZH_ORDER[0]) % SIZES[4]
        fresh = jnp.where(iota(wide, 1) // width == piece, fresh, 0.0).astype(NARROW)
        pick = iota((TALL, count), 1) % TALL == iota((TALL, count), 0) + own * rows
        fresh = jnp.dot(pick.astype(WIDE).astype(NARROW), fresh, preferred_element_type=WIDE)
        first, second = turn(fresh[:, :half], fresh[:, half:head], cos_ref[...], sin_ref[...])
        key_scr[...] = jnp.concatenate([first, second], 1).astype(NARROW).astype(WIDE)
        value_scr[...] = fresh[:, head:]

    lanes = 128
    per_row = count // rows
    for half_at in range(2):
        q_scr[half_at] = q[:, half_at * lanes : (half_at + 1) * lanes].astype(WIDE)
    slot = here * slots + iota((per_row, slots), 1)
    part = iota((per_row, lanes), 1) // (lanes // 4)
    for r in range(rows):
        mine = pl.ds(r, per_row, rows)
        q_row = jnp.concatenate([q_scr[0, mine, :], q_scr[1, mine, :]], 1)
        valid = slot < len_ref[r]
        scores = lax.dot_general(
            q_row.astype(NARROW), keys_ref[r], (((1,), (1,)), ((), ())), preferred_element_type=WIDE
        )
        scores = jnp.where(valid, scores * scale, NONE)
        self_score = jnp.sum(q_row * key_scr[r : r + 1, :], -1, keepdims=True) * scale
        self_score = jnp.where(here == SELF_INDEX, self_score, NONE)
        top = jnp.maximum(jnp.max(scores, -1, keepdims=True), self_score)
        top_hi = top.astype(NARROW).astype(WIDE)
        top_lo = (top - top_hi).astype(NARROW).astype(WIDE)
        top = top_hi + top_lo
        weights = jnp.where(valid, jnp.exp(scores - top), 0.0)
        self_weight = jnp.where(here == SELF_INDEX, jnp.exp(self_score - top), 0.0)
        total = jnp.sum(weights, -1, keepdims=True) + self_weight
        total_hi = total.astype(NARROW).astype(WIDE)
        acc = jnp.dot(weights.astype(NARROW), values_ref[r], preferred_element_type=WIDE)
        acc = acc + self_weight * value_scr[r : r + 1, :]
        q_scr[0, mine, :] = acc[:, :lanes]
        q_scr[1, mine, :] = acc[:, lanes:]
        stat_scr[mine, :] = jnp.where(
            part == 0, top_hi, jnp.where(part == 1, top_lo, jnp.where(part == 2, total_hi, total - total_hi))
        )

    shape = (wouts, TALL, lanes)
    at_row, at_lane = iota(shape, 1), iota(shape, 2)
    stats = stat_scr[...].reshape(shape)
    message = q_scr[0].reshape(shape)
    for i in range(4):
        column = stats[:, :, i * (lanes // 4) : i * (lanes // 4) + 1]
        line = jnp.sum(jnp.where(at_row == at_lane, column, 0.0), 1, keepdims=True)
        message = jnp.where(at_row == own * rows + i, line, message)
    out_ref[:, :, :lanes] = message.astype(NARROW)
    out_ref[:, :, lanes:] = q_scr[1].reshape(shape).astype(NARROW)


def merged(head, own, rows, parts_ref, out_ref):
    wouts = parts_ref.shape[0]
    parts = parts_ref[...].astype(WIDE)
    shape = parts.shape
    diagonal = lax.broadcasted_iota(jnp.int32, shape, 1) == lax.broadcasted_iota(jnp.int32, shape, 2)

    def column(i):
        line = parts[:, own * rows + i : own * rows + i + 1, :] + parts[:, own * rows + i + 1 : own * rows + i + 2, :]
        return jnp.sum(jnp.where(diagonal, line, 0.0), -1, keepdims=True)

    tops, totals = column(0), column(2)
    factors = jnp.exp(tops - jnp.max(tops, 0, keepdims=True))
    total = jnp.sum(factors * totals, 0)
    attended = jnp.sum(factors * parts, 0) / total
    for h in range(own):
        piece = attended[h * rows : (h + 1) * rows, :].astype(NARROW)
        for peer in range(out_ref.shape[0]):
            out_ref[peer, :, h * head : (h + 1) * head] = piece


def limit(mib):
    return pltpu.CompilerParams(vmem_limit_bytes=mib * 2**20)


def body(inputs, w_query, w_keyval, w_out, key_cache, value_cache, lengths, positions):
    rows, slots, head = key_cache.shape
    qcols = w_query.shape[1]
    own = qcols // head
    chips = lax.axis_size(CHIP)
    wouts = lax.axis_size(WOUT)
    core = lax.axis_index("core")
    scale = head ** (-0.5)

    half = head // 2
    freq = 10000.0 ** (-(2.0 * jnp.arange(half, dtype=WIDE)) / head)
    place = jnp.pad(positions, (0, TALL - rows)).astype(WIDE)
    angle = place[:, None] * freq
    cosine = jnp.cos(angle)
    sine = jnp.sin(angle)

    split = ZLO_FIRST * SIZES[1] * 2 * rows
    rolled = jnp.concatenate([inputs[split:], inputs[:split]], 0)
    core_at = core.reshape(1).astype(jnp.int32)
    shape = (chips, rows, qcols + w_keyval.shape[1])
    ours, theirs = pl.pallas_call(
        functools.partial(projected, rows),
        out_shape=(jax.ShapeDtypeStruct(shape, WIDE), jax.ShapeDtypeStruct(shape, NARROW)),
        in_specs=[SMEM] + [VMEM] * 3,
        out_specs=(VMEM, VMEM),
        compiler_params=limit(8),
        name="projected",
    )(core_at, rolled.T, w_query, w_keyval.T)
    theirs = lax.ppermute(theirs, "core", CORES)
    partial = (ours + theirs.astype(WIDE)).astype(NARROW)

    at = lax.axis_index(WOUT).reshape(1).astype(jnp.int32)
    partial, w_turned, at = lax.optimization_barrier((partial, w_out.T, at))
    w_other = lax.ppermute(w_turned, "core", CORES)
    pieces = exchange(partial, CHIP, CHIP_GROUP)
    message = pl.pallas_call(
        functools.partial(own_queries, head, own, rows),
        out_shape=jax.ShapeDtypeStruct((wouts, TALL, head), NARROW),
        in_specs=[VMEM] * 3,
        out_specs=VMEM,
        scratch_shapes=[pltpu.VMEM((TALL, head), WIDE)],
        compiler_params=limit(4),
        name="own_queries",
    )(pieces, cosine, sine)
    message, w_other = lax.optimization_barrier((message, w_other))
    got = exchange(message, WOUT, [WOUT_ORDER])
    message = pl.pallas_call(
        functools.partial(partial_attention, head, own, rows, slots, scale),
        out_shape=jax.ShapeDtypeStruct((wouts, TALL, head), NARROW),
        in_specs=[SMEM, SMEM] + [VMEM] * 5,
        out_specs=VMEM,
        scratch_shapes=[
            pltpu.VMEM((TALL, head), WIDE),
            pltpu.VMEM((TALL, head), WIDE),
            pltpu.VMEM((2, wouts * TALL, head // 2), WIDE),
            pltpu.VMEM((wouts * TALL, 128), WIDE),
        ],
        compiler_params=limit(8),
        name="partial_attention",
    )(lengths, at, got, cosine, sine, key_cache, value_cache)
    parts = exchange(message, WOUT, [WOUT_ORDER])
    attended = pl.pallas_call(
        functools.partial(merged, head, own, rows),
        out_shape=jax.ShapeDtypeStruct((chips, rows, qcols), NARROW),
        in_specs=[VMEM],
        out_specs=VMEM,
        compiler_params=limit(4),
        name="merged",
    )(parts)

    whole = exchange(attended, CHIP, CHIP_GROUP)
    mixed = pl.pallas_call(
        mixed_parts,
        out_shape=jax.ShapeDtypeStruct((2, wouts, 2 * rows, w_out.shape[1]), NARROW),
        in_specs=[SMEM] + [VMEM] * 3,
        out_specs=VMEM,
        compiler_params=limit(8),
        name="mixed_parts",
    )(core_at, whole, w_turned, w_other)
    mixed = exchange(mixed.reshape((2 * wouts,) + mixed.shape[2:]), ("core",) + WOUT, CORE_WOUT_GROUP)
    return pl.pallas_call(
        functools.partial(own_rows, rows),
        out_shape=jax.ShapeDtypeStruct((4 * rows, mixed.shape[2]), NARROW),
        in_specs=[VMEM],
        out_specs=VMEM,
        compiler_params=limit(8),
        name="own_rows",
    )(mixed)


def solution(mesh):
    parted = Mesh(mesh.devices.reshape(SIZES), AXES)
    placed = (
        P(None, WIN),
        P(WIN, WOUT),
        P(WIN, WOUT),
        P(WOUT, WIN),
        P(WIN, WOUT, None),
        P(WIN, WOUT, None),
        P(WIN),
        P(WIN),
    )
    return jax.shard_map(
        body, mesh=parted, in_specs=placed, out_specs=P(WOUT, WIN), check_vma=False
    )
```

```python
import functools

import jax
import jax.numpy as jnp
from jax import lax
from jax.experimental import pallas as pl
from jax.experimental.pallas import tpu as pltpu
from jax.sharding import Mesh
from jax.sharding import PartitionSpec as P

WIDE = jnp.float32
NARROW = jnp.bfloat16
AXES = ("zlo", "y", "core", "x", "zh")
SIZES = (4, 8, 2, 4, 4)
WIN = ("zlo", "y", "core")
CHIP = ("zlo", "y")
WOUT = ("x", "zh")
NONE = -1e30
TALL = 16
SELF_INDEX = 9
CORES = [(0, 1), (1, 0)]
VMEM = pl.BlockSpec(memory_space=pltpu.VMEM)
SMEM = pl.BlockSpec(memory_space=pltpu.SMEM)


ZLO_FIRST = 2
ZH_ORDER = (3, 0, 1, 2)
CHIP_GROUP = [[(ZLO_FIRST + z) % SIZES[0] * SIZES[1] + y for z in range(SIZES[0]) for y in range(SIZES[1])]]
WOUT_ORDER = [x * SIZES[4] + zh for x in range(SIZES[3]) for zh in ZH_ORDER]
CORE_WOUT_GROUP = [[core * len(WOUT_ORDER) + o for core in range(2) for o in WOUT_ORDER]]


def exchange(pieces, axis, group):
    return lax.all_to_all(pieces, axis, 0, 0, axis_index_groups=group, tiled=True)


def turn(first, second, cosine, sine):
    return first * cosine - second * sine, first * sine + second * cosine


def projected(rows, core_ref, x_ref, q_ref, kv_ref, ours_ref, theirs_ref):
    first = core_ref[0] == 0
    cols = q_ref.shape[1]
    step = 256
    for start in range(0, cols + 1, step):
        if start < cols:
            terms = lax.dot_general(
                x_ref[...], q_ref[:, start : start + step], (((0,), (0,)), ((), ())), preferred_element_type=WIDE
            )
        else:
            terms = lax.dot_general(
                x_ref[...], kv_ref[...], (((0,), (1,)), ((), ())), preferred_element_type=WIDE
            )
        terms = terms.reshape(-1, 2 * rows, terms.shape[1])
        low, high = terms[:, :rows], terms[:, rows:]
        ours_ref[:, :, start : start + terms.shape[2]] = jnp.where(first, low, high)
        theirs_ref[:, :, start : start + terms.shape[2]] = jnp.where(first, high, low).astype(NARROW)


def mixed_parts(core_ref, rows_ref, own_ref, other_ref, out_ref):
    core = core_ref[0]
    split = rows_ref.shape[0] - ZLO_FIRST * SIZES[1]
    rows = jnp.concatenate([rows_ref[split:], rows_ref[:split]], 0).reshape(-1, rows_ref.shape[2])
    for at, w_ref in ((core, own_ref), (1 - core, other_ref)):
        part = lax.dot_general(rows, w_ref[...], (((1,), (1,)), ((), ())), preferred_element_type=WIDE)
        part = part.reshape(out_ref.shape[1:]).astype(NARROW)
        for o, place in enumerate(WOUT_ORDER):
            out_ref[at, o] = part[place]


def own_rows(rows, parts_ref, out_ref):
    half = parts_ref.shape[0] // 2
    sums = [jnp.sum(parts_ref[c * half : (c + 1) * half].astype(WIDE), 0) for c in range(2)]
    pieces = [sums[c][chip * rows : (chip + 1) * rows] for chip in range(2) for c in range(2)]
    out_ref[...] = jnp.concatenate(pieces, 0).astype(NARROW)


def own_queries(head, own, rows, pieces_ref, cos_ref, sin_ref, out_ref, scr):
    half = head // 2
    total = jnp.sum(pieces_ref[...].astype(WIDE), 0).astype(NARROW).astype(WIDE)
    cosine, sine = cos_ref[:rows, :], sin_ref[:rows, :]
    scr[...] = jnp.zeros_like(scr)
    for h in range(own):
        start = h * head
        first, second = turn(total[:, start : start + half], total[:, start + half : start + head], cosine, sine)
        scr[h * rows : (h + 1) * rows, :half] = first
        scr[h * rows : (h + 1) * rows, half:] = second
    fresh = total[:, own * head :]
    scr[own * rows : (own + 1) * rows, : fresh.shape[1]] = fresh
    out_ref[...] = jnp.broadcast_to(scr[...].astype(NARROW)[None], out_ref.shape)


def partial_attention(head, own, rows, slots, scale, len_ref, at_ref, got_ref, cos_ref, sin_ref, keys_ref, values_ref, out_ref, self_scr, value_scr):
    half = head // 2
    wouts = got_ref.shape[0]
    width = 2 * head // wouts
    count = wouts * TALL
    here = at_ref[0]
    q = got_ref[...].reshape(count, head)

    iota = functools.partial(lax.broadcasted_iota, jnp.int32)

    def against(keys):
        return lax.dot_general(q, keys, (((1,), (1,)), ((), ())), preferred_element_type=WIDE)

    own_slot = (count, TALL)
    self_valid = jnp.logical_and(iota(own_slot, 0) % rows == iota(own_slot, 1), here == SELF_INDEX)
    self_scr[...] = jnp.full(own_slot, NONE, WIDE)
    value_scr[...] = jnp.zeros_like(value_scr)

    @pl.when(here == SELF_INDEX)
    def _():
        wide = (count, wouts * width)
        copies = iota((head, wouts * width), 1) % width == iota((head, wouts * width), 0)
        fresh = jnp.dot(q, copies.astype(WIDE).astype(NARROW), preferred_element_type=WIDE)
        piece = iota(wide, 0) // TALL
        piece = piece // SIZES[4] * SIZES[4] + (piece + ZH_ORDER[0]) % SIZES[4]
        fresh = jnp.where(iota(wide, 1) // width == piece, fresh, 0.0).astype(NARROW)
        pick = iota((TALL, count), 1) % TALL == iota((TALL, count), 0) + own * rows
        fresh = jnp.dot(pick.astype(WIDE).astype(NARROW), fresh, preferred_element_type=WIDE)
        first, second = turn(fresh[:, :half], fresh[:, half:head], cos_ref[...], sin_ref[...])
        newkey = jnp.concatenate([first, second], 1).astype(NARROW)
        self_scr[...] = jnp.where(self_valid, against(newkey) * scale, NONE)
        value_scr[...] = fresh[:, head:].astype(NARROW)

    row = iota((count, slots), 0) % rows
    length = jnp.zeros((count, slots), jnp.int32)
    scores = jnp.zeros((count, slots), WIDE)
    for r in range(rows):
        length = jnp.where(row == r, len_ref[r], length)
        scores = jnp.where(row == r, against(keys_ref[r]), scores)
    valid = here * slots + iota((count, slots), 1) < length
    scores = jnp.where(valid, scores * scale, NONE)
    self_score = self_scr[...]

    top = jnp.maximum(jnp.max(scores, -1, keepdims=True), jnp.max(self_score, -1, keepdims=True))
    top_hi = top.astype(NARROW).astype(WIDE)
    top_lo = (top - top_hi).astype(NARROW).astype(WIDE)
    top = top_hi + top_lo
    weights = jnp.where(valid, jnp.exp(scores - top), 0.0)
    self_weight = jnp.where(self_valid, jnp.exp(self_score - top), 0.0)
    total = jnp.sum(weights, -1, keepdims=True) + jnp.sum(self_weight, -1, keepdims=True)
    total_hi = total.astype(NARROW).astype(WIDE)
    acc = jnp.dot(self_weight.astype(NARROW), value_scr[...], preferred_element_type=WIDE)
    for r in range(rows):
        w = jnp.where(row == r, weights, 0.0).astype(NARROW)
        acc = acc + jnp.dot(w, values_ref[r], preferred_element_type=WIDE)

    lanes = 128
    shape = (wouts, TALL, lanes)
    at_row, at_lane = iota(shape, 1), iota(shape, 2)
    message = acc[:, :lanes].reshape(shape)
    for i, stat in enumerate((top_hi, top_lo, total_hi, total - total_hi)):
        line = jnp.where(at_row == at_lane, stat.reshape(wouts, TALL, 1), 0.0)
        message = jnp.where(at_row == own * rows + i, jnp.sum(line, 1, keepdims=True), message)
    out_ref[:, :, :lanes] = message.astype(NARROW)
    out_ref[:, :, lanes:] = acc[:, lanes:].reshape(wouts, TALL, head - lanes).astype(NARROW)


def merged(head, own, rows, parts_ref, out_ref):
    wouts = parts_ref.shape[0]
    parts = parts_ref[...].astype(WIDE)
    shape = parts.shape[:2] + (128,)
    diagonal = lax.broadcasted_iota(jnp.int32, shape, 1) == lax.broadcasted_iota(jnp.int32, shape, 2)

    def column(i):
        at = own * rows + i
        line = parts[:, at : at + 1, :128] + parts[:, at + 1 : at + 2, :128]
        return jnp.sum(jnp.where(diagonal, line, 0.0), -1, keepdims=True)

    tops, totals = column(0), column(2)
    factors = jnp.exp(tops - jnp.max(tops, 0, keepdims=True))
    total = jnp.sum(factors * totals, 0)
    attended = jnp.sum(factors * parts, 0) / total
    for h in range(own):
        piece = attended[h * rows : (h + 1) * rows, :].astype(NARROW)
        for peer in range(out_ref.shape[0]):
            out_ref[peer, :, h * head : (h + 1) * head] = piece


def limit(mib):
    return pltpu.CompilerParams(vmem_limit_bytes=mib * 2**20)


def body(inputs, w_query, w_keyval, w_out, key_cache, value_cache, lengths, positions):
    rows, slots, head = key_cache.shape
    qcols = w_query.shape[1]
    own = qcols // head
    chips = lax.axis_size(CHIP)
    wouts = lax.axis_size(WOUT)
    core = lax.axis_index("core")
    scale = head ** (-0.5)

    half = head // 2
    freq = 10000.0 ** (-(2.0 * jnp.arange(half, dtype=WIDE)) / head)
    place = jnp.pad(positions, (0, TALL - rows)).astype(WIDE)
    angle = place[:, None] * freq
    cosine = jnp.cos(angle)
    sine = jnp.sin(angle)

    split = ZLO_FIRST * SIZES[1] * 2 * rows
    rolled = jnp.concatenate([inputs[split:], inputs[:split]], 0)
    core_at = core.reshape(1).astype(jnp.int32)
    shape = (chips, rows, qcols + w_keyval.shape[1])
    ours, theirs = pl.pallas_call(
        functools.partial(projected, rows),
        out_shape=(jax.ShapeDtypeStruct(shape, WIDE), jax.ShapeDtypeStruct(shape, NARROW)),
        in_specs=[SMEM] + [VMEM] * 3,
        out_specs=(VMEM, VMEM),
        compiler_params=limit(8),
        name="projected",
    )(core_at, rolled.T, w_query, w_keyval.T)
    theirs = lax.ppermute(theirs, "core", CORES)
    partial = (ours + theirs.astype(WIDE)).astype(NARROW)

    at = lax.axis_index(WOUT).reshape(1).astype(jnp.int32)
    partial, w_turned, at = lax.optimization_barrier((partial, w_out.T, at))
    w_other = lax.ppermute(w_turned, "core", CORES)
    pieces = exchange(partial, CHIP, CHIP_GROUP)
    message = pl.pallas_call(
        functools.partial(own_queries, head, own, rows),
        out_shape=jax.ShapeDtypeStruct((wouts, TALL, head), NARROW),
        in_specs=[VMEM] * 3,
        out_specs=VMEM,
        scratch_shapes=[pltpu.VMEM((TALL, head), WIDE)],
        compiler_params=limit(4),
        name="own_queries",
    )(pieces, cosine, sine)
    message, w_other = lax.optimization_barrier((message, w_other))
    got = exchange(message, WOUT, [WOUT_ORDER])
    message = pl.pallas_call(
        functools.partial(partial_attention, head, own, rows, slots, scale),
        out_shape=jax.ShapeDtypeStruct((wouts, TALL, head), NARROW),
        in_specs=[SMEM, SMEM] + [VMEM] * 5,
        out_specs=VMEM,
        scratch_shapes=[pltpu.VMEM((wouts * TALL, TALL), WIDE), pltpu.VMEM((TALL, head), NARROW)],
        compiler_params=limit(8),
        name="partial_attention",
    )(lengths, at, got, cosine, sine, key_cache, value_cache)
    parts = exchange(message, WOUT, [WOUT_ORDER])
    attended = pl.pallas_call(
        functools.partial(merged, head, own, rows),
        out_shape=jax.ShapeDtypeStruct((chips, rows, qcols), NARROW),
        in_specs=[VMEM],
        out_specs=VMEM,
        compiler_params=limit(4),
        name="merged",
    )(parts)

    whole = exchange(attended, CHIP, CHIP_GROUP)
    mixed = pl.pallas_call(
        mixed_parts,
        out_shape=jax.ShapeDtypeStruct((2, wouts, 2 * rows, w_out.shape[1]), NARROW),
        in_specs=[SMEM] + [VMEM] * 3,
        out_specs=VMEM,
        compiler_params=limit(8),
        name="mixed_parts",
    )(core_at, whole, w_turned, w_other)
    mixed = exchange(mixed.reshape((2 * wouts,) + mixed.shape[2:]), ("core",) + WOUT, CORE_WOUT_GROUP)
    return pl.pallas_call(
        functools.partial(own_rows, rows),
        out_shape=jax.ShapeDtypeStruct((4 * rows, mixed.shape[2]), NARROW),
        in_specs=[VMEM],
        out_specs=VMEM,
        compiler_params=limit(8),
        name="own_rows",
    )(mixed)


def solution(mesh):
    parted = Mesh(mesh.devices.reshape(SIZES), AXES)
    placed = (
        P(None, WIN),
        P(WIN, WOUT),
        P(WIN, WOUT),
        P(WOUT, WIN),
        P(WIN, WOUT, None),
        P(WIN, WOUT, None),
        P(WIN),
        P(WIN),
    )
    return jax.shard_map(
        body, mesh=parted, in_specs=placed, out_specs=P(WOUT, WIN), check_vma=False
    )
```

```python
import functools

import jax
import jax.numpy as jnp
from jax import lax
from jax.experimental import pallas as pl
from jax.experimental.pallas import tpu as pltpu
from jax.sharding import Mesh
from jax.sharding import PartitionSpec as P

WIDE = jnp.float32
NARROW = jnp.bfloat16
AXES = ("zlo", "y", "core", "x", "zh")
SIZES = (4, 8, 2, 4, 4)
WIN = ("zlo", "y", "core")
CHIP = ("zlo", "y")
WOUT = ("x", "zh")
NONE = -1e30
TALL = 16
SELF_INDEX = 9
CORES = [(0, 1), (1, 0)]
VMEM = pl.BlockSpec(memory_space=pltpu.VMEM)
SMEM = pl.BlockSpec(memory_space=pltpu.SMEM)


ZLO_FIRST = 3
ZH_ORDER = (3, 0, 1, 2)
CHIP_GROUP = [[(ZLO_FIRST + z) % SIZES[0] * SIZES[1] + y for z in range(SIZES[0]) for y in range(SIZES[1])]]
WOUT_ORDER = [x * SIZES[4] + zh for x in range(SIZES[3]) for zh in ZH_ORDER]
CORE_WOUT_GROUP = [[core * len(WOUT_ORDER) + o for core in range(2) for o in WOUT_ORDER]]


def exchange(pieces, axis, group):
    return lax.all_to_all(pieces, axis, 0, 0, axis_index_groups=group, tiled=True)


def turn(first, second, cosine, sine):
    return first * cosine - second * sine, first * sine + second * cosine


def projected(rows, core_ref, x_ref, q_ref, kv_ref, ours_ref, theirs_ref):
    first = core_ref[0] == 0
    cols = q_ref.shape[1]
    step = 256
    for start in range(0, cols + 1, step):
        if start < cols:
            terms = lax.dot_general(
                x_ref[...], q_ref[:, start : start + step], (((0,), (0,)), ((), ())), preferred_element_type=WIDE
            )
        else:
            terms = lax.dot_general(
                x_ref[...], kv_ref[...], (((0,), (1,)), ((), ())), preferred_element_type=WIDE
            )
        terms = terms.reshape(-1, 2 * rows, terms.shape[1])
        low, high = terms[:, :rows], terms[:, rows:]
        ours_ref[:, :, start : start + terms.shape[2]] = jnp.where(first, low, high)
        theirs_ref[:, :, start : start + terms.shape[2]] = jnp.where(first, high, low).astype(NARROW)


def mixed_parts(core_ref, rows_ref, own_ref, other_ref, out_ref):
    core = core_ref[0]
    split = rows_ref.shape[0] - ZLO_FIRST * SIZES[1]
    rows = jnp.concatenate([rows_ref[split:], rows_ref[:split]], 0).reshape(-1, rows_ref.shape[2])
    for at, w_ref in ((core, own_ref), (1 - core, other_ref)):
        part = lax.dot_general(rows, w_ref[...], (((1,), (1,)), ((), ())), preferred_element_type=WIDE)
        part = part.reshape(out_ref.shape[1:]).astype(NARROW)
        for o, place in enumerate(WOUT_ORDER):
            out_ref[at, o] = part[place]


def own_rows(rows, parts_ref, out_ref):
    half = parts_ref.shape[0] // 2
    sums = [jnp.sum(parts_ref[c * half : (c + 1) * half].astype(WIDE), 0) for c in range(2)]
    pieces = [sums[c][chip * rows : (chip + 1) * rows] for chip in range(2) for c in range(2)]
    out_ref[...] = jnp.concatenate(pieces, 0).astype(NARROW)


def own_queries(head, own, rows, pieces_ref, cos_ref, sin_ref, out_ref, scr):
    half = head // 2
    total = jnp.sum(pieces_ref[...].astype(WIDE), 0).astype(NARROW).astype(WIDE)
    cosine, sine = cos_ref[:rows, :], sin_ref[:rows, :]
    scr[...] = jnp.zeros_like(scr)
    for h in range(own):
        start = h * head
        first, second = turn(total[:, start : start + half], total[:, start + half : start + head], cosine, sine)
        scr[h * rows : (h + 1) * rows, :half] = first
        scr[h * rows : (h + 1) * rows, half:] = second
    fresh = total[:, own * head :]
    scr[own * rows : (own + 1) * rows, : fresh.shape[1]] = fresh
    out_ref[...] = jnp.broadcast_to(scr[...].astype(NARROW)[None], out_ref.shape)


def partial_attention(head, own, rows, slots, scale, len_ref, at_ref, got_ref, cos_ref, sin_ref, keys_ref, values_ref, out_ref, self_scr, value_scr):
    half = head // 2
    wouts = got_ref.shape[0]
    width = 2 * head // wouts
    count = wouts * TALL
    here = at_ref[0]
    q = got_ref[...].reshape(count, head)

    iota = functools.partial(lax.broadcasted_iota, jnp.int32)

    def against(keys):
        return lax.dot_general(q, keys, (((1,), (1,)), ((), ())), preferred_element_type=WIDE)

    own_slot = (count, TALL)
    self_valid = jnp.logical_and(iota(own_slot, 0) % rows == iota(own_slot, 1), here == SELF_INDEX)
    self_scr[...] = jnp.full(own_slot, NONE, WIDE)
    value_scr[...] = jnp.zeros_like(value_scr)

    @pl.when(here == SELF_INDEX)
    def _():
        wide = (count, wouts * width)
        copies = iota((head, wouts * width), 1) % width == iota((head, wouts * width), 0)
        fresh = jnp.dot(q, copies.astype(WIDE).astype(NARROW), preferred_element_type=WIDE)
        piece = iota(wide, 0) // TALL
        piece = piece // SIZES[4] * SIZES[4] + (piece + ZH_ORDER[0]) % SIZES[4]
        fresh = jnp.where(iota(wide, 1) // width == piece, fresh, 0.0).astype(NARROW)
        pick = iota((TALL, count), 1) % TALL == iota((TALL, count), 0) + own * rows
        fresh = jnp.dot(pick.astype(WIDE).astype(NARROW), fresh, preferred_element_type=WIDE)
        first, second = turn(fresh[:, :half], fresh[:, half:head], cos_ref[...], sin_ref[...])
        newkey = jnp.concatenate([first, second], 1).astype(NARROW)
        self_scr[...] = jnp.where(self_valid, against(newkey) * scale, NONE)
        value_scr[...] = fresh[:, head:].astype(NARROW)

    row = iota((count, slots), 0) % rows
    length = jnp.zeros((count, slots), jnp.int32)
    scores = jnp.zeros((count, slots), WIDE)
    for r in range(rows):
        length = jnp.where(row == r, len_ref[r], length)
        scores = jnp.where(row == r, against(keys_ref[r]), scores)
    valid = here * slots + iota((count, slots), 1) < length
    scores = jnp.where(valid, scores * scale, NONE)
    self_score = self_scr[...]

    top = jnp.maximum(jnp.max(scores, -1, keepdims=True), jnp.max(self_score, -1, keepdims=True))
    top_hi = top.astype(NARROW).astype(WIDE)
    top_lo = (top - top_hi).astype(NARROW).astype(WIDE)
    top = top_hi + top_lo
    weights = jnp.where(valid, jnp.exp(scores - top), 0.0)
    self_weight = jnp.where(self_valid, jnp.exp(self_score - top), 0.0)
    total = jnp.sum(weights, -1, keepdims=True) + jnp.sum(self_weight, -1, keepdims=True)
    total_hi = total.astype(NARROW).astype(WIDE)
    acc = jnp.dot(self_weight.astype(NARROW), value_scr[...], preferred_element_type=WIDE)
    for r in range(rows):
        w = jnp.where(row == r, weights, 0.0).astype(NARROW)
        acc = acc + jnp.dot(w, values_ref[r], preferred_element_type=WIDE)

    shape = (wouts, TALL, head)
    at_row, at_lane = iota(shape, 1), iota(shape, 2)
    message = acc.reshape(shape)
    for i, stat in enumerate((top_hi, top_lo, total_hi, total - total_hi)):
        line = jnp.where(at_row == at_lane, stat.reshape(wouts, TALL, 1), 0.0)
        message = jnp.where(at_row == own * rows + i, jnp.sum(line, 1, keepdims=True), message)
    out_ref[...] = message.astype(NARROW)


def merged(head, own, rows, parts_ref, out_ref):
    wouts = parts_ref.shape[0]
    parts = parts_ref[...].astype(WIDE)
    shape = parts.shape
    diagonal = lax.broadcasted_iota(jnp.int32, shape, 1) == lax.broadcasted_iota(jnp.int32, shape, 2)

    def column(i):
        line = parts[:, own * rows + i : own * rows + i + 1, :] + parts[:, own * rows + i + 1 : own * rows + i + 2, :]
        return jnp.sum(jnp.where(diagonal, line, 0.0), -1, keepdims=True)

    tops, totals = column(0), column(2)
    factors = jnp.exp(tops - jnp.max(tops, 0, keepdims=True))
    total = jnp.sum(factors * totals, 0)
    attended = jnp.sum(factors * parts, 0) / total
    for h in range(own):
        piece = attended[h * rows : (h + 1) * rows, :].astype(NARROW)
        for peer in range(out_ref.shape[0]):
            out_ref[peer, :, h * head : (h + 1) * head] = piece


def limit(mib):
    return pltpu.CompilerParams(vmem_limit_bytes=mib * 2**20)


def body(inputs, w_query, w_keyval, w_out, key_cache, value_cache, lengths, positions):
    rows, slots, head = key_cache.shape
    qcols = w_query.shape[1]
    own = qcols // head
    chips = lax.axis_size(CHIP)
    wouts = lax.axis_size(WOUT)
    core = lax.axis_index("core")
    scale = head ** (-0.5)

    half = head // 2
    freq = 10000.0 ** (-(2.0 * jnp.arange(half, dtype=WIDE)) / head)
    place = jnp.pad(positions, (0, TALL - rows)).astype(WIDE)
    angle = place[:, None] * freq
    cosine = jnp.cos(angle)
    sine = jnp.sin(angle)

    split = ZLO_FIRST * SIZES[1] * 2 * rows
    rolled = jnp.concatenate([inputs[split:], inputs[:split]], 0)
    core_at = core.reshape(1).astype(jnp.int32)
    shape = (chips, rows, qcols + w_keyval.shape[1])
    ours, theirs = pl.pallas_call(
        functools.partial(projected, rows),
        out_shape=(jax.ShapeDtypeStruct(shape, WIDE), jax.ShapeDtypeStruct(shape, NARROW)),
        in_specs=[SMEM] + [VMEM] * 3,
        out_specs=(VMEM, VMEM),
        compiler_params=limit(8),
        name="projected",
    )(core_at, rolled.T, w_query, w_keyval.T)
    theirs = lax.ppermute(theirs, "core", CORES)
    partial = (ours + theirs.astype(WIDE)).astype(NARROW)

    at = lax.axis_index(WOUT).reshape(1).astype(jnp.int32)
    partial, w_turned, at = lax.optimization_barrier((partial, w_out.T, at))
    w_other = lax.ppermute(w_turned, "core", CORES)
    pieces = exchange(partial, CHIP, CHIP_GROUP)
    message = pl.pallas_call(
        functools.partial(own_queries, head, own, rows),
        out_shape=jax.ShapeDtypeStruct((wouts, TALL, head), NARROW),
        in_specs=[VMEM] * 3,
        out_specs=VMEM,
        scratch_shapes=[pltpu.VMEM((TALL, head), WIDE)],
        compiler_params=limit(4),
        name="own_queries",
    )(pieces, cosine, sine)
    message, w_other = lax.optimization_barrier((message, w_other))
    got = exchange(message, WOUT, [WOUT_ORDER])
    message = pl.pallas_call(
        functools.partial(partial_attention, head, own, rows, slots, scale),
        out_shape=jax.ShapeDtypeStruct((wouts, TALL, head), NARROW),
        in_specs=[SMEM, SMEM] + [VMEM] * 5,
        out_specs=VMEM,
        scratch_shapes=[pltpu.VMEM((wouts * TALL, TALL), WIDE), pltpu.VMEM((TALL, head), NARROW)],
        compiler_params=limit(8),
        name="partial_attention",
    )(lengths, at, got, cosine, sine, key_cache, value_cache)
    parts = exchange(message, WOUT, [WOUT_ORDER])
    attended = pl.pallas_call(
        functools.partial(merged, head, own, rows),
        out_shape=jax.ShapeDtypeStruct((chips, rows, qcols), NARROW),
        in_specs=[VMEM],
        out_specs=VMEM,
        compiler_params=limit(4),
        name="merged",
    )(parts)

    whole = exchange(attended, CHIP, CHIP_GROUP)
    mixed = pl.pallas_call(
        mixed_parts,
        out_shape=jax.ShapeDtypeStruct((2, wouts, 2 * rows, w_out.shape[1]), NARROW),
        in_specs=[SMEM] + [VMEM] * 3,
        out_specs=VMEM,
        compiler_params=limit(8),
        name="mixed_parts",
    )(core_at, whole, w_turned, w_other)
    mixed = exchange(mixed.reshape((2 * wouts,) + mixed.shape[2:]), ("core",) + WOUT, CORE_WOUT_GROUP)
    return pl.pallas_call(
        functools.partial(own_rows, rows),
        out_shape=jax.ShapeDtypeStruct((4 * rows, mixed.shape[2]), NARROW),
        in_specs=[VMEM],
        out_specs=VMEM,
        compiler_params=limit(8),
        name="own_rows",
    )(mixed)


def solution(mesh):
    parted = Mesh(mesh.devices.reshape(SIZES), AXES)
    placed = (
        P(None, WIN),
        P(WIN, WOUT),
        P(WIN, WOUT),
        P(WOUT, WIN),
        P(WIN, WOUT, None),
        P(WIN, WOUT, None),
        P(WIN),
        P(WIN),
    )
    return jax.shard_map(
        body, mesh=parted, in_specs=placed, out_specs=P(WOUT, WIN), check_vma=False
    )
```
